128 devices in a mesh: row: 16 (over y, x), col: 8 (over z, core).
Axes of the slice: x: 4, y: 4, z: 4, core: 2. Of those that a mesh axis runs over, the one named last changes fastest.
Arguments:
- source_points: bfloat16 [64, 262144], P(None, 'row'), may hold values from -3 to 3
- target_points: bfloat16 [64, 1048576], P(None, 'col'), may hold values from -4 to 4
- source_mass: float32 [262144], P('row'), may hold values from 0.5 to 4
- target_mass: float32 [1048576], P('col'), may hold values from 0.5 to 4
- tile_cols: int32 [2048, 8, 4], P('row', 'col'), may hold values from 0 to 1023, as said below
- tile_counts: int32 [2048, 8], P('row', 'col'), may hold values from 1 to 4
Outputs:
- source_potential: float32 [262144], P('row')
- target_potential: float32 [1048576], P('col')
The draws below stay inside these ranges and needn't reach their ends.
Inputs may be any that keep to these rules, and one draw needn't show every extreme that they name: `tile_cols`: for each row block and target shard the 4 entries are distinct; only the first tile_counts entries are live; every target block of every shard is live for some row block.
All inputs are finite; a program needn't handle non-finite values.
Results may differ from the reference program's by a relative error of at most 0.0003.
Values sent between devices are 32-bit elements; how exact they have to be, the bound alone decides.
No kernel may reach another device: no remote copies, remote signals or barrier semaphores. Data moves between devices by JAX's collectives and lax.ppermute only.
A program may use at most 192 MiB of HBM per device.

```python
import math
import jax
import jax.numpy as jnp
from jax import lax

D = 64
TILE = 128
SLOTS = 4
ITERS = 2
TB_DEV = 1024
NRB = 2048
COL_SHARDS = 8
NS = 262144
NT = 1048576


def shifted_cells(key):
    first, second, third, fourth = jax.random.split(jax.random.fold_in(key, 77), 4)
    chosen = jax.random.randint(first, (1, NS), 0, 8) == 0
    signs = 2.0 * jax.random.randint(second, (1, NS), 0, 2).astype(jnp.float32) - 1.0
    strength = jax.random.uniform(third, (1, NS), jnp.float32, 2.2, 2.6)
    noise = jnp.clip(0.1 * jax.random.normal(fourth, (D, NS), jnp.float32), -0.3, 0.3)
    return (chosen, signs * strength + noise)


def draw_source_points(key, part):
    chosen, moved = shifted_cells(key)
    key = jax.random.fold_in(key, 5)
    values = jnp.clip(0.25 * jax.random.normal(key, (D, NS), jnp.float32), -1.5, 1.5)
    return jnp.where(chosen, moved, values).astype(jnp.bfloat16)


def draw_tile_cols(key, part):
    key = jax.random.fold_in(key, 11)
    first, second = jax.random.split(key)
    shifts = jax.random.randint(first, (1, COL_SHARDS), 0, TB_DEV)
    leading = (jnp.arange(NRB, dtype=jnp.int32)[:, None] + shifts) % TB_DEV
    ranks = jax.random.randint(second, (NRB, COL_SHARDS, TB_DEV - 1), 0, 1 << 20) * TB_DEV
    ranks = ranks + jnp.arange(TB_DEV - 1, dtype=jnp.int32)
    offsets = jnp.argsort(ranks, axis=-1)[..., :SLOTS - 1].astype(jnp.int32) + 1
    offsets = jnp.concatenate([jnp.zeros((NRB, COL_SHARDS, 1), jnp.int32), offsets], axis=-1)
    return ((leading[:, :, None] + offsets) % TB_DEV).astype(jnp.int32)


def draw_tile_counts(key, part):
    key = jax.random.fold_in(key, 12)
    ceiling = 1 + (SLOTS - 1) * jnp.arange(COL_SHARDS, dtype=jnp.int32) // max(COL_SHARDS - 1, 1)
    counts = jax.random.randint(key, (NRB, COL_SHARDS), 1, ceiling[None, :] + 2)
    counts = jnp.minimum(counts, SLOTS)
    counts = counts.at[0].set(SLOTS)
    return counts.astype(jnp.int32)


def block_scale(own_key, extent, cuts, low, largest):
    def one(axis_at, parts):
        heights = jax.random.uniform(jax.random.fold_in(jax.random.fold_in(own_key, 6), axis_at), (parts,), jnp.float32, low / len(cuts), largest / len(cuts))
        return jnp.repeat(jnp.exp(heights), extent[axis_at] // parts).reshape((-1,) + (1,) * (len(extent) - axis_at - 1))

    factor_of = one(*cuts[0])
    for cut in cuts[1:]:
        factor_of = factor_of * one(*cut)
    return factor_of


def normal_values(key, extent, spread, bound, cuts=(), held_as=jnp.bfloat16):
    loudness = block_scale(key, extent, cuts, -0.22, 0.18) if cuts else 1.0
    result = jax.random.normal(key, extent, jnp.float32) * spread * loudness
    return jnp.minimum(jnp.maximum(result, -bound), bound).astype(held_as)


def setup_inputs(seed: int = 0) -> dict:
    seeds = jax.random.split(jax.random.key(seed), 7)
    return {
        "source_points": draw_source_points(jax.random.fold_in(seeds[6], 71), 0),
        "target_points": normal_values(seeds[1], (D, NT), 0.25, 4.0, ((1, 8),)),
        "source_mass": jnp.clip(jnp.exp(math.log(4.0) - 2.0794415 * jax.random.uniform(seeds[2], (NS,), jnp.float32) ** block_scale(seeds[2], (NS,), ((0, 16),), -0.2, 0.2)), 0.5, 4.0),
        "target_mass": jnp.clip(jnp.exp(math.log(4.0) - 2.0794415 * jax.random.uniform(seeds[3], (NT,), jnp.float32) ** block_scale(seeds[3], (NT,), ((0, 8),), -0.2, 0.2)), 0.5, 4.0),
        "tile_cols": draw_tile_cols(jax.random.fold_in(seeds[6], 71), 0),
        "tile_counts": draw_tile_counts(jax.random.fold_in(seeds[6], 71), 0),
    }


very_negative = -1e30
first_epsilon = 0.5


def reference(source_points, target_points, source_mass, target_mass, tile_cols, tile_counts):
    src_float = source_points.astype(jnp.float32)
    tgt_float = target_points.astype(jnp.float32)
    src_half = 0.5 * jnp.sum(src_float * src_float, axis=0)
    tgt_half = 0.5 * jnp.sum(tgt_float * tgt_float, axis=0)
    blocks = NT // TILE
    tgt_tiles = tgt_float.reshape(D, blocks, TILE)
    tgt_half_tiles = tgt_half.reshape(blocks, TILE)
    shard_base = (jnp.arange(COL_SHARDS, dtype=jnp.int32) * TB_DEV)[None, :, None]
    global_cols = (tile_cols + shard_base).reshape(NRB, COL_SHARDS * SLOTS).astype(jnp.int32)
    alive = (jnp.arange(SLOTS, dtype=jnp.int32)[None, None, :] < tile_counts[:, :, None]).reshape(NRB, COL_SHARDS * SLOTS)
    log_a = jnp.log(source_mass) - jnp.log(jnp.sum(source_mass))
    log_b = jnp.log(target_mass) - jnp.log(jnp.sum(target_mass))
    row_ids = jnp.arange(NRB, dtype=jnp.int32)

    def cost(row_block, columns):
        start = (row_block * TILE).astype(jnp.int32)
        block = lax.dynamic_slice_in_dim(src_float, start, TILE, 1)
        half = lax.dynamic_slice_in_dim(src_half, start, TILE, 0)
        picked = tgt_tiles[:, columns, :]
        inner = jnp.einsum("di,dkj->ikj", block, picked, precision=lax.Precision.HIGHEST)
        return half[:, None, None] + tgt_half_tiles[columns][None] - inner

    def row_pass(target_pot, epsilon):
        pot_tiles = target_pot.reshape(blocks, TILE)

        def visit(args):
            row_block, columns, live = args
            masked = live[None, :, None]
            scores = jnp.where(masked, (pot_tiles[columns][None] - cost(row_block, columns)) / epsilon, very_negative)
            highest = jnp.max(scores, axis=(1, 2))
            summed = jnp.sum(jnp.where(masked, jnp.exp(scores - highest[:, None, None]), 0.0), axis=(1, 2))
            return highest + jnp.log(summed)

        lse = lax.map(visit, (row_ids, global_cols, alive)).reshape(NS)
        return epsilon * (log_a - lse)

    def col_pass(source_pot, epsilon):
        def scores_of(row_block, columns):
            start = (row_block * TILE).astype(jnp.int32)
            local = lax.dynamic_slice_in_dim(source_pot, start, TILE, 0)
            return (local[:, None, None] - cost(row_block, columns)) / epsilon

        def sweep_max(carry, args):
            row_block, columns, live = args
            scores = jnp.where(live[None, :, None], scores_of(row_block, columns), very_negative)
            return carry.at[columns].max(jnp.max(scores, axis=0)), None

        start_top = jnp.full((blocks, TILE), very_negative, jnp.float32)
        col_top, _ = lax.scan(sweep_max, start_top, (row_ids, global_cols, alive))

        def sweep_sum(carry, args):
            row_block, columns, live = args
            scores = scores_of(row_block, columns)
            terms = jnp.where(live[None, :, None], jnp.exp(scores - col_top[columns][None]), 0.0)
            return carry.at[columns].add(jnp.sum(terms, axis=0)), None

        col_total, _ = lax.scan(sweep_sum, jnp.zeros((blocks, TILE), jnp.float32), (row_ids, global_cols, alive))
        lse = (col_top + jnp.log(col_total)).reshape(NT)
        return epsilon * (log_b - lse)

    target_pot = jnp.zeros((NT,), jnp.float32)
    source_pot = jnp.zeros((NS,), jnp.float32)
    for step in range(ITERS):
        epsilon = first_epsilon * 0.5 ** step
        source_pot = row_pass(target_pot, epsilon)
        target_pot = col_pass(source_pot, epsilon)
    return source_pot, target_pot
```

```python
import functools
import math

import jax
import jax.numpy as jnp
from jax import lax
from jax.experimental import pallas as pl
from jax.experimental.pallas import tpu as pltpu
from jax.sharding import PartitionSpec as P

ITERS = 2
TILE = 128
very_negative = -1e30
first_epsilon = 0.5
LOG2E = 1.4426950408889634
LN2 = 0.6931471805599453
SMALLEST = 2.0**-100
LARGEST = 2.0**120
VMEM_LIMIT = 50 * 1024 * 1024


def split3(row):
    hi = row.astype(jnp.bfloat16).astype(jnp.float32)
    rest = row - hi
    mid = rest.astype(jnp.bfloat16).astype(jnp.float32)
    lo = (rest - mid).astype(jnp.bfloat16).astype(jnp.float32)
    return hi, mid, lo


def products(x_ref, y_ref, f_ref, r):
    xb = x_ref[:, pl.ds(pl.multiple_of(r * TILE, TILE), TILE)]
    yb = y_ref[r]
    if f_ref is not None:
        hi, mid, lo = split3(f_ref[pl.ds(r, 1), :])
        place = lax.broadcasted_iota(jnp.int32, (16, TILE), 0)
        extra = jnp.where(
            place == 0, hi, jnp.where(place == 1, mid, jnp.where(place == 2, lo, 0.0))
        )
        xb = jnp.concatenate([xb, extra.astype(jnp.bfloat16)], axis=0)
        yb = jnp.concatenate([yb, jnp.ones((16, yb.shape[1]), jnp.bfloat16)], axis=0)
    return jnp.dot(xb.T, yb, preferred_element_type=jnp.float32)


def row_pass_kernel(kappa, first, slots, *refs):
    if first:
        cols, counts, x_ref, y_hbm, out_ref, y_ref, g_out, hx_ref, total, sems = refs
        f_ref = None
    else:
        cols, counts, x_ref, y_ref, f_ref, g_ref, out_ref, total = refs
    blocks = out_ref.shape[0]
    lane = lax.broadcasted_iota(jnp.int32, (TILE, TILE), 1)

    if first:

        def copy(r, k):
            start = pl.multiple_of(cols[r * slots + k] * TILE, TILE)
            return pltpu.make_async_copy(
                y_hbm.at[:, pl.ds(start, TILE)],
                y_ref.at[r, :, pl.ds(k * TILE, TILE)],
                sems.at[r],
            )

        @pl.loop(0, blocks)
        def _(r):
            for k in range(slots):
                copy(r, k).start()

    def shifts(r):
        live = counts[r]
        rows = []
        for k in range(slots):
            if first:
                row = g_out[pl.ds(r * slots + k, 1), :]
            else:
                row = g_ref[pl.ds(cols[r * slots + k], 1), :]
            rows.append(jnp.where(k < live, row, very_negative))
        return rows

    @pl.loop(0, blocks)
    def _(r):
        if first:
            pltpu.make_async_copy(y_ref.at[r], y_ref.at[r], sems.at[r]).wait()
            yf = y_ref[r].astype(jnp.float32)
            half = -0.5 * jnp.sum(yf * yf, axis=0, keepdims=True)
            for k in range(slots):
                g_out[pl.ds(r * slots + k, 1), :] = half[:, k * TILE : (k + 1) * TILE]
            xf = x_ref[:, pl.ds(pl.multiple_of(r * TILE, TILE), TILE)].astype(jnp.float32)
            hx_ref[pl.ds(r, 1), :] = 0.5 * jnp.sum(xf * xf, axis=0, keepdims=True)
        scores = products(x_ref, y_ref, f_ref, r)
        terms = jnp.zeros((TILE, TILE), jnp.float32)
        for k, row in enumerate(shifts(r)):
            terms += jnp.exp2((scores[:, k * TILE : (k + 1) * TILE] + row) * kappa)
        summed = jnp.sum(terms, axis=1, keepdims=True)
        total[...] = jnp.where(lane == r, summed, total[...])

    sums = total[...]
    out_ref[...] = jnp.log2(sums).T
    fine = jnp.logical_and(jnp.min(sums) >= SMALLEST, jnp.max(sums) <= LARGEST)

    @pl.when(jnp.logical_not(fine))
    def _():
        @pl.loop(0, blocks)
        def _(r):
            scores = products(x_ref, y_ref, f_ref, r)
            scores = jnp.concatenate(
                [
                    scores[:, k * TILE : (k + 1) * TILE] + row
                    for k, row in enumerate(shifts(r))
                ],
                axis=1,
            )
            top = jnp.max(scores, axis=1, keepdims=True)
            summed = jnp.sum(jnp.exp2((scores - top) * kappa), axis=1, keepdims=True)
            total[...] = jnp.where(lane == r, top * kappa + jnp.log2(summed), total[...])

        out_ref[...] = total[...].T


def col_pass_kernel(kappa, first, slots, *refs):
    cols, counts, x_ref, y_ref, f_ref, g_ref, out_ref, total = refs
    blocks = f_ref.shape[0]

    def shifts(r):
        live = counts[r]
        rows = []
        for k in range(slots):
            if first:
                row = g_ref[pl.ds(r * slots + k, 1), :]
            else:
                row = g_ref[pl.ds(cols[r * slots + k], 1), :]
            rows.append(jnp.where(k < live, row, very_negative))
        return rows

    total[...] = jnp.zeros_like(total)

    def visit(r, carry):
        least, most = carry
        scores = products(x_ref, y_ref, f_ref, r)
        live = counts[r]
        for k, row in enumerate(shifts(r)):
            terms = jnp.exp2((scores[:, k * TILE : (k + 1) * TILE] + row) * kappa)
            summed = jnp.sum(terms, axis=0, keepdims=True)
            at = pl.ds(cols[r * slots + k], 1)
            total[at, :] += summed
            least = jnp.minimum(least, jnp.where(k < live, summed, 1.0))
            most = jnp.maximum(most, summed)
        return least, most

    ones = jnp.ones((1, TILE), jnp.float32)
    least, most = lax.fori_loop(0, blocks, visit, (ones, ones))
    sums = total[...]
    out_ref[...] = jnp.where(sums > 0.0, jnp.log2(sums), very_negative)
    fine = jnp.logical_and(jnp.min(least) >= SMALLEST, jnp.max(most) <= LARGEST / blocks)

    @pl.when(jnp.logical_not(fine))
    def _():
        out_ref[...] = jnp.full_like(out_ref, very_negative)

        @pl.loop(0, blocks)
        def _(r):
            scores = products(x_ref, y_ref, f_ref, r)
            live = counts[r]
            for k, row in enumerate(shifts(r)):

                @pl.when(k < live)
                def _():
                    part = scores[:, k * TILE : (k + 1) * TILE] + row
                    top = jnp.max(part, axis=0, keepdims=True)
                    summed = jnp.sum(jnp.exp2((part - top) * kappa), axis=0, keepdims=True)
                    mine = top * kappa + jnp.log2(summed)
                    at = pl.ds(cols[r * slots + k], 1)
                    old = out_ref[at, :]
                    peak = jnp.maximum(old, mine)
                    out_ref[at, :] = peak + jnp.log2(
                        jnp.exp2(old - peak) + jnp.exp2(mine - peak)
                    )


SMEM = functools.partial(pl.BlockSpec, memory_space=pltpu.SMEM)
VMEM = functools.partial(pl.BlockSpec, memory_space=pltpu.VMEM)
PARAMS = dict(compiler_params=pltpu.CompilerParams(vmem_limit_bytes=VMEM_LIMIT))


def lse(stack):
    top = jnp.max(stack, axis=0)
    return top + jnp.log2(jnp.sum(jnp.exp2(stack - top[None]), axis=0))


def shift_z(value, by, cols):
    return lax.ppermute(value, "col", [(i, (i + 2 * by) % cols) for i in range(cols)])


def over_cols(part, cols):
    half = part.shape[0] // 2
    core = lax.axis_index("col") % 2
    swap = [(i, i ^ 1) for i in range(cols)]
    away = lax.dynamic_slice_in_dim(part, (1 - core) * half, half, 0)
    mine = lax.dynamic_slice_in_dim(part, core * half, half, 0)
    mine = lse(jnp.stack([mine, lax.ppermute(away, "col", swap)]))
    chips = cols // 2
    mine = lse(jnp.stack([mine] + [shift_z(mine, by, cols) for by in range(1, chips)]))
    other = lax.ppermute(mine, "col", swap)
    low = jnp.where(core == 0, mine, other)
    high = jnp.where(core == 0, other, mine)
    return jnp.concatenate([low, high], axis=0)


def body(source_points, target_points, source_mass, target_mass, tile_cols, tile_counts):
    width, rows = source_points.shape
    row_blocks = rows // TILE
    target_cells = target_points.shape[1]
    target_blocks = target_cells // TILE
    slots = tile_cols.shape[2]
    row_devices = lax.axis_size("row")
    col_devices = lax.axis_size("col")
    own_blocks = target_blocks // row_devices
    me = lax.axis_index("row")
    f32 = jnp.float32

    cols = tile_cols.reshape(row_blocks * slots)
    counts = tile_counts.reshape(row_blocks)
    mass_a = source_mass.reshape(row_blocks, TILE)
    log_a = jnp.log2(mass_a)
    own_mass = lax.dynamic_slice_in_dim(target_mass, me * own_blocks * TILE, own_blocks * TILE, 0)
    log_b = jnp.log2(own_mass).reshape(own_blocks, TILE)
    own_points = lax.dynamic_slice_in_dim(
        target_points, me * own_blocks * TILE, own_blocks * TILE, 1
    ).astype(f32)
    own_half = (0.5 * jnp.sum(own_points * own_points, axis=0)).reshape(own_blocks, TILE)
    part_a = jnp.log2(jnp.sum(source_mass))
    part_b = jnp.log2(jnp.sum(target_mass))

    shape = jax.ShapeDtypeStruct
    epsilon = first_epsilon
    part, tiles, halves, half_x = pl.pallas_call(
        functools.partial(row_pass_kernel, LOG2E / epsilon, True, slots),
        out_shape=(
            shape((row_blocks, TILE), f32),
            pltpu.VMEM((row_blocks, width, slots * TILE), jnp.bfloat16),
            shape((row_blocks * slots, TILE), f32),
            shape((row_blocks, TILE), f32),
        ),
        in_specs=[SMEM(), SMEM(), VMEM(), pl.BlockSpec(memory_space=pl.ANY)],
        out_specs=(VMEM(), VMEM(), VMEM(), VMEM()),
        scratch_shapes=[
            pltpu.VMEM((TILE, row_blocks), f32),
            pltpu.SemaphoreType.DMA((row_blocks,)),
        ],
        name="row_pass_first",
        **PARAMS,
    )(cols, counts, source_points, target_points)
    tiles = pltpu.with_memory_space_constraint(tiles, pltpu.VMEM)

    f_pot = jnp.zeros((row_blocks, TILE), f32)
    g_own = -own_half
    g_pot = halves
    total_a = total_b = None
    for step in range(ITERS):
        epsilon = first_epsilon * 0.5**step
        kappa = LOG2E / epsilon
        if step > 0:
            part = pl.pallas_call(
                functools.partial(row_pass_kernel, kappa, False, slots),
                out_shape=shape((row_blocks, TILE), f32),
                in_specs=[SMEM(), SMEM(), VMEM(), VMEM(), VMEM(), VMEM()],
                out_specs=VMEM(),
                scratch_shapes=[pltpu.VMEM((TILE, row_blocks), f32)],
                name="row_pass",
                **PARAMS,
            )(cols, counts, source_points, tiles, f_pot, g_pot)
        if step == 0:
            extra = jnp.full((16, TILE), part_b, f32)
            both = over_cols(jnp.concatenate([part, extra], axis=0), col_devices)
            part, total_b = both[:row_blocks], both[row_blocks, 0]
        else:
            part = over_cols(part, col_devices)
        f_pot = f_pot + (epsilon * LN2) * (log_a - part)

        part = pl.pallas_call(
            functools.partial(col_pass_kernel, kappa, step == 0, slots),
            out_shape=shape((target_blocks, TILE), f32),
            in_specs=[SMEM(), SMEM(), VMEM(), VMEM(), VMEM(), VMEM()],
            out_specs=VMEM(),
            scratch_shapes=[pltpu.VMEM((target_blocks, TILE), f32)],
            name="col_pass",
            **PARAMS,
        )(cols, counts, source_points, tiles, f_pot, g_pot)
        part = part.reshape(row_devices, own_blocks, TILE)
        if step == 0:
            extra = jnp.full((row_devices, 8, TILE), part_a, f32)
            part = jnp.concatenate([part, extra], axis=1)
        part = lse(lax.all_to_all(part, "row", 0, 0))
        if step == 0:
            part, total_a = part[:own_blocks], part[own_blocks, 0]
        g_own = g_own + (epsilon * LN2) * (log_b - part)
        send = g_own
        if step == ITERS - 1:
            both_eps = first_epsilon * (2.0 - 0.5**step)
            send = g_own + own_half + (both_eps * LN2) * (total_a - total_b)
        g_pot = lax.all_to_all(
            jnp.broadcast_to(send[None], (row_devices, own_blocks, TILE)), "row", 0, 0
        ).reshape(target_blocks, TILE)

    earlier = first_epsilon * (2.0 - 0.5 ** (ITERS - 1)) - epsilon
    source = f_pot + half_x - LN2 * (epsilon * total_a + earlier * (total_a - total_b))
    return (source.reshape(rows), g_pot.reshape(target_cells))


def solution(mesh):
    return jax.shard_map(
        body,
        mesh=mesh,
        in_specs=(
            P(None, "row"),
            P(None, "col"),
            P("row"),
            P("col"),
            P("row", "col", None),
            P("row", "col"),
        ),
        out_specs=(P("row"), P("col")),
        check_vma=False,
    )
```

```python
import functools
import math

import jax
import jax.numpy as jnp
from jax import lax
from jax.experimental import pallas as pl
from jax.experimental.pallas import tpu as pltpu
from jax.sharding import PartitionSpec as P

ITERS = 2
TILE = 128
very_negative = -1e30
first_epsilon = 0.5
LOG2E = 1.4426950408889634
LN2 = 0.6931471805599453
SMALLEST = 2.0**-100
LARGEST = 2.0**120
VMEM_LIMIT = 16 * 1024 * 1024
UNROLL = 16
CHUNK = 64


def split3(row):
    hi = row.astype(jnp.bfloat16).astype(jnp.float32)
    rest = row - hi
    mid = rest.astype(jnp.bfloat16).astype(jnp.float32)
    lo = (rest - mid).astype(jnp.bfloat16).astype(jnp.float32)
    return hi, mid, lo


def products(x_ref, y_ref, f_ref, cols, slots, r):
    lhs = x_ref[r]
    picked = [
        y_ref[:, pl.ds(pl.multiple_of(cols[r * slots + k] * TILE, TILE), TILE)]
        for k in range(slots)
    ]
    yb = jnp.concatenate(picked, axis=1)
    rhs = [yb, yb]
    if f_ref is not None:
        hi, mid, lo = split3(f_ref[pl.ds(r, 1), :])
        place = lax.broadcasted_iota(jnp.int32, (16, TILE), 0)
        extra = jnp.where(
            place == 0, hi, jnp.where(place == 1, mid, jnp.where(place == 2, lo, 0.0))
        )
        lhs = jnp.concatenate([lhs, extra.astype(jnp.bfloat16).T], axis=1)
        rhs.append(jnp.ones((16, yb.shape[1]), jnp.bfloat16))
    return jnp.dot(lhs, jnp.concatenate(rhs, axis=0), preferred_element_type=jnp.float32)


def shifts(cols, counts, g_ref, slots, r):
    live = counts[r]
    return [
        jnp.where(k < live, g_ref[pl.ds(cols[r * slots + k], 1), :], very_negative)
        for k in range(slots)
    ]


def prepare(kappa, x_hbm, y_hbm, x_ref, x2_ref, y_ref, g_ref, hx_ref, x_in, x_sem, y_sem):
    width = y_ref.shape[0]
    blocks = hx_ref.shape[0]
    target_blocks = g_ref.shape[0]
    chunks = target_blocks // CHUNK
    x_copy = pltpu.make_async_copy(x_hbm, x_in, x_sem)
    x_copy.start()

    def y_copy(c):
        at = pl.ds(pl.multiple_of(c * (CHUNK * TILE), CHUNK * TILE), CHUNK * TILE)
        return pltpu.make_async_copy(y_hbm.at[:, at], y_ref.at[:, at], y_sem.at[c])

    @pl.loop(0, chunks)
    def _(c):
        y_copy(c).start()

    x_copy.wait()

    @pl.loop(0, blocks, unroll=4)
    def _(r):
        xf = x_in[:, pl.ds(pl.multiple_of(r * TILE, TILE), TILE)].astype(jnp.float32)
        hx_ref[pl.ds(r, 1), :] = 0.5 * jnp.sum(xf * xf, axis=0, keepdims=True)
        scaled = xf * kappa
        hi = scaled.astype(jnp.bfloat16)
        lo = (scaled - hi.astype(jnp.float32)).astype(jnp.bfloat16)
        turned = jnp.concatenate([hi, lo], axis=0).T
        x_ref[r] = turned
        x2_ref[r] = turned + turned

    @pl.loop(0, chunks)
    def _(c):
        y_copy(c).wait()

        @pl.loop(0, CHUNK // 8, unroll=2)
        def _(q):
            first = c * CHUNK + q * 8
            at = pl.ds(pl.multiple_of(first * TILE, 8 * TILE), 8 * TILE)
            yf = y_ref[:, at].astype(jnp.float32)
            half = (-0.5 * kappa) * jnp.sum(yf * yf, axis=0, keepdims=True)
            for k in range(8):
                g_ref[pl.ds(first + k, 1), :] = half[:, k * TILE : (k + 1) * TILE]


def row_pass_kernel(kappa, slots, *refs):
    if kappa is not None:
        (cols, counts, x_hbm, y_hbm, out_ref, x_ref, x2_ref, y_ref, g_ref, hx_ref,
         total, x_in, x_sem, y_sem) = refs
        f_ref = None
        prepare(kappa, x_hbm, y_hbm, x_ref, x2_ref, y_ref, g_ref, hx_ref, x_in, x_sem, y_sem)
    else:
        cols, counts, x_ref, y_ref, f_ref, g_ref, out_ref, total = refs
    blocks = out_ref.shape[0]
    lane = lax.broadcasted_iota(jnp.int32, (TILE, TILE), 1)

    @pl.loop(0, blocks, unroll=UNROLL)
    def _(r):
        scores = products(x_ref, y_ref, f_ref, cols, slots, r)
        terms = None
        for k, row in enumerate(shifts(cols, counts, g_ref, slots, r)):
            term = jnp.exp2(scores[:, k * TILE : (k + 1) * TILE] + row)
            terms = term if terms is None else terms + term
        summed = jnp.sum(terms, axis=1, keepdims=True)
        total[...] = jnp.where(lane == r, summed, total[...])

    sums = total[...]
    out_ref[...] = jnp.log2(sums).T
    fine = jnp.logical_and(jnp.min(sums) >= SMALLEST, jnp.max(sums) <= LARGEST)

    @pl.when(jnp.logical_not(fine))
    def _():
        @pl.loop(0, blocks)
        def _(r):
            scores = products(x_ref, y_ref, f_ref, cols, slots, r)
            rows = shifts(cols, counts, g_ref, slots, r)
            parts = [scores[:, k * TILE : (k + 1) * TILE] + row for k, row in enumerate(rows)]
            top = functools.reduce(jnp.maximum, parts)
            top = jnp.max(top, axis=1, keepdims=True)
            terms = sum(jnp.exp2(part - top) for part in parts)
            summed = jnp.sum(terms, axis=1, keepdims=True)
            total[...] = jnp.where(lane == r, top + jnp.log2(summed), total[...])

        out_ref[...] = total[...].T


def col_pass_kernel(slots, with_mass, *refs):
    if with_mass:
        cols, counts, x_ref, y_ref, f_ref, g_ref, mass_ref, out_ref, total = refs
    else:
        cols, counts, x_ref, y_ref, f_ref, g_ref, out_ref, total = refs
    blocks = f_ref.shape[0]
    devices, height, _ = out_ref.shape
    own = total.shape[0] // devices
    total[...] = jnp.zeros_like(total)

    def visit(r, carry):
        least, most = carry
        scores = products(x_ref, y_ref, f_ref, cols, slots, r)
        live = counts[r]
        for k, row in enumerate(shifts(cols, counts, g_ref, slots, r)):
            terms = jnp.exp2(scores[:, k * TILE : (k + 1) * TILE] + row)
            summed = jnp.sum(terms, axis=0, keepdims=True)
            total[pl.ds(cols[r * slots + k], 1), :] += summed
            least = jnp.minimum(least, jnp.where(k < live, summed, 1.0))
            most = jnp.maximum(most, summed)
        return least, most

    ones = jnp.ones((1, TILE), jnp.float32)
    least, most = lax.fori_loop(0, blocks, visit, (ones, ones), unroll=UNROLL)
    fine = jnp.logical_and(jnp.min(least) >= SMALLEST, jnp.max(most) <= LARGEST / blocks)

    @pl.when(fine)
    def _():
        sums = total[...]
        total[...] = jnp.where(sums > 0.0, jnp.log2(sums), very_negative)

    @pl.when(jnp.logical_not(fine))
    def _():
        total[...] = jnp.full_like(total, very_negative)

        @pl.loop(0, blocks)
        def _(r):
            scores = products(x_ref, y_ref, f_ref, cols, slots, r)
            live = counts[r]
            for k, row in enumerate(shifts(cols, counts, g_ref, slots, r)):

                @pl.when(k < live)
                def _():
                    part = scores[:, k * TILE : (k + 1) * TILE] + row
                    top = jnp.max(part, axis=0, keepdims=True)
                    mine = top + jnp.log2(
                        jnp.sum(jnp.exp2(part - top), axis=0, keepdims=True)
                    )
                    at = pl.ds(cols[r * slots + k], 1)
                    old = total[at, :]
                    peak = jnp.maximum(old, mine)
                    total[at, :] = peak + jnp.log2(jnp.exp2(old - peak) + jnp.exp2(mine - peak))

    out_ref[:, :own, :] = total[...].reshape(devices, own, TILE)
    if with_mass:
        mass = mass_ref[...]
        mass = jnp.sum(jnp.sum(mass, axis=0, keepdims=True), axis=1, keepdims=True)
        out_ref[:, own:, :] = jnp.broadcast_to(
            jnp.log2(mass)[None], (devices, height - own, TILE)
        )


SMEM = functools.partial(pl.BlockSpec, memory_space=pltpu.SMEM)
VMEM = functools.partial(pl.BlockSpec, memory_space=pltpu.VMEM)
ANY = functools.partial(pl.BlockSpec, memory_space=pl.ANY)


def first_row_pass(cols, counts, source_points, target_points, slots):
    width, rows = source_points.shape
    blocks = rows // TILE
    target_blocks = target_points.shape[1] // TILE
    shape = jax.ShapeDtypeStruct
    bf16, f32 = jnp.bfloat16, jnp.float32
    return pl.pallas_call(
        functools.partial(row_pass_kernel, LOG2E / first_epsilon, slots),
        out_shape=(
            shape((blocks, TILE), f32),
            pltpu.VMEM((blocks, TILE, 2 * width), bf16),
            pltpu.VMEM((blocks, TILE, 2 * width), bf16),
            pltpu.VMEM(target_points.shape, bf16),
            shape((target_blocks, TILE), f32),
            shape((blocks, TILE), f32),
        ),
        in_specs=[SMEM(), SMEM(), ANY(), ANY()],
        out_specs=(VMEM(),) * 6,
        scratch_shapes=[
            pltpu.VMEM((TILE, blocks), f32),
            pltpu.VMEM(source_points.shape, bf16),
            pltpu.SemaphoreType.DMA,
            pltpu.SemaphoreType.DMA((target_blocks // CHUNK,)),
        ],
        name="row_pass_first",
        compiler_params=pltpu.CompilerParams(vmem_limit_bytes=VMEM_LIMIT),
    )(
        cols,
        counts,
        pltpu.with_memory_space_constraint(source_points, pltpu.HBM),
        pltpu.with_memory_space_constraint(target_points, pltpu.HBM),
    )


def row_pass(cols, counts, x, y, f_pot, g_pot, slots):
    return pl.pallas_call(
        functools.partial(row_pass_kernel, None, slots),
        out_shape=jax.ShapeDtypeStruct(f_pot.shape, jnp.float32),
        in_specs=[SMEM(), SMEM(), VMEM(), VMEM(), VMEM(), VMEM()],
        out_specs=VMEM(),
        scratch_shapes=[pltpu.VMEM((TILE, f_pot.shape[0]), jnp.float32)],
        name="row_pass",
        compiler_params=pltpu.CompilerParams(vmem_limit_bytes=VMEM_LIMIT),
    )(cols, counts, x, y, f_pot, g_pot)


def col_pass(cols, counts, x, y, f_pot, g_pot, mass, slots, devices):
    target_blocks = g_pot.shape[0]
    height = target_blocks // devices + (8 if mass is not None else 0)
    extra = () if mass is None else (mass,)
    return pl.pallas_call(
        functools.partial(col_pass_kernel, slots, mass is not None),
        out_shape=jax.ShapeDtypeStruct((devices, height, TILE), jnp.float32),
        in_specs=[SMEM(), SMEM()] + [VMEM()] * (4 + len(extra)),
        out_specs=VMEM(),
        scratch_shapes=[pltpu.VMEM((target_blocks, TILE), jnp.float32)],
        name="col_pass",
        compiler_params=pltpu.CompilerParams(vmem_limit_bytes=VMEM_LIMIT),
    )(cols, counts, x, y, f_pot, g_pot, *extra)


def lse(stack):
    top = jnp.max(stack, axis=0)
    return top + jnp.log2(jnp.sum(jnp.exp2(stack - top[None]), axis=0))


def shift_z(value, by, cols):
    return lax.ppermute(value, "col", [(i, (i + 2 * by) % cols) for i in range(cols)])


def over_cols(part, cols):
    half = part.shape[0] // 2
    core = lax.axis_index("col") % 2
    swap = [(i, i ^ 1) for i in range(cols)]
    away = lax.dynamic_slice_in_dim(part, (1 - core) * half, half, 0)
    mine = lax.dynamic_slice_in_dim(part, core * half, half, 0)
    mine = lse(jnp.stack([mine, lax.ppermute(away, "col", swap)]))
    chips = cols // 2
    mine = lse(jnp.stack([mine] + [shift_z(mine, by, cols) for by in range(1, chips)]))
    other = lax.ppermute(mine, "col", swap)
    low = jnp.where(core == 0, mine, other)
    high = jnp.where(core == 0, other, mine)
    return jnp.concatenate([low, high], axis=0)


def body(source_points, target_points, source_mass, target_mass, tile_cols, tile_counts):
    width, rows = source_points.shape
    row_blocks = rows // TILE
    target_cells = target_points.shape[1]
    target_blocks = target_cells // TILE
    slots = tile_cols.shape[2]
    row_devices = lax.axis_size("row")
    col_devices = lax.axis_size("col")
    own_blocks = target_blocks // row_devices
    me = lax.axis_index("row")
    f32 = jnp.float32

    cols = tile_cols.reshape(row_blocks * slots)
    counts = tile_counts.reshape(row_blocks)
    mass_a = source_mass.reshape(row_blocks, TILE)
    log_a = jnp.log2(mass_a)
    own_mass = lax.dynamic_slice_in_dim(target_mass, me * own_blocks * TILE, own_blocks * TILE, 0)
    log_b = jnp.log2(own_mass).reshape(own_blocks, TILE)
    part_b = jnp.log2(jnp.sum(target_mass))

    part, x1, x2, y, g_pot, half_x = first_row_pass(
        cols, counts, source_points, target_points, slots
    )
    x1, x2, y = (pltpu.with_memory_space_constraint(v, pltpu.VMEM) for v in (x1, x2, y))

    f_pot = jnp.zeros((row_blocks, TILE), f32)
    g_own = lax.dynamic_slice_in_dim(g_pot, me * own_blocks, own_blocks, 0)
    half_own = g_own * (-LN2 * first_epsilon)
    total_a = total_b = None
    for step in range(ITERS):
        epsilon = first_epsilon * 0.5**step
        x = x1 if step == 0 else x2
        if step > 0:
            part = row_pass(cols, counts, x, y, f_pot, g_pot, slots)
        if step == 0:
            extra = jnp.full((16, TILE), part_b, f32)
            both = over_cols(jnp.concatenate([part, extra], axis=0), col_devices)
            part, total_b = both[:row_blocks], both[row_blocks, 0]
        else:
            part = over_cols(part, col_devices)
        f_pot = f_pot + (log_a - part)

        part = col_pass(
            cols, counts, x, y, f_pot, g_pot, mass_a if step == 0 else None, slots, row_devices
        )
        part = lse(lax.all_to_all(part, "row", 0, 0))
        if step == 0:
            part, total_a = part[:own_blocks], part[own_blocks, 0]
        g_own = g_own + (log_b - part)
        if step < ITERS - 1:
            g_own, f_pot = 2.0 * g_own, 2.0 * f_pot
            send = g_own
        else:
            both_eps = first_epsilon * (2.0 - 0.5**step)
            send = LN2 * (epsilon * g_own + both_eps * (total_a - total_b)) + half_own
        g_pot = lax.all_to_all(
            jnp.broadcast_to(send[None], (row_devices, own_blocks, TILE)), "row", 0, 0
        ).reshape(target_blocks, TILE)

    earlier = first_epsilon * (2.0 - 0.5 ** (ITERS - 1)) - epsilon
    source = half_x + LN2 * (
        epsilon * f_pot - epsilon * total_a - earlier * (total_a - total_b)
    )
    return (source.reshape(rows), g_pot.reshape(target_cells))


def solution(mesh):
    return jax.shard_map(
        body,
        mesh=mesh,
        in_specs=(
            P(None, "row"),
            P(None, "col"),
            P("row"),
            P("col"),
            P("row", "col", None),
            P("row", "col"),
        ),
        out_specs=(P("row"), P("col")),
        check_vma=False,
    )
```

```python
import functools
import math

import jax
import jax.numpy as jnp
from jax import lax
from jax.experimental import pallas as pl
from jax.experimental.pallas import tpu as pltpu
from jax.sharding import PartitionSpec as P

ITERS = 2
TILE = 128
very_negative = -1e30
first_epsilon = 0.5
LOG2E = 1.4426950408889634
LN2 = 0.6931471805599453
SMALLEST = 2.0**-100
LARGEST = 2.0**120
VMEM_LIMIT = 16 * 1024 * 1024
UNROLL = 16
CHUNK = 64
ROW_OFFSET = 64.0
COL_OFFSET = 80.0


def split3(row):
    hi = row.astype(jnp.bfloat16).astype(jnp.float32)
    rest = row - hi
    mid = rest.astype(jnp.bfloat16).astype(jnp.float32)
    lo = (rest - mid).astype(jnp.bfloat16).astype(jnp.float32)
    return hi, mid, lo


def products(x_ref, y_ref, f_ref, cols, slots, r, offset):
    lhs = x_ref[r]
    picked = [
        y_ref[:, pl.ds(pl.multiple_of(cols[k, r] * TILE, TILE), TILE)]
        for k in range(slots)
    ]
    yb = jnp.concatenate(picked, axis=1)
    rhs = [yb, yb]
    if f_ref is not None:
        hi, mid, lo = split3(f_ref[pl.ds(r, 1), :] + offset)
        place = lax.broadcasted_iota(jnp.int32, (16, TILE), 0)
        extra = jnp.where(
            place == 0, hi, jnp.where(place == 1, mid, jnp.where(place == 2, lo, 0.0))
        )
        lhs = jnp.concatenate([lhs, extra.astype(jnp.bfloat16).T], axis=1)
        rhs.append(jnp.ones((16, yb.shape[1]), jnp.bfloat16))
    return jnp.dot(lhs, jnp.concatenate(rhs, axis=0), preferred_element_type=jnp.float32)


def shifts(cols, counts, g_ref, slots, r):
    live = counts[r]
    return [
        jnp.where(k < live, g_ref[pl.ds(cols[k, r], 1), :], very_negative)
        for k in range(slots)
    ]


def prepare(kappa, x_hbm, y_hbm, x_ref, x2_ref, y_ref, g_ref, hx_ref, x_in, x_sem, y_sem, others):
    width = y_ref.shape[0]
    blocks = hx_ref.shape[0]
    target_blocks = g_ref.shape[0]
    chunks = target_blocks // CHUNK
    x_copy = pltpu.make_async_copy(x_hbm, x_in, x_sem)
    x_copy.start()

    def y_copy(c):
        at = pl.ds(pl.multiple_of(c * (CHUNK * TILE), CHUNK * TILE), CHUNK * TILE)
        return pltpu.make_async_copy(y_hbm.at[:, at], y_ref.at[:, at], y_sem.at[c])

    for other in others:
        other.start()

    @pl.loop(0, chunks)
    def _(c):
        y_copy(c).start()

    x_copy.wait()

    @pl.loop(0, blocks, unroll=4)
    def _(r):
        xf = x_in[:, pl.ds(pl.multiple_of(r * TILE, TILE), TILE)].astype(jnp.float32)
        hx_ref[pl.ds(r, 1), :] = 0.5 * jnp.sum(xf * xf, axis=0, keepdims=True)
        scaled = xf * kappa
        hi = scaled.astype(jnp.bfloat16)
        lo = (scaled - hi.astype(jnp.float32)).astype(jnp.bfloat16)
        turned = jnp.concatenate([hi, lo], axis=0).T
        x_ref[r] = turned
        x2_ref[r] = turned + turned

    @pl.loop(0, chunks)
    def _(c):
        y_copy(c).wait()

        @pl.loop(0, CHUNK // 8, unroll=2)
        def _(q):
            first = c * CHUNK + q * 8
            at = pl.ds(pl.multiple_of(first * TILE, 8 * TILE), 8 * TILE)
            yf = y_ref[:, at].astype(jnp.float32)
            half = (-0.5 * kappa) * jnp.sum(yf * yf, axis=0, keepdims=True)
            for k in range(8):
                g_ref[pl.ds(first + k, 1), :] = half[:, k * TILE : (k + 1) * TILE]

    for other in others:
        other.wait()


def row_pass_kernel(kappa, slots, *refs):
    if kappa is not None:
        (cols, counts, first_own, a_hbm, b_hbm, x_hbm, y_hbm, out_ref, x_ref, x2_ref, y_ref,
         g_ref, hx_ref, a_ref, b_ref, own_ref, total, x_in, b_in, sems, y_sem) = refs
        f_ref = None
        a_copy = pltpu.make_async_copy(a_hbm, a_ref, sems.at[1])
        b_copy = pltpu.make_async_copy(b_hbm, b_in, sems.at[2])
        prepare(kappa, x_hbm, y_hbm, x_ref, x2_ref, y_ref, g_ref, hx_ref, x_in, sems.at[0],
                y_sem, (a_copy, b_copy))
        own = pl.ds(pl.multiple_of(first_own[0], own_ref.shape[0]), own_ref.shape[0])
        own_ref[...] = g_ref[own, :]
        b_ref[...] = jnp.log2(b_in[own, :])
        offset = 0.0
    else:
        cols, counts, x_ref, y_ref, f_ref, g_ref, out_ref, total = refs
        offset = ROW_OFFSET
    blocks = total.shape[1]
    lane = lax.broadcasted_iota(jnp.int32, (TILE, TILE), 1)

    @pl.loop(0, blocks, unroll=UNROLL)
    def _(r):
        scores = products(x_ref, y_ref, f_ref, cols, slots, r, offset)
        terms = None
        for k, row in enumerate(shifts(cols, counts, g_ref, slots, r)):
            term = jnp.exp2(scores[:, k * TILE : (k + 1) * TILE] + row)
            terms = term if terms is None else terms + term
        summed = jnp.sum(terms, axis=1, keepdims=True)
        total[...] = jnp.where(lane == r, summed, total[...])

    sums = total[...]
    out_ref[:blocks, :] = (jnp.log2(sums) - offset).T
    if kappa is not None:
        mass = jnp.sum(jnp.sum(b_in[...], axis=0, keepdims=True), axis=1, keepdims=True)
        out_ref[blocks:, :] = jnp.broadcast_to(jnp.log2(mass), (8, TILE))
        a_ref[...] = jnp.log2(a_ref[...])
    fine = jnp.logical_and(jnp.min(sums) >= SMALLEST, jnp.max(sums) <= LARGEST)

    @pl.when(jnp.logical_not(fine))
    def _():
        @pl.loop(0, blocks)
        def _(r):
            scores = products(x_ref, y_ref, f_ref, cols, slots, r, offset)
            rows = shifts(cols, counts, g_ref, slots, r)
            parts = [scores[:, k * TILE : (k + 1) * TILE] + row for k, row in enumerate(rows)]
            top = functools.reduce(jnp.maximum, parts)
            top = jnp.max(top, axis=1, keepdims=True)
            terms = sum(jnp.exp2(part - top) for part in parts)
            summed = jnp.sum(terms, axis=1, keepdims=True)
            total[...] = jnp.where(lane == r, top + jnp.log2(summed), total[...])

        out_ref[:blocks, :] = (total[...] - offset).T


def col_pass_kernel(slots, with_mass, *refs):
    if with_mass:
        cols, counts, x_ref, y_ref, f_ref, g_ref, mass_ref, out_ref, total = refs
    else:
        cols, counts, x_ref, y_ref, f_ref, g_ref, out_ref, total = refs
    blocks = f_ref.shape[0]
    devices, height, _ = out_ref.shape
    own = total.shape[0] // devices
    total[...] = jnp.zeros_like(total)

    def visit(r, carry):
        least, most = carry
        scores = products(x_ref, y_ref, f_ref, cols, slots, r, COL_OFFSET)
        live = counts[r]
        for k, row in enumerate(shifts(cols, counts, g_ref, slots, r)):
            terms = jnp.exp2(scores[:, k * TILE : (k + 1) * TILE] + row)
            summed = jnp.sum(terms, axis=0, keepdims=True)
            total[pl.ds(cols[k, r], 1), :] += summed
            least = jnp.minimum(least, jnp.where(k < live, summed, 1.0))
            most = jnp.maximum(most, summed)
        return least, most

    ones = jnp.ones((1, TILE), jnp.float32)
    least, most = lax.fori_loop(0, blocks, visit, (ones, ones), unroll=UNROLL)
    fine = jnp.logical_and(jnp.min(least) >= SMALLEST, jnp.max(most) <= LARGEST / blocks)

    @pl.when(fine)
    def _():
        sums = total[...]
        total[...] = jnp.where(sums > 0.0, jnp.log2(sums) - COL_OFFSET, very_negative)

    @pl.when(jnp.logical_not(fine))
    def _():
        total[...] = jnp.full_like(total, very_negative)

        @pl.loop(0, blocks)
        def _(r):
            scores = products(x_ref, y_ref, f_ref, cols, slots, r, COL_OFFSET)
            live = counts[r]
            for k, row in enumerate(shifts(cols, counts, g_ref, slots, r)):

                @pl.when(k < live)
                def _():
                    part = scores[:, k * TILE : (k + 1) * TILE] + row
                    top = jnp.max(part, axis=0, keepdims=True)
                    summed = jnp.sum(jnp.exp2(part - top), axis=0, keepdims=True)
                    mine = top - COL_OFFSET + jnp.log2(summed)
                    at = pl.ds(cols[k, r], 1)
                    old = total[at, :]
                    peak = jnp.maximum(old, mine)
                    total[at, :] = peak + jnp.log2(jnp.exp2(old - peak) + jnp.exp2(mine - peak))

    out_ref[:, :own, :] = total[...].reshape(devices, own, TILE)
    if with_mass:
        mass = mass_ref[...]
        mass = jnp.sum(jnp.sum(mass, axis=0, keepdims=True), axis=1, keepdims=True)
        out_ref[:, own:, :] = jnp.broadcast_to(
            jnp.log2(mass)[None], (devices, height - own, TILE)
        )


SMEM = functools.partial(pl.BlockSpec, memory_space=pltpu.SMEM)
VMEM = functools.partial(pl.BlockSpec, memory_space=pltpu.VMEM)
ANY = functools.partial(pl.BlockSpec, memory_space=pl.ANY)


def first_row_pass(cols, counts, own, source_mass, target_mass, source_points, target_points, slots):
    width, rows = source_points.shape
    blocks = rows // TILE
    target_blocks = target_points.shape[1] // TILE
    devices = lax.axis_size("row")
    shape = jax.ShapeDtypeStruct
    bf16, f32 = jnp.bfloat16, jnp.float32
    in_hbm = [
        pltpu.with_memory_space_constraint(v, pltpu.HBM)
        for v in (source_mass, target_mass, source_points, target_points)
    ]
    return pl.pallas_call(
        functools.partial(row_pass_kernel, LOG2E / first_epsilon, slots),
        out_shape=(
            shape((blocks + 8, TILE), f32),
            pltpu.VMEM((blocks, TILE, 2 * width), bf16),
            pltpu.VMEM((blocks, TILE, 2 * width), bf16),
            pltpu.VMEM(target_points.shape, bf16),
            shape((target_blocks, TILE), f32),
            shape((blocks, TILE), f32),
            shape((blocks, TILE), f32),
            shape((target_blocks // devices, TILE), f32),
            shape((target_blocks // devices, TILE), f32),
        ),
        in_specs=[SMEM(), SMEM(), SMEM(), ANY(), ANY(), ANY(), ANY()],
        out_specs=(VMEM(),) * 9,
        scratch_shapes=[
            pltpu.VMEM((TILE, blocks), f32),
            pltpu.VMEM(source_points.shape, bf16),
            pltpu.VMEM((target_blocks, TILE), f32),
            pltpu.SemaphoreType.DMA((3,)),
            pltpu.SemaphoreType.DMA((target_blocks // CHUNK,)),
        ],
        name="row_pass_first",
        compiler_params=pltpu.CompilerParams(vmem_limit_bytes=VMEM_LIMIT),
    )(cols, counts, own, *in_hbm)


def row_pass(cols, counts, x, y, f_pot, g_pot, slots):
    return pl.pallas_call(
        functools.partial(row_pass_kernel, None, slots),
        out_shape=jax.ShapeDtypeStruct(f_pot.shape, jnp.float32),
        in_specs=[SMEM(), SMEM(), VMEM(), VMEM(), VMEM(), VMEM()],
        out_specs=VMEM(),
        scratch_shapes=[pltpu.VMEM((TILE, f_pot.shape[0]), jnp.float32)],
        name="row_pass",
        compiler_params=pltpu.CompilerParams(vmem_limit_bytes=VMEM_LIMIT),
    )(cols, counts, x, y, f_pot, g_pot)


def col_pass(cols, counts, x, y, f_pot, g_pot, mass, slots, devices):
    target_blocks = g_pot.shape[0]
    height = target_blocks // devices + (8 if mass is not None else 0)
    extra = () if mass is None else (mass,)
    return pl.pallas_call(
        functools.partial(col_pass_kernel, slots, mass is not None),
        out_shape=jax.ShapeDtypeStruct((devices, height, TILE), jnp.float32),
        in_specs=[SMEM(), SMEM()] + [VMEM()] * (4 + len(extra)),
        out_specs=VMEM(),
        scratch_shapes=[pltpu.VMEM((target_blocks, TILE), jnp.float32)],
        name="col_pass",
        compiler_params=pltpu.CompilerParams(vmem_limit_bytes=VMEM_LIMIT),
    )(cols, counts, x, y, f_pot, g_pot, *extra)


def lse(stack):
    top = jnp.max(stack, axis=0)
    return top + jnp.log2(jnp.sum(jnp.exp2(stack - top[None]), axis=0))


def lse_two(one, two):
    top = jnp.maximum(one, two)
    return top + jnp.log2(1.0 + jnp.exp2(jnp.minimum(one, two) - top))


def over_cols(part, cols):
    for mask in (1, 2, 6):
        pairs = [(i, i ^ mask) for i in range(cols)]
        part = lse_two(part, lax.ppermute(part, "col", pairs))
    return part


def exchange(blocks, rest):
    blocks, rest = lax.optimization_barrier((blocks, rest))
    return lax.optimization_barrier((lax.all_to_all(blocks, "row", 0, 0), rest))


def body(source_points, target_points, source_mass, target_mass, tile_cols, tile_counts):
    width, rows = source_points.shape
    row_blocks = rows // TILE
    target_cells = target_points.shape[1]
    target_blocks = target_cells // TILE
    slots = tile_cols.shape[2]
    row_devices = lax.axis_size("row")
    col_devices = lax.axis_size("col")
    own_blocks = target_blocks // row_devices

    cols = tile_cols.transpose(1, 2, 0).reshape(slots, row_blocks)
    counts = tile_counts.reshape(row_blocks)
    mass_a = source_mass.reshape(row_blocks, TILE)
    first_own = (lax.axis_index("row") * own_blocks).reshape(1)

    part, x1, x2, y, g_pot, half_x, log_a, log_b, g_own = first_row_pass(
        cols,
        counts,
        first_own,
        mass_a,
        target_mass.reshape(target_blocks, TILE),
        source_points,
        target_points,
        slots,
    )
    x1, x2, y = (pltpu.with_memory_space_constraint(v, pltpu.VMEM) for v in (x1, x2, y))

    half_own = g_own * (-LN2 * first_epsilon)
    f_pot = total_a = total_b = None
    for step in range(ITERS):
        epsilon = first_epsilon * 0.5**step
        x = x1 if step == 0 else x2
        if step == 0:
            both = over_cols(part, col_devices)
            part, total_b = both[:row_blocks], both[row_blocks, 0]
            f_pot = log_a - part
        else:
            part = over_cols(row_pass(cols, counts, x, y, f_pot, g_pot, slots), col_devices)
            f_pot = f_pot + (log_a - part)

        part = col_pass(
            cols, counts, x, y, f_pot, g_pot, mass_a if step == 0 else None, slots, row_devices
        )
        if step == ITERS - 1:
            earlier = first_epsilon * (2.0 - 0.5**step) - epsilon
            source = half_x + LN2 * (
                epsilon * f_pot - epsilon * total_a - earlier * (total_a - total_b)
            )
            rest = (source, log_b, g_own, half_own, total_a - total_b)
        else:
            rest = (f_pot, half_x, log_a, log_b, g_own, half_own, total_b)
        stack, rest = exchange(part, rest)
        part = lse(stack)
        if step == 0:
            f_pot, half_x, log_a, log_b, g_own, half_own, total_b = rest
            part, total_a = part[:own_blocks], part[own_blocks, 0]
        else:
            source, log_b, g_own, half_own, totals = rest
        g_own = g_own + (log_b - part)
        if step < ITERS - 1:
            g_own, f_pot = 2.0 * g_own, 2.0 * f_pot
            send = g_own
            rest = (f_pot, half_x, log_a, log_b, g_own, half_own, total_a, total_b)
        else:
            both_eps = first_epsilon * (2.0 - 0.5**step)
            send = LN2 * (epsilon * g_own + both_eps * totals) + half_own
            rest = (source,)
        send = jnp.broadcast_to(send[None], (row_devices, own_blocks, TILE))
        g_pot, rest = exchange(send, rest)
        g_pot = g_pot.reshape(target_blocks, TILE)
        if step < ITERS - 1:
            f_pot, half_x, log_a, log_b, g_own, half_own, total_a, total_b = rest
    return (rest[0].reshape(rows), g_pot.reshape(target_cells))


def solution(mesh):
    return jax.shard_map(
        body,
        mesh=mesh,
        in_specs=(
            P(None, "row"),
            P(None, "col"),
            P("row"),
            P("col"),
            P("row", "col", None),
            P("row", "col"),
        ),
        out_specs=(P("row"), P("col")),
        check_vma=False,
    )
```

```python
import functools
import math

import jax
import jax.numpy as jnp
from jax import lax
from jax.experimental import pallas as pl
from jax.experimental.pallas import tpu as pltpu
from jax.sharding import PartitionSpec as P

ITERS = 2
TILE = 128
very_negative = -1e30
first_epsilon = 0.5
LOG2E = 1.4426950408889634
LN2 = 0.6931471805599453
SMALLEST = 2.0**-100
LARGEST = 2.0**120
VMEM_LIMIT = 16 * 1024 * 1024
UNROLL = 16
CHUNK = 64
ROW_OFFSET = 64.0
COL_OFFSET = 80.0


def split3(row):
    hi = row.astype(jnp.bfloat16).astype(jnp.float32)
    rest = row - hi
    mid = rest.astype(jnp.bfloat16).astype(jnp.float32)
    lo = (rest - mid).astype(jnp.bfloat16).astype(jnp.float32)
    return hi, mid, lo


def products(x_ref, y_ref, f_ref, cols, slots, r, offset):
    lhs = x_ref[r]
    picked = [
        y_ref[:, pl.ds(pl.multiple_of(cols[k, r] * TILE, TILE), TILE)]
        for k in range(slots)
    ]
    yb = jnp.concatenate(picked, axis=1)
    rhs = [yb, yb]
    if f_ref is not None:
        hi, mid, lo = split3(f_ref[pl.ds(r, 1), :] + offset)
        place = lax.broadcasted_iota(jnp.int32, (16, TILE), 0)
        extra = jnp.where(
            place == 0, hi, jnp.where(place == 1, mid, jnp.where(place == 2, lo, 0.0))
        )
        lhs = jnp.concatenate([lhs, extra.astype(jnp.bfloat16).T], axis=1)
        rhs.append(jnp.ones((16, yb.shape[1]), jnp.bfloat16))
    return jnp.dot(lhs, jnp.concatenate(rhs, axis=0), preferred_element_type=jnp.float32)


def shifts(cols, counts, g_ref, slots, r):
    live = counts[r]
    return [
        jnp.where(k < live, g_ref[pl.ds(cols[k, r], 1), :], very_negative)
        for k in range(slots)
    ]


def prepare(kappa, x_hbm, y_hbm, x_ref, x2_ref, y_ref, g_ref, hx_ref, x_in, x_sem, y_sem, others):
    width = y_ref.shape[0]
    blocks = hx_ref.shape[0]
    target_blocks = g_ref.shape[0]
    chunks = target_blocks // CHUNK
    x_copy = pltpu.make_async_copy(x_hbm, x_in, x_sem)
    x_copy.start()

    def y_copy(c):
        at = pl.ds(pl.multiple_of(c * (CHUNK * TILE), CHUNK * TILE), CHUNK * TILE)
        return pltpu.make_async_copy(y_hbm.at[:, at], y_ref.at[:, at], y_sem.at[c])

    for other in others:
        other.start()

    @pl.loop(0, chunks)
    def _(c):
        y_copy(c).start()

    x_copy.wait()

    @pl.loop(0, blocks, unroll=4)
    def _(r):
        xf = x_in[:, pl.ds(pl.multiple_of(r * TILE, TILE), TILE)].astype(jnp.float32)
        hx_ref[pl.ds(r, 1), :] = 0.5 * jnp.sum(xf * xf, axis=0, keepdims=True)
        scaled = xf * kappa
        hi = scaled.astype(jnp.bfloat16)
        lo = (scaled - hi.astype(jnp.float32)).astype(jnp.bfloat16)
        turned = jnp.concatenate([hi, lo], axis=0).T
        x_ref[r] = turned
        x2_ref[r] = turned + turned

    @pl.loop(0, chunks)
    def _(c):
        y_copy(c).wait()

        @pl.loop(0, CHUNK // 8, unroll=2)
        def _(q):
            first = c * CHUNK + q * 8
            at = pl.ds(pl.multiple_of(first * TILE, 8 * TILE), 8 * TILE)
            yf = y_ref[:, at].astype(jnp.float32)
            half = (-0.5 * kappa) * jnp.sum(yf * yf, axis=0, keepdims=True)
            for k in range(8):
                g_ref[pl.ds(first + k, 1), :] = half[:, k * TILE : (k + 1) * TILE]

    for other in others:
        other.wait()


def row_pass_kernel(kappa, slots, *refs):
    if kappa is not None:
        (first_own, cols_hbm, counts_hbm, a_hbm, b_hbm, x_hbm, y_hbm, out_ref, x_ref, x2_ref,
         y_ref, g_ref, hx_ref, a_ref, b_ref, own_ref, total, x_in, b_in, cols, counts, sems,
         y_sem) = refs
        f_ref = None
        small = ((a_hbm, a_ref), (b_hbm, b_in), (cols_hbm, cols), (counts_hbm, counts))
        others = [
            pltpu.make_async_copy(source, target, sems.at[1 + i])
            for i, (source, target) in enumerate(small)
        ]
        prepare(kappa, x_hbm, y_hbm, x_ref, x2_ref, y_ref, g_ref, hx_ref, x_in, sems.at[0],
                y_sem, others)
        own = pl.ds(pl.multiple_of(first_own[0], own_ref.shape[0]), own_ref.shape[0])
        own_ref[...] = g_ref[own, :]
        b_ref[...] = jnp.log2(b_in[own, :])
        offset = 0.0
    else:
        cols, counts, x_ref, y_ref, f_ref, g_ref, out_ref, total = refs
        offset = ROW_OFFSET
    blocks = total.shape[1]
    lane = lax.broadcasted_iota(jnp.int32, (TILE, TILE), 1)

    @pl.loop(0, blocks, unroll=UNROLL)
    def _(r):
        scores = products(x_ref, y_ref, f_ref, cols, slots, r, offset)
        terms = None
        for k, row in enumerate(shifts(cols, counts, g_ref, slots, r)):
            term = jnp.exp2(scores[:, k * TILE : (k + 1) * TILE] + row)
            terms = term if terms is None else terms + term
        summed = jnp.sum(terms, axis=1, keepdims=True)
        total[...] = jnp.where(lane == r, summed, total[...])

    sums = total[...]
    out_ref[:blocks, :] = (jnp.log2(sums) - offset).T
    if kappa is not None:
        mass = jnp.sum(jnp.sum(b_in[...], axis=0, keepdims=True), axis=1, keepdims=True)
        out_ref[blocks:, :] = jnp.broadcast_to(jnp.log2(mass), (8, TILE))
        a_ref[...] = jnp.log2(a_ref[...])
    fine = jnp.logical_and(jnp.min(sums) >= SMALLEST, jnp.max(sums) <= LARGEST)

    @pl.when(jnp.logical_not(fine))
    def _():
        @pl.loop(0, blocks)
        def _(r):
            scores = products(x_ref, y_ref, f_ref, cols, slots, r, offset)
            rows = shifts(cols, counts, g_ref, slots, r)
            parts = [scores[:, k * TILE : (k + 1) * TILE] + row for k, row in enumerate(rows)]
            top = functools.reduce(jnp.maximum, parts)
            top = jnp.max(top, axis=1, keepdims=True)
            terms = sum(jnp.exp2(part - top) for part in parts)
            summed = jnp.sum(terms, axis=1, keepdims=True)
            total[...] = jnp.where(lane == r, top + jnp.log2(summed), total[...])

        out_ref[:blocks, :] = (total[...] - offset).T


def col_pass_kernel(slots, with_mass, *refs):
    if with_mass:
        cols, counts, x_ref, y_ref, f_ref, g_ref, mass_ref, out_ref, total = refs
    else:
        cols, counts, x_ref, y_ref, f_ref, g_ref, out_ref, total = refs
    blocks = f_ref.shape[0]
    devices, height, _ = out_ref.shape
    own = total.shape[0] // devices
    total[...] = jnp.zeros_like(total)

    def visit(r, carry):
        least, most = carry
        scores = products(x_ref, y_ref, f_ref, cols, slots, r, COL_OFFSET)
        live = counts[r]
        for k, row in enumerate(shifts(cols, counts, g_ref, slots, r)):
            terms = jnp.exp2(scores[:, k * TILE : (k + 1) * TILE] + row)
            summed = jnp.sum(terms, axis=0, keepdims=True)
            total[pl.ds(cols[k, r], 1), :] += summed
            least = jnp.minimum(least, jnp.where(k < live, summed, 1.0))
            most = jnp.maximum(most, summed)
        return least, most

    ones = jnp.ones((1, TILE), jnp.float32)
    least, most = lax.fori_loop(0, blocks, visit, (ones, ones), unroll=UNROLL)
    fine = jnp.logical_and(jnp.min(least) >= SMALLEST, jnp.max(most) <= LARGEST / blocks)

    @pl.when(fine)
    def _():
        sums = total[...]
        total[...] = jnp.where(sums > 0.0, jnp.log2(sums) - COL_OFFSET, very_negative)

    @pl.when(jnp.logical_not(fine))
    def _():
        total[...] = jnp.full_like(total, very_negative)

        @pl.loop(0, blocks)
        def _(r):
            scores = products(x_ref, y_ref, f_ref, cols, slots, r, COL_OFFSET)
            live = counts[r]
            for k, row in enumerate(shifts(cols, counts, g_ref, slots, r)):

                @pl.when(k < live)
                def _():
                    part = scores[:, k * TILE : (k + 1) * TILE] + row
                    top = jnp.max(part, axis=0, keepdims=True)
                    summed = jnp.sum(jnp.exp2(part - top), axis=0, keepdims=True)
                    mine = top - COL_OFFSET + jnp.log2(summed)
                    at = pl.ds(cols[k, r], 1)
                    old = total[at, :]
                    peak = jnp.maximum(old, mine)
                    total[at, :] = peak + jnp.log2(jnp.exp2(old - peak) + jnp.exp2(mine - peak))

    out_ref[:, :own, :] = total[...].reshape(devices, own, TILE)
    if with_mass:
        mass = mass_ref[...]
        mass = jnp.sum(jnp.sum(mass, axis=0, keepdims=True), axis=1, keepdims=True)
        out_ref[:, own:, :] = jnp.broadcast_to(
            jnp.log2(mass)[None], (devices, height - own, TILE)
        )


SMEM = functools.partial(pl.BlockSpec, memory_space=pltpu.SMEM)
VMEM = functools.partial(pl.BlockSpec, memory_space=pltpu.VMEM)
ANY = functools.partial(pl.BlockSpec, memory_space=pl.ANY)


def first_row_pass(cols, counts, own, source_mass, target_mass, source_points, target_points, slots):
    width, rows = source_points.shape
    blocks = rows // TILE
    target_blocks = target_points.shape[1] // TILE
    devices = lax.axis_size("row")
    shape = jax.ShapeDtypeStruct
    bf16, f32 = jnp.bfloat16, jnp.float32
    in_hbm = [
        pltpu.with_memory_space_constraint(v, pltpu.HBM)
        for v in (cols, counts, source_mass, target_mass, source_points, target_points)
    ]
    return pl.pallas_call(
        functools.partial(row_pass_kernel, LOG2E / first_epsilon, slots),
        out_shape=(
            shape((blocks + 8, TILE), f32),
            pltpu.VMEM((blocks, TILE, 2 * width), bf16),
            pltpu.VMEM((blocks, TILE, 2 * width), bf16),
            pltpu.VMEM(target_points.shape, bf16),
            shape((target_blocks, TILE), f32),
            shape((blocks, TILE), f32),
            shape((blocks, TILE), f32),
            shape((target_blocks // devices, TILE), f32),
            shape((target_blocks // devices, TILE), f32),
        ),
        in_specs=[SMEM()] + [ANY()] * 6,
        out_specs=(VMEM(),) * 9,
        scratch_shapes=[
            pltpu.VMEM((TILE, blocks), f32),
            pltpu.VMEM(source_points.shape, bf16),
            pltpu.VMEM((target_blocks, TILE), f32),
            pltpu.SMEM(cols.shape, jnp.int32),
            pltpu.SMEM(counts.shape, jnp.int32),
            pltpu.SemaphoreType.DMA((5,)),
            pltpu.SemaphoreType.DMA((target_blocks // CHUNK,)),
        ],
        name="row_pass_first",
        compiler_params=pltpu.CompilerParams(vmem_limit_bytes=VMEM_LIMIT),
    )(own, *in_hbm)


def row_pass(cols, counts, x, y, f_pot, g_pot, slots):
    return pl.pallas_call(
        functools.partial(row_pass_kernel, None, slots),
        out_shape=jax.ShapeDtypeStruct(f_pot.shape, jnp.float32),
        in_specs=[SMEM(), SMEM(), VMEM(), VMEM(), VMEM(), VMEM()],
        out_specs=VMEM(),
        scratch_shapes=[pltpu.VMEM((TILE, f_pot.shape[0]), jnp.float32)],
        name="row_pass",
        compiler_params=pltpu.CompilerParams(vmem_limit_bytes=VMEM_LIMIT),
    )(cols, counts, x, y, f_pot, g_pot)


def col_pass(cols, counts, x, y, f_pot, g_pot, mass, slots, devices):
    target_blocks = g_pot.shape[0]
    height = target_blocks // devices + (8 if mass is not None else 0)
    extra = () if mass is None else (mass,)
    return pl.pallas_call(
        functools.partial(col_pass_kernel, slots, mass is not None),
        out_shape=jax.ShapeDtypeStruct((devices, height, TILE), jnp.float32),
        in_specs=[SMEM(), SMEM()] + [VMEM()] * (4 + len(extra)),
        out_specs=VMEM(),
        scratch_shapes=[pltpu.VMEM((target_blocks, TILE), jnp.float32)],
        name="col_pass",
        compiler_params=pltpu.CompilerParams(vmem_limit_bytes=VMEM_LIMIT),
    )(cols, counts, x, y, f_pot, g_pot, *extra)


def combine_kernel(epsilon, both_eps, *refs):
    if both_eps is None:
        stack_ref, mass_ref, g_ref, send_ref, new_ref, total_ref = refs
    else:
        stack_ref, mass_ref, g_ref, first_ref, a_ref, b_ref, send_ref = refs
    devices = stack_ref.shape[0]
    own = mass_ref.shape[0]
    top = stack_ref[0]
    for d in range(1, devices):
        top = jnp.maximum(top, stack_ref[d])
    summed = jnp.exp2(stack_ref[0] - top)
    for d in range(1, devices):
        summed += jnp.exp2(stack_ref[d] - top)
    whole = top + jnp.log2(summed)
    new = g_ref[...] + (mass_ref[...] - whole[:own])
    if both_eps is None:
        new = 2.0 * new
        new_ref[...] = new
        total_ref[...] = whole[own:]
    else:
        totals = a_ref[:1, :] - b_ref[:1, :]
        half = first_ref[...] * first_epsilon
        new = LN2 * (epsilon * new + both_eps * totals - half)
    for d in range(devices):
        send_ref[d] = new


def combine(stack, log_b, g_own, last):
    shape = jax.ShapeDtypeStruct
    own = log_b.shape[0]
    send = shape((stack.shape[0], own, TILE), jnp.float32)
    if last is None:
        more, scales = (), (None, None)
        out = (send, shape(log_b.shape, jnp.float32), shape((8, TILE), jnp.float32))
    else:
        more, scales = last[:3], last[3:]
        out = send
    return pl.pallas_call(
        functools.partial(combine_kernel, *scales),
        out_shape=out,
        in_specs=[VMEM()] * (3 + len(more)),
        out_specs=jax.tree.map(lambda _: VMEM(), out),
        name="combine",
        compiler_params=pltpu.CompilerParams(vmem_limit_bytes=VMEM_LIMIT // 2),
    )(stack, log_b, g_own, *more)


def lse_two(one, two):
    top = jnp.maximum(one, two)
    return top + jnp.log2(1.0 + jnp.exp2(jnp.minimum(one, two) - top))


def over_cols(part, cols):
    for mask in (1, 2, 6):
        pairs = [(i, i ^ mask) for i in range(cols)]
        part = lse_two(part, lax.ppermute(part, "col", pairs))
    return part


def exchange(blocks, rest):
    blocks, rest = lax.optimization_barrier((blocks, rest))
    return lax.optimization_barrier((lax.all_to_all(blocks, "row", 0, 0), rest))


def body(source_points, target_points, source_mass, target_mass, tile_cols, tile_counts):
    width, rows = source_points.shape
    row_blocks = rows // TILE
    target_cells = target_points.shape[1]
    target_blocks = target_cells // TILE
    slots = tile_cols.shape[2]
    row_devices = lax.axis_size("row")
    col_devices = lax.axis_size("col")
    own_blocks = target_blocks // row_devices

    cols = tile_cols.transpose(1, 2, 0).reshape(slots, row_blocks)
    counts = tile_counts.reshape(row_blocks)
    mass_a = source_mass.reshape(row_blocks, TILE)
    first_own = (lax.axis_index("row") * own_blocks).reshape(1)

    part, x1, x2, y, g_pot, half_x, log_a, log_b, g_own = first_row_pass(
        cols,
        counts,
        first_own,
        mass_a,
        target_mass.reshape(target_blocks, TILE),
        source_points,
        target_points,
        slots,
    )
    x1, x2, y = (pltpu.with_memory_space_constraint(v, pltpu.VMEM) for v in (x1, x2, y))

    g_first = g_own
    f_pot = total_a = total_b = source = None
    for step in range(ITERS):
        epsilon = first_epsilon * 0.5**step
        x = x1 if step == 0 else x2
        if step == 0:
            both = over_cols(part, col_devices)
            part, total_b = both[:row_blocks], both[row_blocks:]
            f_pot = log_a - part
        else:
            part = over_cols(row_pass(cols, counts, x, y, f_pot, g_pot, slots), col_devices)
            f_pot = f_pot + (log_a - part)

        part = col_pass(
            cols, counts, x, y, f_pot, g_pot, mass_a if step == 0 else None, slots, row_devices
        )
        if step < ITERS - 1:
            f_pot = 2.0 * f_pot
            stack, rest = exchange(part, (f_pot, total_b))
            f_pot, total_b = rest
            send, g_own, total_a = combine(stack, log_b, g_own, None)
            g_pot, rest = exchange(send, (f_pot, total_b))
            f_pot, total_b = rest
        else:
            earlier = first_epsilon * (2.0 - 0.5**step) - epsilon
            totals = epsilon * total_a[:1] + earlier * (total_a[:1] - total_b[:1])
            source = half_x + LN2 * (epsilon * f_pot - totals)
            stack, source = exchange(part, source)
            both_eps = first_epsilon * (2.0 - 0.5**step)
            send = combine(
                stack, log_b, g_own, (g_first, total_a, total_b, epsilon, both_eps)
            )
            g_pot, source = exchange(send, source)
        g_pot = g_pot.reshape(target_blocks, TILE)
    return (source.reshape(rows), g_pot.reshape(target_cells))


def solution(mesh):
    return jax.shard_map(
        body,
        mesh=mesh,
        in_specs=(
            P(None, "row"),
            P(None, "col"),
            P("row"),
            P("col"),
            P("row", "col", None),
            P("row", "col"),
        ),
        out_specs=(P("row"), P("col")),
        check_vma=False,
    )
```

```python
import functools

import jax
import jax.numpy as jnp
from jax import lax
from jax.experimental import pallas as pl
from jax.experimental.pallas import tpu as pltpu
from jax.sharding import PartitionSpec as P

TILE = 128
very_negative = -1e30
first_epsilon = 0.5
LOG2E = 1.4426950408889634
LN2 = 0.6931471805599453
SMALLEST = 2.0**-100
LARGEST = 2.0**120
VMEM_LIMIT = 16 * 1024 * 1024
UNROLL = 16
CHUNK = 64
ROW_OFFSET = 64.0
COL_OFFSET = 80.0


def split3(row):
    hi = row.astype(jnp.bfloat16).astype(jnp.float32)
    rest = row - hi
    mid = rest.astype(jnp.bfloat16).astype(jnp.float32)
    lo = (rest - mid).astype(jnp.bfloat16).astype(jnp.float32)
    return hi, mid, lo


def products(x_ref, y_ref, f_ref, cols, slots, r, offset):
    lhs = x_ref[r]
    picked = [
        y_ref[:, pl.ds(pl.multiple_of(cols[k, r] * TILE, TILE), TILE)]
        for k in range(slots)
    ]
    yb = jnp.concatenate(picked, axis=1)
    rhs = [yb, yb]
    if f_ref is not None:
        hi, mid, lo = split3(f_ref[pl.ds(r, 1), :] + offset)
        place = lax.broadcasted_iota(jnp.int32, (16, TILE), 0)
        extra = jnp.where(
            place == 0, hi, jnp.where(place == 1, mid, jnp.where(place == 2, lo, 0.0))
        )
        lhs = jnp.concatenate([lhs, extra.astype(jnp.bfloat16).T], axis=1)
        rhs.append(jnp.ones((16, yb.shape[1]), jnp.bfloat16))
    return jnp.dot(lhs, jnp.concatenate(rhs, axis=0), preferred_element_type=jnp.float32)


def shifts(cols, counts, g_ref, slots, r):
    live = counts[r]
    return [
        jnp.where(k < live, g_ref[pl.ds(cols[k, r], 1), :], very_negative)
        for k in range(slots)
    ]


def log2_sum(values):
    summed = jnp.sum(jnp.sum(values, axis=0, keepdims=True), axis=1, keepdims=True)
    return jnp.broadcast_to(jnp.log2(summed), (8, TILE))


def prepare(kappa, x_hbm, y_hbm, x_ref, x2_ref, y_ref, g_ref, hx_ref, x_in, x_sem, y_sem, others):
    width = y_ref.shape[0]
    blocks = hx_ref.shape[0]
    target_blocks = g_ref.shape[0]
    chunks = target_blocks // CHUNK
    x_copy = pltpu.make_async_copy(x_hbm, x_in, x_sem)
    x_copy.start()

    def y_copy(c):
        at = pl.ds(pl.multiple_of(c * (CHUNK * TILE), CHUNK * TILE), CHUNK * TILE)
        return pltpu.make_async_copy(y_hbm.at[:, at], y_ref.at[:, at], y_sem.at[c])

    for other in others:
        other.start()

    @pl.loop(0, chunks)
    def _(c):
        y_copy(c).start()

    x_copy.wait()

    @pl.loop(0, blocks, unroll=4)
    def _(r):
        xf = x_in[:, pl.ds(pl.multiple_of(r * TILE, TILE), TILE)].astype(jnp.float32)
        hx_ref[pl.ds(r, 1), :] = 0.5 * jnp.sum(xf * xf, axis=0, keepdims=True)
        scaled = xf * kappa
        hi = scaled.astype(jnp.bfloat16)
        lo = (scaled - hi.astype(jnp.float32)).astype(jnp.bfloat16)
        turned = jnp.concatenate([hi, lo], axis=0).T
        x_ref[r] = turned
        x2_ref[r] = turned + turned

    @pl.loop(0, chunks)
    def _(c):
        y_copy(c).wait()

        @pl.loop(0, CHUNK // 8, unroll=2)
        def _(q):
            first = c * CHUNK + q * 8
            at = pl.ds(pl.multiple_of(first * TILE, 8 * TILE), 8 * TILE)
            yf = y_ref[:, at].astype(jnp.float32)
            half = (-0.5 * kappa) * jnp.sum(yf * yf, axis=0, keepdims=True)
            for k in range(8):
                g_ref[pl.ds(first + k, 1), :] = half[:, k * TILE : (k + 1) * TILE]

    for other in others:
        other.wait()


def row_pass_kernel(kappa, slots, *refs):
    if kappa is not None:
        (cols_hbm, counts_hbm, a_hbm, b_hbm, x_hbm, y_hbm, out_ref, x_ref, x2_ref,
         y_ref, g_ref, hx_ref, a_ref, b_ref, mass_ref, total, x_in, cols, counts, sems, y_sem) = refs
        f_ref = None
        small = ((a_hbm, a_ref), (b_hbm, b_ref), (cols_hbm, cols), (counts_hbm, counts))
        others = [
            pltpu.make_async_copy(source, target, sems.at[1 + i])
            for i, (source, target) in enumerate(small)
        ]
        prepare(kappa, x_hbm, y_hbm, x_ref, x2_ref, y_ref, g_ref, hx_ref, x_in, sems.at[0],
                y_sem, others)
        offset = 0.0
    else:
        (cols, counts, x_ref, y_ref, f_ref, g_ref, g_first_ref, b_ref, mass_ref, out_ref,
         total) = refs
        offset = ROW_OFFSET
    blocks = total.shape[1]
    lane = lax.broadcasted_iota(jnp.int32, (TILE, TILE), 1)

    @pl.loop(0, blocks, unroll=UNROLL)
    def _(r):
        scores = products(x_ref, y_ref, f_ref, cols, slots, r, offset)
        terms = None
        for k, row in enumerate(shifts(cols, counts, g_ref, slots, r)):
            term = jnp.exp2(scores[:, k * TILE : (k + 1) * TILE] + row)
            terms = term if terms is None else terms + term
        summed = jnp.sum(terms, axis=1, keepdims=True)
        total[...] = jnp.where(lane == r, summed, total[...])

    sums = total[...]
    out_ref[:blocks, :] = (jnp.log2(sums) - offset).T
    if kappa is not None:
        mass_ref[...] = log2_sum(b_ref[...])
        a_ref[...] = jnp.log2(a_ref[...])
        b_ref[...] = jnp.log2(b_ref[...])
    else:
        out_ref[blocks : blocks + 8, :] = mass_ref[...]
        last = g_first_ref[...] + b_ref[...] - 0.5 * g_ref[...]
        out_ref[blocks + 8 :, :] = log2_sum(jnp.exp2(last))
    fine = jnp.logical_and(jnp.min(sums) >= SMALLEST, jnp.max(sums) <= LARGEST)

    @pl.when(jnp.logical_not(fine))
    def _():
        @pl.loop(0, blocks)
        def _(r):
            scores = products(x_ref, y_ref, f_ref, cols, slots, r, offset)
            rows = shifts(cols, counts, g_ref, slots, r)
            parts = [scores[:, k * TILE : (k + 1) * TILE] + row for k, row in enumerate(rows)]
            top = functools.reduce(jnp.maximum, parts)
            top = jnp.max(top, axis=1, keepdims=True)
            terms = sum(jnp.exp2(part - top) for part in parts)
            summed = jnp.sum(terms, axis=1, keepdims=True)
            total[...] = jnp.where(lane == r, top + jnp.log2(summed), total[...])

        out_ref[:blocks, :] = (total[...] - offset).T


def col_pass_kernel(slots, *refs):
    cols, counts, x_ref, y_ref, f_ref, g_ref, out_ref, total = refs
    blocks = f_ref.shape[0]
    total[...] = jnp.zeros_like(total)

    def visit(r, carry):
        least, most = carry
        scores = products(x_ref, y_ref, f_ref, cols, slots, r, COL_OFFSET)
        live = counts[r]
        for k, row in enumerate(shifts(cols, counts, g_ref, slots, r)):
            terms = jnp.exp2(scores[:, k * TILE : (k + 1) * TILE] + row)
            summed = jnp.sum(terms, axis=0, keepdims=True)
            total[pl.ds(cols[k, r], 1), :] += summed
            least = jnp.minimum(least, jnp.where(k < live, summed, 1.0))
            most = jnp.maximum(most, summed)
        return least, most

    ones = jnp.ones((1, TILE), jnp.float32)
    least, most = lax.fori_loop(0, blocks, visit, (ones, ones), unroll=UNROLL)
    fine = jnp.logical_and(jnp.min(least) >= SMALLEST, jnp.max(most) <= LARGEST / blocks)

    @pl.when(fine)
    def _():
        sums = total[...]
        total[...] = jnp.where(sums > 0.0, jnp.log2(sums) - COL_OFFSET, very_negative)

    @pl.when(jnp.logical_not(fine))
    def _():
        total[...] = jnp.full_like(total, very_negative)

        @pl.loop(0, blocks)
        def _(r):
            scores = products(x_ref, y_ref, f_ref, cols, slots, r, COL_OFFSET)
            live = counts[r]
            for k, row in enumerate(shifts(cols, counts, g_ref, slots, r)):

                @pl.when(k < live)
                def _():
                    part = scores[:, k * TILE : (k + 1) * TILE] + row
                    top = jnp.max(part, axis=0, keepdims=True)
                    summed = jnp.sum(jnp.exp2(part - top), axis=0, keepdims=True)
                    mine = top - COL_OFFSET + jnp.log2(summed)
                    at = pl.ds(cols[k, r], 1)
                    old = total[at, :]
                    peak = jnp.maximum(old, mine)
                    total[at, :] = peak + jnp.log2(jnp.exp2(old - peak) + jnp.exp2(mine - peak))

    out_ref[...] = total[...].reshape(out_ref.shape)


SMEM = functools.partial(pl.BlockSpec, memory_space=pltpu.SMEM)
VMEM = functools.partial(pl.BlockSpec, memory_space=pltpu.VMEM)
ANY = functools.partial(pl.BlockSpec, memory_space=pl.ANY)


def first_row_pass(cols, counts, source_mass, target_mass, source_points, target_points, slots):
    width, rows = source_points.shape
    blocks = rows // TILE
    target_blocks = target_points.shape[1] // TILE
    shape = jax.ShapeDtypeStruct
    bf16, f32 = jnp.bfloat16, jnp.float32
    in_hbm = [
        pltpu.with_memory_space_constraint(v, pltpu.HBM)
        for v in (cols, counts, source_mass, target_mass, source_points, target_points)
    ]
    return pl.pallas_call(
        functools.partial(row_pass_kernel, LOG2E / first_epsilon, slots),
        out_shape=(
            shape((blocks, TILE), f32),
            pltpu.VMEM((blocks, TILE, 2 * width), bf16),
            pltpu.VMEM((blocks, TILE, 2 * width), bf16),
            pltpu.VMEM(target_points.shape, bf16),
            shape((target_blocks, TILE), f32),
            shape((blocks, TILE), f32),
            shape((blocks, TILE), f32),
            shape((target_blocks, TILE), f32),
            shape((8, TILE), f32),
        ),
        in_specs=[ANY()] * 6,
        out_specs=(VMEM(),) * 9,
        scratch_shapes=[
            pltpu.VMEM((TILE, blocks), f32),
            pltpu.VMEM(source_points.shape, bf16),
            pltpu.SMEM(cols.shape, jnp.int32),
            pltpu.SMEM(counts.shape, jnp.int32),
            pltpu.SemaphoreType.DMA((5,)),
            pltpu.SemaphoreType.DMA((target_blocks // CHUNK,)),
        ],
        name="row_pass_first",
        compiler_params=pltpu.CompilerParams(vmem_limit_bytes=VMEM_LIMIT),
    )(*in_hbm)


def row_pass(cols, counts, x, y, f_pot, g_pot, g_first, log_b, mass, slots):
    return pl.pallas_call(
        functools.partial(row_pass_kernel, None, slots),
        out_shape=jax.ShapeDtypeStruct((f_pot.shape[0] + 16, TILE), jnp.float32),
        in_specs=[SMEM(), SMEM()] + [VMEM()] * 7,
        out_specs=VMEM(),
        scratch_shapes=[pltpu.VMEM((TILE, f_pot.shape[0]), jnp.float32)],
        name="row_pass",
        compiler_params=pltpu.CompilerParams(vmem_limit_bytes=VMEM_LIMIT),
    )(cols, counts, x, y, f_pot, g_pot, g_first, log_b, mass)


def col_pass(cols, counts, x, y, f_pot, g_pot, slots, devices):
    target_blocks = g_pot.shape[0]
    return pl.pallas_call(
        functools.partial(col_pass_kernel, slots),
        out_shape=jax.ShapeDtypeStruct(
            (devices, target_blocks // devices, TILE), jnp.float32
        ),
        in_specs=[SMEM(), SMEM()] + [VMEM()] * 4,
        out_specs=VMEM(),
        scratch_shapes=[pltpu.VMEM((target_blocks, TILE), jnp.float32)],
        name="col_pass",
        compiler_params=pltpu.CompilerParams(vmem_limit_bytes=VMEM_LIMIT),
    )(cols, counts, x, y, f_pot, g_pot)


def combine_kernel(epsilon, both_eps, *refs):
    if both_eps is None:
        first_own, stack_ref, b_ref, g_ref, send_ref, new_ref = refs
    else:
        first_own, stack_ref, b_ref, g_ref, first_ref, totals_ref, send_ref = refs
    devices, own, _ = stack_ref.shape
    here = pl.ds(pl.multiple_of(first_own[0], own), own)
    top = stack_ref[0]
    for d in range(1, devices):
        top = jnp.maximum(top, stack_ref[d])
    summed = jnp.exp2(stack_ref[0] - top)
    for d in range(1, devices):
        summed += jnp.exp2(stack_ref[d] - top)
    gain = b_ref[here, :] - (top + jnp.log2(summed))
    if both_eps is None:
        new = 2.0 * (g_ref[here, :] + gain)
        new_ref[...] = new
    else:
        difference = totals_ref[8:9, :] - totals_ref[:1, :]
        half = first_ref[here, :] * first_epsilon
        new = LN2 * (epsilon * (g_ref[...] + gain) + both_eps * difference - half)
    for d in range(devices):
        send_ref[d] = new


def combine(first_own, stack, log_b, g_pot, last):
    shape = jax.ShapeDtypeStruct
    send = shape(stack.shape, jnp.float32)
    if last is None:
        more, scales = (), (None, None)
        out = (send, shape(stack.shape[1:], jnp.float32))
    else:
        more, scales = last[:2], last[2:]
        out = send
    return pl.pallas_call(
        functools.partial(combine_kernel, *scales),
        out_shape=out,
        in_specs=[SMEM()] + [VMEM()] * (3 + len(more)),
        out_specs=jax.tree.map(lambda _: VMEM(), out),
        name="combine",
        compiler_params=pltpu.CompilerParams(vmem_limit_bytes=VMEM_LIMIT // 2),
    )(first_own, stack, log_b, g_pot, *more)


def lse_of(parts):
    top = functools.reduce(jnp.maximum, parts)
    return top + jnp.log2(sum(jnp.exp2(part - top) for part in parts))


def over_cols(part, cols):
    def moved(value, pairs):
        return lax.ppermute(value, "col", pairs)

    part = lse_of([part, moved(part, [(i, i ^ 1) for i in range(cols)])])
    away = sorted(range(2, cols, 2), key=lambda by: -min(by, cols - by))
    return lse_of([part] + [moved(part, [(i, (i + by) % cols) for i in range(cols)]) for by in away])


def exchange(blocks, rest):
    blocks, rest = lax.optimization_barrier((blocks, rest))
    return lax.optimization_barrier((lax.all_to_all(blocks, "row", 0, 0), rest))


def body(source_points, target_points, source_mass, target_mass, tile_cols, tile_counts):
    width, rows = source_points.shape
    row_blocks = rows // TILE
    target_cells = target_points.shape[1]
    target_blocks = target_cells // TILE
    slots = tile_cols.shape[2]
    row_devices = lax.axis_size("row")
    col_devices = lax.axis_size("col")
    own_blocks = target_blocks // row_devices

    cols = tile_cols.transpose(1, 2, 0).reshape(slots, row_blocks)
    counts = tile_counts.reshape(row_blocks)
    mass_a = source_mass.reshape(row_blocks, TILE)
    first_own = (lax.axis_index("row") * own_blocks).reshape(1)
    counts, first_own = lax.optimization_barrier((counts, first_own))

    part, x1, x2, y, g_first, half_x, log_a, log_b, mass = first_row_pass(
        cols,
        counts,
        mass_a,
        target_mass.reshape(target_blocks, TILE),
        source_points,
        target_points,
        slots,
    )
    x1, x2, y = (pltpu.with_memory_space_constraint(v, pltpu.VMEM) for v in (x1, x2, y))

    f_pot = log_a - over_cols(part, col_devices)
    part = col_pass(cols, counts, x1, y, f_pot, g_first, slots, row_devices)
    stack, (f_pot, first_own) = exchange(part, (2.0 * f_pot, first_own))
    send, g_own = combine(first_own, stack, log_b, g_first, None)
    g_pot, (f_pot, first_own) = exchange(send, (f_pot, first_own))
    g_pot = g_pot.reshape(target_blocks, TILE)

    first, second = first_epsilon, 0.5 * first_epsilon
    part = row_pass(cols, counts, x2, y, f_pot, g_pot, g_first, log_b, mass, slots)
    both = over_cols(part, col_devices)
    part, totals = both[:row_blocks], both[row_blocks:]
    f_pot = f_pot + (log_a - part)
    total_b, total_a = totals[:1], totals[8:9]
    source = half_x + LN2 * (
        second * f_pot - (second + first) * total_a + first * total_b
    )
    part = col_pass(cols, counts, x2, y, f_pot, g_pot, slots, row_devices)
    stack, (source, totals, first_own) = exchange(part, (source, totals, first_own))
    send = combine(first_own, stack, log_b, g_own, (g_first, totals, second, first + second))
    target, source = exchange(send, source)
    return (source.reshape(rows), target.reshape(target_cells))


def solution(mesh):
    return jax.shard_map(
        body,
        mesh=mesh,
        in_specs=(
            P(None, "row"),
            P(None, "col"),
            P("row"),
            P("col"),
            P("row", "col", None),
            P("row", "col"),
        ),
        out_specs=(P("row"), P("col")),
        check_vma=False,
    )
```

```python
import functools

import jax
import jax.numpy as jnp
from jax import lax
from jax.experimental import pallas as pl
from jax.experimental.pallas import tpu as pltpu
from jax.sharding import PartitionSpec as P

TILE = 128
very_negative = -1e30
first_epsilon = 0.5
LOG2E = 1.4426950408889634
LN2 = 0.6931471805599453
SMALLEST = 2.0**-100
LARGEST = 2.0**120
VMEM_LIMIT = 16 * 1024 * 1024
UNROLL = 32
CHUNK = 64
ROW_OFFSET = 64.0
COL_OFFSET = 80.0


def split3(row):
    hi = row.astype(jnp.bfloat16).astype(jnp.float32)
    rest = row - hi
    mid = rest.astype(jnp.bfloat16).astype(jnp.float32)
    lo = (rest - mid).astype(jnp.bfloat16).astype(jnp.float32)
    return hi, mid, lo


def products(x_ref, y_ref, f_ref, cols, slots, r, offset):
    lhs = x_ref[r]
    picked = [
        y_ref[:, pl.ds(pl.multiple_of(cols[k, r] * TILE, TILE), TILE)]
        for k in range(slots)
    ]
    yb = jnp.concatenate(picked, axis=1)
    rhs = [yb, yb]
    if f_ref is not None:
        hi, mid, lo = split3(f_ref[pl.ds(r, 1), :] + offset)
        place = lax.broadcasted_iota(jnp.int32, (16, TILE), 0)
        extra = jnp.where(
            place == 0, hi, jnp.where(place == 1, mid, jnp.where(place == 2, lo, 0.0))
        )
        lhs = jnp.concatenate([lhs, extra.astype(jnp.bfloat16).T], axis=1)
        rhs.append(jnp.ones((16, yb.shape[1]), jnp.bfloat16))
    return jnp.dot(lhs, jnp.concatenate(rhs, axis=0), preferred_element_type=jnp.float32)


def shifts(cols, counts, g_ref, slots, r):
    live = counts[r]
    return [
        jnp.where(k < live, g_ref[pl.ds(cols[k, r], 1), :], very_negative)
        for k in range(slots)
    ]


def log2_sum(values):
    summed = jnp.sum(jnp.sum(values, axis=0, keepdims=True), axis=1, keepdims=True)
    return jnp.broadcast_to(jnp.log2(summed), (8, TILE))


def prepare(kappa, x_hbm, y_hbm, x_ref, x2_ref, y_ref, g_ref, hx_ref, x_in, x_sem, y_sem, others):
    width = y_ref.shape[0]
    blocks = hx_ref.shape[0]
    target_blocks = g_ref.shape[0]
    chunks = target_blocks // CHUNK
    x_copy = pltpu.make_async_copy(x_hbm, x_in, x_sem)
    x_copy.start()

    def y_copy(c):
        at = pl.ds(pl.multiple_of(c * (CHUNK * TILE), CHUNK * TILE), CHUNK * TILE)
        return pltpu.make_async_copy(y_hbm.at[:, at], y_ref.at[:, at], y_sem.at[c])

    for other in others:
        other.start()

    @pl.loop(0, chunks)
    def _(c):
        y_copy(c).start()

    x_copy.wait()

    @pl.loop(0, blocks, unroll=4)
    def _(r):
        xf = x_in[:, pl.ds(pl.multiple_of(r * TILE, TILE), TILE)].astype(jnp.float32)
        hx_ref[pl.ds(r, 1), :] = 0.5 * jnp.sum(xf * xf, axis=0, keepdims=True)
        scaled = xf * kappa
        hi = scaled.astype(jnp.bfloat16)
        lo = (scaled - hi.astype(jnp.float32)).astype(jnp.bfloat16)
        turned = jnp.concatenate([hi, lo], axis=0).T
        x_ref[r] = turned
        x2_ref[r] = turned + turned

    @pl.loop(0, chunks)
    def _(c):
        y_copy(c).wait()

        @pl.loop(0, CHUNK // 8, unroll=2)
        def _(q):
            first = c * CHUNK + q * 8
            at = pl.ds(pl.multiple_of(first * TILE, 8 * TILE), 8 * TILE)
            yf = y_ref[:, at].astype(jnp.float32)
            half = (-0.5 * kappa) * jnp.sum(yf * yf, axis=0, keepdims=True)
            for k in range(8):
                g_ref[pl.ds(first + k, 1), :] = half[:, k * TILE : (k + 1) * TILE]

    for other in others:
        other.wait()


def row_pass_kernel(kappa, slots, *refs):
    if kappa is not None:
        (cols_hbm, counts_hbm, a_hbm, b_hbm, x_hbm, y_hbm, out_ref, x_ref, x2_ref,
         y_ref, g_ref, hx_ref, a_ref, b_ref, mass_ref, total, x_in, cols, counts, sems, y_sem) = refs
        f_ref = None
        small = ((a_hbm, a_ref), (b_hbm, b_ref), (cols_hbm, cols), (counts_hbm, counts))
        others = [
            pltpu.make_async_copy(source, target, sems.at[1 + i])
            for i, (source, target) in enumerate(small)
        ]
        prepare(kappa, x_hbm, y_hbm, x_ref, x2_ref, y_ref, g_ref, hx_ref, x_in, sems.at[0],
                y_sem, others)
        offset = 0.0
    else:
        (cols, counts, x_ref, y_ref, f_ref, g_ref, g_first_ref, b_ref, mass_ref, out_ref,
         total) = refs
        offset = ROW_OFFSET
    blocks = total.shape[1]
    lane = lax.broadcasted_iota(jnp.int32, (TILE, TILE), 1)

    @pl.loop(0, blocks, unroll=UNROLL)
    def _(r):
        scores = products(x_ref, y_ref, f_ref, cols, slots, r, offset)
        terms = None
        for k, row in enumerate(shifts(cols, counts, g_ref, slots, r)):
            term = jnp.exp2(scores[:, k * TILE : (k + 1) * TILE] + row)
            terms = term if terms is None else terms + term
        summed = jnp.sum(terms, axis=1, keepdims=True)
        total[...] = jnp.where(lane == r, summed, total[...])

    sums = total[...]
    out_ref[:blocks, :] = (jnp.log2(sums) - offset).T
    if kappa is not None:
        mass_ref[...] = log2_sum(b_ref[...])
        a_ref[...] = jnp.log2(a_ref[...])
        b_ref[...] = jnp.log2(b_ref[...])
    else:
        out_ref[blocks : blocks + 8, :] = mass_ref[...]
        last = g_first_ref[...] + b_ref[...] - 0.5 * g_ref[...]
        out_ref[blocks + 8 :, :] = log2_sum(jnp.exp2(last))
    fine = jnp.logical_and(jnp.min(sums) >= SMALLEST, jnp.max(sums) <= LARGEST)

    @pl.when(jnp.logical_not(fine))
    def _():
        @pl.loop(0, blocks)
        def _(r):
            scores = products(x_ref, y_ref, f_ref, cols, slots, r, offset)
            rows = shifts(cols, counts, g_ref, slots, r)
            parts = [scores[:, k * TILE : (k + 1) * TILE] + row for k, row in enumerate(rows)]
            top = functools.reduce(jnp.maximum, parts)
            top = jnp.max(top, axis=1, keepdims=True)
            terms = sum(jnp.exp2(part - top) for part in parts)
            summed = jnp.sum(terms, axis=1, keepdims=True)
            total[...] = jnp.where(lane == r, top + jnp.log2(summed), total[...])

        out_ref[:blocks, :] = (total[...] - offset).T


def col_pass_kernel(slots, *refs):
    cols, counts, x_ref, y_ref, f_ref, g_ref, out_ref, total = refs
    blocks = f_ref.shape[0]
    total[...] = jnp.zeros_like(total)

    def visit(r, carry):
        least, most = carry
        scores = products(x_ref, y_ref, f_ref, cols, slots, r, COL_OFFSET)
        live = counts[r]
        for k, row in enumerate(shifts(cols, counts, g_ref, slots, r)):
            terms = jnp.exp2(scores[:, k * TILE : (k + 1) * TILE] + row)
            summed = jnp.sum(terms, axis=0, keepdims=True)
            total[pl.ds(cols[k, r], 1), :] += summed
            least = jnp.minimum(least, jnp.where(k < live, summed, 1.0))
            most = jnp.maximum(most, summed)
        return least, most

    ones = jnp.ones((1, TILE), jnp.float32)
    least, most = lax.fori_loop(0, blocks, visit, (ones, ones), unroll=UNROLL)
    fine = jnp.logical_and(jnp.min(least) >= SMALLEST, jnp.max(most) <= LARGEST / blocks)

    @pl.when(fine)
    def _():
        sums = total[...]
        total[...] = jnp.where(sums > 0.0, jnp.log2(sums) - COL_OFFSET, very_negative)

    @pl.when(jnp.logical_not(fine))
    def _():
        total[...] = jnp.full_like(total, very_negative)

        @pl.loop(0, blocks)
        def _(r):
            scores = products(x_ref, y_ref, f_ref, cols, slots, r, COL_OFFSET)
            live = counts[r]
            for k, row in enumerate(shifts(cols, counts, g_ref, slots, r)):

                @pl.when(k < live)
                def _():
                    part = scores[:, k * TILE : (k + 1) * TILE] + row
                    top = jnp.max(part, axis=0, keepdims=True)
                    summed = jnp.sum(jnp.exp2(part - top), axis=0, keepdims=True)
                    mine = top - COL_OFFSET + jnp.log2(summed)
                    at = pl.ds(cols[k, r], 1)
                    old = total[at, :]
                    peak = jnp.maximum(old, mine)
                    total[at, :] = peak + jnp.log2(jnp.exp2(old - peak) + jnp.exp2(mine - peak))

    out_ref[...] = total[...].reshape(out_ref.shape)


SMEM = functools.partial(pl.BlockSpec, memory_space=pltpu.SMEM)
VMEM = functools.partial(pl.BlockSpec, memory_space=pltpu.VMEM)
ANY = functools.partial(pl.BlockSpec, memory_space=pl.ANY)


def first_row_pass(cols, counts, source_mass, target_mass, source_points, target_points, slots):
    width, rows = source_points.shape
    blocks = rows // TILE
    target_blocks = target_points.shape[1] // TILE
    shape = jax.ShapeDtypeStruct
    bf16, f32 = jnp.bfloat16, jnp.float32
    in_hbm = [
        pltpu.with_memory_space_constraint(v, pltpu.HBM)
        for v in (cols, counts, source_mass, target_mass, source_points, target_points)
    ]
    return pl.pallas_call(
        functools.partial(row_pass_kernel, LOG2E / first_epsilon, slots),
        out_shape=(
            shape((blocks, TILE), f32),
            pltpu.VMEM((blocks, TILE, 2 * width), bf16),
            pltpu.VMEM((blocks, TILE, 2 * width), bf16),
            pltpu.VMEM(target_points.shape, bf16),
            shape((target_blocks, TILE), f32),
            shape((blocks, TILE), f32),
            shape((blocks, TILE), f32),
            shape((target_blocks, TILE), f32),
            shape((8, TILE), f32),
        ),
        in_specs=[ANY()] * 6,
        out_specs=(VMEM(),) * 9,
        scratch_shapes=[
            pltpu.VMEM((TILE, blocks), f32),
            pltpu.VMEM(source_points.shape, bf16),
            pltpu.SMEM(cols.shape, jnp.int32),
            pltpu.SMEM(counts.shape, jnp.int32),
            pltpu.SemaphoreType.DMA((5,)),
            pltpu.SemaphoreType.DMA((target_blocks // CHUNK,)),
        ],
        name="row_pass_first",
        compiler_params=pltpu.CompilerParams(vmem_limit_bytes=VMEM_LIMIT),
    )(*in_hbm)


def row_pass(cols, counts, x, y, f_pot, g_pot, g_first, log_b, mass, slots):
    return pl.pallas_call(
        functools.partial(row_pass_kernel, None, slots),
        out_shape=jax.ShapeDtypeStruct((f_pot.shape[0] + 16, TILE), jnp.float32),
        in_specs=[SMEM(), SMEM()] + [VMEM()] * 7,
        out_specs=VMEM(),
        scratch_shapes=[pltpu.VMEM((TILE, f_pot.shape[0]), jnp.float32)],
        name="row_pass",
        compiler_params=pltpu.CompilerParams(vmem_limit_bytes=VMEM_LIMIT),
    )(cols, counts, x, y, f_pot, g_pot, g_first, log_b, mass)


def col_pass(cols, counts, x, y, f_pot, g_pot, slots, devices):
    target_blocks = g_pot.shape[0]
    return pl.pallas_call(
        functools.partial(col_pass_kernel, slots),
        out_shape=jax.ShapeDtypeStruct(
            (devices, target_blocks // devices, TILE), jnp.float32
        ),
        in_specs=[SMEM(), SMEM()] + [VMEM()] * 4,
        out_specs=VMEM(),
        scratch_shapes=[pltpu.VMEM((target_blocks, TILE), jnp.float32)],
        name="col_pass",
        compiler_params=pltpu.CompilerParams(vmem_limit_bytes=VMEM_LIMIT),
    )(cols, counts, x, y, f_pot, g_pot)


def combine_kernel(epsilon, both_eps, *refs):
    if both_eps is None:
        first_own, stack_ref, b_ref, g_ref, send_ref, new_ref = refs
    else:
        first_own, stack_ref, b_ref, g_ref, first_ref, totals_ref, send_ref = refs
    devices, own, _ = stack_ref.shape
    here = pl.ds(pl.multiple_of(first_own[0], own), own)
    top = stack_ref[0]
    for d in range(1, devices):
        top = jnp.maximum(top, stack_ref[d])
    summed = jnp.exp2(stack_ref[0] - top)
    for d in range(1, devices):
        summed += jnp.exp2(stack_ref[d] - top)
    gain = b_ref[here, :] - (top + jnp.log2(summed))
    if both_eps is None:
        new = 2.0 * (g_ref[here, :] + gain)
        new_ref[...] = new
    else:
        difference = totals_ref[8:9, :] - totals_ref[:1, :]
        half = first_ref[here, :] * first_epsilon
        new = LN2 * (epsilon * (g_ref[...] + gain) + both_eps * difference - half)
    for d in range(devices):
        send_ref[d] = new


def combine(first_own, stack, log_b, g_pot, last):
    shape = jax.ShapeDtypeStruct
    send = shape(stack.shape, jnp.float32)
    if last is None:
        more, scales = (), (None, None)
        out = (send, shape(stack.shape[1:], jnp.float32))
    else:
        more, scales = last[:2], last[2:]
        out = send
    return pl.pallas_call(
        functools.partial(combine_kernel, *scales),
        out_shape=out,
        in_specs=[SMEM()] + [VMEM()] * (3 + len(more)),
        out_specs=jax.tree.map(lambda _: VMEM(), out),
        name="combine",
        compiler_params=pltpu.CompilerParams(vmem_limit_bytes=VMEM_LIMIT // 2),
    )(first_own, stack, log_b, g_pot, *more)


def lse_of(parts):
    top = functools.reduce(jnp.maximum, parts)
    return top + jnp.log2(sum(jnp.exp2(part - top) for part in parts))


def over_cols(part, cols):
    def moved(value, pairs):
        return lax.ppermute(value, "col", pairs)

    part = lse_of([part, moved(part, [(i, i ^ 1) for i in range(cols)])])
    away = sorted(range(2, cols, 2), key=lambda by: -min(by, cols - by))
    return lse_of([part] + [moved(part, [(i, (i + by) % cols) for i in range(cols)]) for by in away])


def exchange(blocks, rest):
    blocks, rest = lax.optimization_barrier((blocks, rest))
    return lax.optimization_barrier((lax.all_to_all(blocks, "row", 0, 0), rest))


def body(source_points, target_points, source_mass, target_mass, tile_cols, tile_counts):
    width, rows = source_points.shape
    row_blocks = rows // TILE
    target_cells = target_points.shape[1]
    target_blocks = target_cells // TILE
    slots = tile_cols.shape[2]
    row_devices = lax.axis_size("row")
    col_devices = lax.axis_size("col")
    own_blocks = target_blocks // row_devices

    cols = tile_cols.transpose(1, 2, 0).reshape(slots, row_blocks)
    counts = tile_counts.reshape(row_blocks)
    mass_a = source_mass.reshape(row_blocks, TILE)
    first_own = (lax.axis_index("row") * own_blocks).reshape(1)
    counts, first_own = lax.optimization_barrier((counts, first_own))

    part, x1, x2, y, g_first, half_x, log_a, log_b, mass = first_row_pass(
        cols,
        counts,
        mass_a,
        target_mass.reshape(target_blocks, TILE),
        source_points,
        target_points,
        slots,
    )
    x1, x2, y = (pltpu.with_memory_space_constraint(v, pltpu.VMEM) for v in (x1, x2, y))

    f_pot = log_a - over_cols(part, col_devices)
    part = col_pass(cols, counts, x1, y, f_pot, g_first, slots, row_devices)
    stack, (f_pot, first_own) = exchange(part, (2.0 * f_pot, first_own))
    send, g_own = combine(first_own, stack, log_b, g_first, None)
    g_pot, (f_pot, first_own) = exchange(send, (f_pot, first_own))
    g_pot = g_pot.reshape(target_blocks, TILE)

    first, second = first_epsilon, 0.5 * first_epsilon
    part = row_pass(cols, counts, x2, y, f_pot, g_pot, g_first, log_b, mass, slots)
    both = over_cols(part, col_devices)
    part, totals = both[:row_blocks], both[row_blocks:]
    f_pot = f_pot + (log_a - part)
    total_b, total_a = totals[:1], totals[8:9]
    source = half_x + LN2 * (
        second * f_pot - (second + first) * total_a + first * total_b
    )
    part = col_pass(cols, counts, x2, y, f_pot, g_pot, slots, row_devices)
    stack, (source, totals, first_own) = exchange(part, (source, totals, first_own))
    send = combine(first_own, stack, log_b, g_own, (g_first, totals, second, first + second))
    target, source = exchange(send, source)
    return (source.reshape(rows), target.reshape(target_cells))


def solution(mesh):
    return jax.shard_map(
        body,
        mesh=mesh,
        in_specs=(
            P(None, "row"),
            P(None, "col"),
            P("row"),
            P("col"),
            P("row", "col", None),
            P("row", "col"),
        ),
        out_specs=(P("row"), P("col")),
        check_vma=False,
    )
```

```python
import functools

import jax
import jax.numpy as jnp
from jax import lax
from jax.experimental import pallas as pl
from jax.experimental.pallas import tpu as pltpu
from jax.sharding import PartitionSpec as P

TILE = 128
very_negative = -1e30
first_epsilon = 0.5
LOG2E = 1.4426950408889634
LN2 = 0.6931471805599453
SMALLEST = 2.0**-100
LARGEST = 2.0**120
VMEM_LIMIT = 16 * 1024 * 1024
ROW_UNROLL = 128
COL_UNROLL = 64
CHUNK = 64
ROW_OFFSET = 64.0
COL_OFFSET = 80.0


def split3(row):
    hi = row.astype(jnp.bfloat16).astype(jnp.float32)
    rest = row - hi
    mid = rest.astype(jnp.bfloat16).astype(jnp.float32)
    lo = (rest - mid).astype(jnp.bfloat16).astype(jnp.float32)
    return hi, mid, lo


def products(x_ref, y_ref, f_ref, cols, slots, r, offset):
    lhs = x_ref[r]
    picked = [
        y_ref[:, pl.ds(pl.multiple_of(cols[k, r] * TILE, TILE), TILE)]
        for k in range(slots)
    ]
    yb = jnp.concatenate(picked, axis=1)
    rhs = [yb, yb]
    if f_ref is not None:
        hi, mid, lo = split3(f_ref[pl.ds(r, 1), :] + offset)
        place = lax.broadcasted_iota(jnp.int32, (16, TILE), 0)
        extra = jnp.where(
            place == 0, hi, jnp.where(place == 1, mid, jnp.where(place == 2, lo, 0.0))
        )
        lhs = jnp.concatenate([lhs, extra.astype(jnp.bfloat16).T], axis=1)
        rhs.append(jnp.ones((16, yb.shape[1]), jnp.bfloat16))
    return jnp.dot(lhs, jnp.concatenate(rhs, axis=0), preferred_element_type=jnp.float32)


def shifts(cols, counts, g_ref, slots, r):
    live = counts[r]
    return [
        jnp.where(k < live, g_ref[pl.ds(cols[k, r], 1), :], very_negative)
        for k in range(slots)
    ]


def log2_sum(values):
    summed = jnp.sum(jnp.sum(values, axis=0, keepdims=True), axis=1, keepdims=True)
    return jnp.broadcast_to(jnp.log2(summed), (8, TILE))


def prepare(kappa, x_hbm, y_hbm, x_ref, x2_ref, y_ref, g_ref, hx_ref, x_in, x_sem, y_sem, others):
    width = y_ref.shape[0]
    blocks = hx_ref.shape[0]
    target_blocks = g_ref.shape[0]
    chunks = target_blocks // CHUNK
    x_copy = pltpu.make_async_copy(x_hbm, x_in, x_sem)
    x_copy.start()

    def y_copy(c):
        at = pl.ds(pl.multiple_of(c * (CHUNK * TILE), CHUNK * TILE), CHUNK * TILE)
        return pltpu.make_async_copy(y_hbm.at[:, at], y_ref.at[:, at], y_sem.at[c])

    for other in others:
        other.start()

    @pl.loop(0, chunks)
    def _(c):
        y_copy(c).start()

    x_copy.wait()

    @pl.loop(0, blocks, unroll=4)
    def _(r):
        xf = x_in[:, pl.ds(pl.multiple_of(r * TILE, TILE), TILE)].astype(jnp.float32)
        hx_ref[pl.ds(r, 1), :] = 0.5 * jnp.sum(xf * xf, axis=0, keepdims=True)
        scaled = xf * kappa
        hi = scaled.astype(jnp.bfloat16)
        lo = (scaled - hi.astype(jnp.float32)).astype(jnp.bfloat16)
        turned = jnp.concatenate([hi, lo], axis=0).T
        x_ref[r] = turned
        x2_ref[r] = turned + turned

    @pl.loop(0, chunks)
    def _(c):
        y_copy(c).wait()

        @pl.loop(0, CHUNK // 8, unroll=2)
        def _(q):
            first = c * CHUNK + q * 8
            at = pl.ds(pl.multiple_of(first * TILE, 8 * TILE), 8 * TILE)
            yf = y_ref[:, at].astype(jnp.float32)
            half = (-0.5 * kappa) * jnp.sum(yf * yf, axis=0, keepdims=True)
            for k in range(8):
                g_ref[pl.ds(first + k, 1), :] = half[:, k * TILE : (k + 1) * TILE]

    for other in others:
        other.wait()


def row_pass_kernel(kappa, slots, *refs):
    if kappa is not None:
        (cols_hbm, counts_hbm, a_hbm, b_hbm, x_hbm, y_hbm, out_ref, x_ref, x2_ref,
         y_ref, g_ref, hx_ref, a_ref, b_ref, mass_ref, total, x_in, cols, counts, sems, y_sem) = refs
        f_ref = None
        small = ((a_hbm, a_ref), (b_hbm, b_ref), (cols_hbm, cols), (counts_hbm, counts))
        others = [
            pltpu.make_async_copy(source, target, sems.at[1 + i])
            for i, (source, target) in enumerate(small)
        ]
        prepare(kappa, x_hbm, y_hbm, x_ref, x2_ref, y_ref, g_ref, hx_ref, x_in, sems.at[0],
                y_sem, others)
        offset = 0.0
    else:
        (cols, counts, x_ref, y_ref, f_ref, g_ref, g_first_ref, b_ref, mass_ref, out_ref,
         total) = refs
        offset = ROW_OFFSET
    blocks = total.shape[1]
    lane = lax.broadcasted_iota(jnp.int32, (TILE, TILE), 1)

    @pl.loop(0, blocks, unroll=ROW_UNROLL)
    def _(r):
        scores = products(x_ref, y_ref, f_ref, cols, slots, r, offset)
        terms = None
        for k, row in enumerate(shifts(cols, counts, g_ref, slots, r)):
            term = jnp.exp2(scores[:, k * TILE : (k + 1) * TILE] + row)
            terms = term if terms is None else terms + term
        summed = jnp.sum(terms, axis=1, keepdims=True)
        total[...] = jnp.where(lane == r, summed, total[...])

    sums = total[...]
    out_ref[:blocks, :] = (jnp.log2(sums) - offset).T
    if kappa is not None:
        mass_ref[...] = log2_sum(b_ref[...])
        a_ref[...] = jnp.log2(a_ref[...])
        b_ref[...] = jnp.log2(b_ref[...])
    else:
        out_ref[blocks : blocks + 8, :] = mass_ref[...]
        last = g_first_ref[...] + b_ref[...] - 0.5 * g_ref[...]
        out_ref[blocks + 8 :, :] = log2_sum(jnp.exp2(last))
    fine = jnp.logical_and(jnp.min(sums) >= SMALLEST, jnp.max(sums) <= LARGEST)

    @pl.when(jnp.logical_not(fine))
    def _():
        @pl.loop(0, blocks)
        def _(r):
            scores = products(x_ref, y_ref, f_ref, cols, slots, r, offset)
            rows = shifts(cols, counts, g_ref, slots, r)
            parts = [scores[:, k * TILE : (k + 1) * TILE] + row for k, row in enumerate(rows)]
            top = functools.reduce(jnp.maximum, parts)
            top = jnp.max(top, axis=1, keepdims=True)
            terms = sum(jnp.exp2(part - top) for part in parts)
            summed = jnp.sum(terms, axis=1, keepdims=True)
            total[...] = jnp.where(lane == r, top + jnp.log2(summed), total[...])

        out_ref[:blocks, :] = (total[...] - offset).T


def col_pass_kernel(slots, *refs):
    cols, counts, x_ref, y_ref, f_ref, g_ref, out_ref, total = refs
    blocks = f_ref.shape[0]
    total[...] = jnp.zeros_like(total)

    def visit(r, carry):
        least, most = carry
        scores = products(x_ref, y_ref, f_ref, cols, slots, r, COL_OFFSET)
        live = counts[r]
        for k, row in enumerate(shifts(cols, counts, g_ref, slots, r)):
            terms = jnp.exp2(scores[:, k * TILE : (k + 1) * TILE] + row)
            summed = jnp.sum(terms, axis=0, keepdims=True)
            total[pl.ds(cols[k, r], 1), :] += summed
            least = jnp.minimum(least, jnp.where(k < live, summed, 1.0))
            most = jnp.maximum(most, summed)
        return least, most

    ones = jnp.ones((1, TILE), jnp.float32)
    least, most = lax.fori_loop(0, blocks, visit, (ones, ones), unroll=COL_UNROLL)
    fine = jnp.logical_and(jnp.min(least) >= SMALLEST, jnp.max(most) <= LARGEST / blocks)

    @pl.when(fine)
    def _():
        sums = total[...]
        total[...] = jnp.where(sums > 0.0, jnp.log2(sums) - COL_OFFSET, very_negative)

    @pl.when(jnp.logical_not(fine))
    def _():
        total[...] = jnp.full_like(total, very_negative)

        @pl.loop(0, blocks)
        def _(r):
            scores = products(x_ref, y_ref, f_ref, cols, slots, r, COL_OFFSET)
            live = counts[r]
            for k, row in enumerate(shifts(cols, counts, g_ref, slots, r)):

                @pl.when(k < live)
                def _():
                    part = scores[:, k * TILE : (k + 1) * TILE] + row
                    top = jnp.max(part, axis=0, keepdims=True)
                    summed = jnp.sum(jnp.exp2(part - top), axis=0, keepdims=True)
                    mine = top - COL_OFFSET + jnp.log2(summed)
                    at = pl.ds(cols[k, r], 1)
                    old = total[at, :]
                    peak = jnp.maximum(old, mine)
                    total[at, :] = peak + jnp.log2(jnp.exp2(old - peak) + jnp.exp2(mine - peak))

    out_ref[...] = total[...].reshape(out_ref.shape)


SMEM = functools.partial(pl.BlockSpec, memory_space=pltpu.SMEM)
VMEM = functools.partial(pl.BlockSpec, memory_space=pltpu.VMEM)
ANY = functools.partial(pl.BlockSpec, memory_space=pl.ANY)


def first_row_pass(cols, counts, source_mass, target_mass, source_points, target_points, slots):
    width, rows = source_points.shape
    blocks = rows // TILE
    target_blocks = target_points.shape[1] // TILE
    shape = jax.ShapeDtypeStruct
    bf16, f32 = jnp.bfloat16, jnp.float32
    in_hbm = [
        pltpu.with_memory_space_constraint(v, pltpu.HBM)
        for v in (cols, counts, source_mass, target_mass, source_points, target_points)
    ]
    return pl.pallas_call(
        functools.partial(row_pass_kernel, LOG2E / first_epsilon, slots),
        out_shape=(
            shape((blocks, TILE), f32),
            pltpu.VMEM((blocks, TILE, 2 * width), bf16),
            pltpu.VMEM((blocks, TILE, 2 * width), bf16),
            pltpu.VMEM(target_points.shape, bf16),
            shape((target_blocks, TILE), f32),
            shape((blocks, TILE), f32),
            shape((blocks, TILE), f32),
            shape((target_blocks, TILE), f32),
            shape((8, TILE), f32),
        ),
        in_specs=[ANY()] * 6,
        out_specs=(VMEM(),) * 9,
        scratch_shapes=[
            pltpu.VMEM((TILE, blocks), f32),
            pltpu.VMEM(source_points.shape, bf16),
            pltpu.SMEM(cols.shape, jnp.int32),
            pltpu.SMEM(counts.shape, jnp.int32),
            pltpu.SemaphoreType.DMA((5,)),
            pltpu.SemaphoreType.DMA((target_blocks // CHUNK,)),
        ],
        name="row_pass_first",
        compiler_params=pltpu.CompilerParams(vmem_limit_bytes=VMEM_LIMIT),
    )(*in_hbm)


def row_pass(cols, counts, x, y, f_pot, g_pot, g_first, log_b, mass, slots):
    return pl.pallas_call(
        functools.partial(row_pass_kernel, None, slots),
        out_shape=jax.ShapeDtypeStruct((f_pot.shape[0] + 16, TILE), jnp.float32),
        in_specs=[SMEM(), SMEM()] + [VMEM()] * 7,
        out_specs=VMEM(),
        scratch_shapes=[pltpu.VMEM((TILE, f_pot.shape[0]), jnp.float32)],
        name="row_pass",
        compiler_params=pltpu.CompilerParams(vmem_limit_bytes=VMEM_LIMIT),
    )(cols, counts, x, y, f_pot, g_pot, g_first, log_b, mass)


def col_pass(cols, counts, x, y, f_pot, g_pot, slots, devices):
    target_blocks = g_pot.shape[0]
    return pl.pallas_call(
        functools.partial(col_pass_kernel, slots),
        out_shape=jax.ShapeDtypeStruct(
            (devices, target_blocks // devices, TILE), jnp.float32
        ),
        in_specs=[SMEM(), SMEM()] + [VMEM()] * 4,
        out_specs=VMEM(),
        scratch_shapes=[pltpu.VMEM((target_blocks, TILE), jnp.float32)],
        name="col_pass",
        compiler_params=pltpu.CompilerParams(vmem_limit_bytes=VMEM_LIMIT),
    )(cols, counts, x, y, f_pot, g_pot)


def combine_kernel(epsilon, both_eps, *refs):
    if both_eps is None:
        first_own, stack_ref, b_ref, g_ref, send_ref, new_ref = refs
    else:
        first_own, stack_ref, b_ref, g_ref, first_ref, totals_ref, send_ref = refs
    devices, own, _ = stack_ref.shape
    here = pl.ds(pl.multiple_of(first_own[0], own), own)
    top = stack_ref[0]
    for d in range(1, devices):
        top = jnp.maximum(top, stack_ref[d])
    summed = jnp.exp2(stack_ref[0] - top)
    for d in range(1, devices):
        summed += jnp.exp2(stack_ref[d] - top)
    gain = b_ref[here, :] - (top + jnp.log2(summed))
    if both_eps is None:
        new = 2.0 * (g_ref[here, :] + gain)
        new_ref[...] = new
    else:
        difference = totals_ref[8:9, :] - totals_ref[:1, :]
        half = first_ref[here, :] * first_epsilon
        new = LN2 * (epsilon * (g_ref[...] + gain) + both_eps * difference - half)
    for d in range(devices):
        send_ref[d] = new


def combine(first_own, stack, log_b, g_pot, last):
    shape = jax.ShapeDtypeStruct
    send = shape(stack.shape, jnp.float32)
    if last is None:
        more, scales = (), (None, None)
        out = (send, shape(stack.shape[1:], jnp.float32))
    else:
        more, scales = last[:2], last[2:]
        out = send
    return pl.pallas_call(
        functools.partial(combine_kernel, *scales),
        out_shape=out,
        in_specs=[SMEM()] + [VMEM()] * (3 + len(more)),
        out_specs=jax.tree.map(lambda _: VMEM(), out),
        name="combine",
        compiler_params=pltpu.CompilerParams(vmem_limit_bytes=VMEM_LIMIT // 2),
    )(first_own, stack, log_b, g_pot, *more)


def lse_of(parts):
    top = functools.reduce(jnp.maximum, parts)
    return top + jnp.log2(sum(jnp.exp2(part - top) for part in parts))


def over_cols(part, cols):
    def moved(value, pairs):
        return lax.ppermute(value, "col", pairs)

    part = lse_of([part, moved(part, [(i, i ^ 1) for i in range(cols)])])
    away = sorted(range(2, cols, 2), key=lambda by: -min(by, cols - by))
    return lse_of([part] + [moved(part, [(i, (i + by) % cols) for i in range(cols)]) for by in away])


def exchange(blocks, rest):
    blocks, rest = lax.optimization_barrier((blocks, rest))
    return lax.optimization_barrier((lax.all_to_all(blocks, "row", 0, 0), rest))


def body(source_points, target_points, source_mass, target_mass, tile_cols, tile_counts):
    width, rows = source_points.shape
    row_blocks = rows // TILE
    target_cells = target_points.shape[1]
    target_blocks = target_cells // TILE
    slots = tile_cols.shape[2]
    row_devices = lax.axis_size("row")
    col_devices = lax.axis_size("col")
    own_blocks = target_blocks // row_devices

    cols = tile_cols.transpose(1, 2, 0).reshape(slots, row_blocks)
    counts = tile_counts.reshape(row_blocks)
    mass_a = source_mass.reshape(row_blocks, TILE)
    first_own = (lax.axis_index("row") * own_blocks).reshape(1)
    counts, first_own = lax.optimization_barrier((counts, first_own))

    part, x1, x2, y, g_first, half_x, log_a, log_b, mass = first_row_pass(
        cols,
        counts,
        mass_a,
        target_mass.reshape(target_blocks, TILE),
        source_points,
        target_points,
        slots,
    )
    x1, x2, y = (pltpu.with_memory_space_constraint(v, pltpu.VMEM) for v in (x1, x2, y))

    f_pot = log_a - over_cols(part, col_devices)
    part = col_pass(cols, counts, x1, y, f_pot, g_first, slots, row_devices)
    stack, (f_pot, first_own) = exchange(part, (2.0 * f_pot, first_own))
    send, g_own = combine(first_own, stack, log_b, g_first, None)
    g_pot, (f_pot, first_own) = exchange(send, (f_pot, first_own))
    g_pot = g_pot.reshape(target_blocks, TILE)

    first, second = first_epsilon, 0.5 * first_epsilon
    part = row_pass(cols, counts, x2, y, f_pot, g_pot, g_first, log_b, mass, slots)
    both = over_cols(part, col_devices)
    part, totals = both[:row_blocks], both[row_blocks:]
    f_pot = f_pot + (log_a - part)
    total_b, total_a = totals[:1], totals[8:9]
    source = half_x + LN2 * (
        second * f_pot - (second + first) * total_a + first * total_b
    )
    part = col_pass(cols, counts, x2, y, f_pot, g_pot, slots, row_devices)
    stack, (source, totals, first_own) = exchange(part, (source, totals, first_own))
    send = combine(first_own, stack, log_b, g_own, (g_first, totals, second, first + second))
    send, source = lax.optimization_barrier((send, source))
    target = lax.all_to_all(send, "row", 0, 0)
    return (source.reshape(rows), target.reshape(target_cells))


def solution(mesh):
    return jax.shard_map(
        body,
        mesh=mesh,
        in_specs=(
            P(None, "row"),
            P(None, "col"),
            P("row"),
            P("col"),
            P("row", "col", None),
            P("row", "col"),
        ),
        out_specs=(P("row"), P("col")),
        check_vma=False,
    )
```

```python
import functools

import jax
import jax.numpy as jnp
from jax import lax
from jax.experimental import pallas as pl
from jax.experimental.pallas import tpu as pltpu
from jax.sharding import PartitionSpec as P

TILE = 128
very_negative = -1e30
first_epsilon = 0.5
LOG2E = 1.4426950408889634
LN2 = 0.6931471805599453
SMALLEST = 2.0**-100
LARGEST = 2.0**120
VMEM_LIMIT = 16 * 1024 * 1024
ROW_UNROLL = 128
COL_UNROLL = 64
CHUNK = 64
ROW_OFFSET = 64.0
COL_OFFSET = 80.0


def split3(row):
    hi = row.astype(jnp.bfloat16).astype(jnp.float32)
    rest = row - hi
    mid = rest.astype(jnp.bfloat16).astype(jnp.float32)
    lo = (rest - mid).astype(jnp.bfloat16).astype(jnp.float32)
    return hi, mid, lo


def products(x_ref, y_ref, f_ref, cols, slots, r, offset):
    lhs = x_ref[r]
    picked = [
        y_ref[:, pl.ds(pl.multiple_of(cols[k, r] * TILE, TILE), TILE)]
        for k in range(slots)
    ]
    yb = jnp.concatenate(picked, axis=1)
    rhs = [yb, yb]
    if f_ref is not None:
        hi, mid, lo = split3(f_ref[pl.ds(r, 1), :] + offset)
        place = lax.broadcasted_iota(jnp.int32, (16, TILE), 0)
        extra = jnp.where(
            place == 0, hi, jnp.where(place == 1, mid, jnp.where(place == 2, lo, 0.0))
        )
        lhs = jnp.concatenate([lhs, extra.astype(jnp.bfloat16).T], axis=1)
        rhs.append(jnp.ones((16, yb.shape[1]), jnp.bfloat16))
    return jnp.dot(lhs, jnp.concatenate(rhs, axis=0), preferred_element_type=jnp.float32)


def shifts(cols, counts, g_ref, slots, r):
    live = counts[r]
    return [
        jnp.where(k < live, g_ref[pl.ds(cols[k, r], 1), :], very_negative)
        for k in range(slots)
    ]


def log2_sum(values):
    summed = jnp.sum(jnp.sum(values, axis=0, keepdims=True), axis=1, keepdims=True)
    return jnp.broadcast_to(jnp.log2(summed), (8, TILE))


def prepare(kappa, x_hbm, y_hbm, x_ref, x2_ref, y_ref, g_ref, hx_ref, x_in, x_sem, y_sem, others):
    width = y_ref.shape[0]
    blocks = hx_ref.shape[0]
    target_blocks = g_ref.shape[0]
    chunks = target_blocks // CHUNK
    x_copy = pltpu.make_async_copy(x_hbm, x_in, x_sem)
    x_copy.start()

    def y_copy(c):
        at = pl.ds(pl.multiple_of(c * (CHUNK * TILE), CHUNK * TILE), CHUNK * TILE)
        return pltpu.make_async_copy(y_hbm.at[:, at], y_ref.at[:, at], y_sem.at[c])

    for other in others:
        other.start()

    @pl.loop(0, chunks)
    def _(c):
        y_copy(c).start()

    x_copy.wait()

    @pl.loop(0, blocks, unroll=4)
    def _(r):
        xf = x_in[:, pl.ds(pl.multiple_of(r * TILE, TILE), TILE)].astype(jnp.float32)
        hx_ref[pl.ds(r, 1), :] = 0.5 * jnp.sum(xf * xf, axis=0, keepdims=True)
        scaled = xf * kappa
        hi = scaled.astype(jnp.bfloat16)
        lo = (scaled - hi.astype(jnp.float32)).astype(jnp.bfloat16)
        turned = jnp.concatenate([hi, lo], axis=0).T
        x_ref[r] = turned
        x2_ref[r] = turned + turned

    @pl.loop(0, chunks)
    def _(c):
        y_copy(c).wait()

        @pl.loop(0, CHUNK // 8, unroll=2)
        def _(q):
            first = c * CHUNK + q * 8
            at = pl.ds(pl.multiple_of(first * TILE, 8 * TILE), 8 * TILE)
            yf = y_ref[:, at].astype(jnp.float32)
            half = (-0.5 * kappa) * jnp.sum(yf * yf, axis=0, keepdims=True)
            for k in range(8):
                g_ref[pl.ds(first + k, 1), :] = half[:, k * TILE : (k + 1) * TILE]

    for other in others:
        other.wait()


def row_pass_kernel(kappa, slots, *refs):
    if kappa is not None:
        (cols_hbm, counts_hbm, a_hbm, b_hbm, x_hbm, y_hbm, out_ref, x_ref, x2_ref,
         y_ref, g_ref, hx_ref, a_ref, b_ref, mass_ref, total, x_in, cols, counts, sems, y_sem) = refs
        f_ref = None
        small = ((a_hbm, a_ref), (b_hbm, b_ref), (cols_hbm, cols), (counts_hbm, counts))
        others = [
            pltpu.make_async_copy(source, target, sems.at[1 + i])
            for i, (source, target) in enumerate(small)
        ]
        prepare(kappa, x_hbm, y_hbm, x_ref, x2_ref, y_ref, g_ref, hx_ref, x_in, sems.at[0],
                y_sem, others)
        offset = 0.0
    else:
        (cols, counts, x_ref, y_ref, f_ref, g_ref, g_first_ref, b_ref, mass_ref, out_ref,
         total) = refs
        offset = ROW_OFFSET
    blocks = total.shape[1]
    lane = lax.broadcasted_iota(jnp.int32, (TILE, TILE), 1)

    @pl.loop(0, blocks, unroll=ROW_UNROLL)
    def _(r):
        scores = products(x_ref, y_ref, f_ref, cols, slots, r, offset)
        terms = None
        for k, row in enumerate(shifts(cols, counts, g_ref, slots, r)):
            term = jnp.exp2(scores[:, k * TILE : (k + 1) * TILE] + row)
            terms = term if terms is None else terms + term
        summed = jnp.sum(terms, axis=1, keepdims=True)
        total[...] = jnp.where(lane == r, summed, total[...])

    sums = total[...]
    out_ref[:blocks, :] = (jnp.log2(sums) - offset).T
    if kappa is not None:
        mass_ref[...] = log2_sum(b_ref[...])
        a_ref[...] = jnp.log2(a_ref[...])
        b_ref[...] = jnp.log2(b_ref[...])
    else:
        out_ref[blocks : blocks + 8, :] = mass_ref[...]
        last = g_first_ref[...] + b_ref[...] - 0.5 * g_ref[...]
        out_ref[blocks + 8 :, :] = log2_sum(jnp.exp2(last))
    fine = jnp.logical_and(jnp.min(sums) >= SMALLEST, jnp.max(sums) <= LARGEST)

    @pl.when(jnp.logical_not(fine))
    def _():
        @pl.loop(0, blocks)
        def _(r):
            scores = products(x_ref, y_ref, f_ref, cols, slots, r, offset)
            rows = shifts(cols, counts, g_ref, slots, r)
            parts = [scores[:, k * TILE : (k + 1) * TILE] + row for k, row in enumerate(rows)]
            top = functools.reduce(jnp.maximum, parts)
            top = jnp.max(top, axis=1, keepdims=True)
            terms = sum(jnp.exp2(part - top) for part in parts)
            summed = jnp.sum(terms, axis=1, keepdims=True)
            total[...] = jnp.where(lane == r, top + jnp.log2(summed), total[...])

        out_ref[:blocks, :] = (total[...] - offset).T


def col_pass_kernel(slots, last, *refs):
    if last is None:
        cols, counts, x_ref, y_ref, f_ref, g_ref, out_ref, total = refs
    else:
        (cols, counts, x_ref, y_ref, f_ref, g_ref, hx_ref, totals_ref, out_ref, source_hbm, total,
         source, sem) = refs
        second, first = last
        total_b, total_a = totals_ref[:1, :], totals_ref[8:9, :]
        shift = first * total_b - (second + first) * total_a
        source[...] = hx_ref[...] + LN2 * (second * f_ref[...] + shift)
        source_copy = pltpu.make_async_copy(source, source_hbm, sem)
        source_copy.start()
    blocks = f_ref.shape[0]
    total[...] = jnp.zeros_like(total)

    def visit(r, carry):
        least, most = carry
        scores = products(x_ref, y_ref, f_ref, cols, slots, r, COL_OFFSET)
        live = counts[r]
        for k, row in enumerate(shifts(cols, counts, g_ref, slots, r)):
            terms = jnp.exp2(scores[:, k * TILE : (k + 1) * TILE] + row)
            summed = jnp.sum(terms, axis=0, keepdims=True)
            total[pl.ds(cols[k, r], 1), :] += summed
            least = jnp.minimum(least, jnp.where(k < live, summed, 1.0))
            most = jnp.maximum(most, summed)
        return least, most

    ones = jnp.ones((1, TILE), jnp.float32)
    least, most = lax.fori_loop(0, blocks, visit, (ones, ones), unroll=COL_UNROLL)
    sums = total[...]
    result = jnp.where(sums > 0.0, jnp.log2(sums) - COL_OFFSET, very_negative)
    out_ref[...] = result.reshape(out_ref.shape)
    fine = jnp.logical_and(jnp.min(least) >= SMALLEST, jnp.max(most) <= LARGEST / blocks)

    @pl.when(jnp.logical_not(fine))
    def _():
        total[...] = jnp.full_like(total, very_negative)

        @pl.loop(0, blocks)
        def _(r):
            scores = products(x_ref, y_ref, f_ref, cols, slots, r, COL_OFFSET)
            live = counts[r]
            for k, row in enumerate(shifts(cols, counts, g_ref, slots, r)):

                @pl.when(k < live)
                def _():
                    part = scores[:, k * TILE : (k + 1) * TILE] + row
                    top = jnp.max(part, axis=0, keepdims=True)
                    summed = jnp.sum(jnp.exp2(part - top), axis=0, keepdims=True)
                    mine = top - COL_OFFSET + jnp.log2(summed)
                    at = pl.ds(cols[k, r], 1)
                    old = total[at, :]
                    peak = jnp.maximum(old, mine)
                    total[at, :] = peak + jnp.log2(jnp.exp2(old - peak) + jnp.exp2(mine - peak))

        out_ref[...] = total[...].reshape(out_ref.shape)

    if last is not None:
        source_copy.wait()


SMEM = functools.partial(pl.BlockSpec, memory_space=pltpu.SMEM)
VMEM = functools.partial(pl.BlockSpec, memory_space=pltpu.VMEM)
ANY = functools.partial(pl.BlockSpec, memory_space=pl.ANY)


def first_row_pass(cols, counts, source_mass, target_mass, source_points, target_points, slots):
    width, rows = source_points.shape
    blocks = rows // TILE
    target_blocks = target_points.shape[1] // TILE
    shape = jax.ShapeDtypeStruct
    bf16, f32 = jnp.bfloat16, jnp.float32
    in_hbm = [
        pltpu.with_memory_space_constraint(v, pltpu.HBM)
        for v in (cols, counts, source_mass, target_mass, source_points, target_points)
    ]
    return pl.pallas_call(
        functools.partial(row_pass_kernel, LOG2E / first_epsilon, slots),
        out_shape=(
            shape((blocks, TILE), f32),
            pltpu.VMEM((blocks, TILE, 2 * width), bf16),
            pltpu.VMEM((blocks, TILE, 2 * width), bf16),
            pltpu.VMEM(target_points.shape, bf16),
            shape((target_blocks, TILE), f32),
            shape((blocks, TILE), f32),
            shape((blocks, TILE), f32),
            shape((target_blocks, TILE), f32),
            shape((8, TILE), f32),
        ),
        in_specs=[ANY()] * 6,
        out_specs=(VMEM(),) * 9,
        scratch_shapes=[
            pltpu.VMEM((TILE, blocks), f32),
            pltpu.VMEM(source_points.shape, bf16),
            pltpu.SMEM(cols.shape, jnp.int32),
            pltpu.SMEM(counts.shape, jnp.int32),
            pltpu.SemaphoreType.DMA((5,)),
            pltpu.SemaphoreType.DMA((target_blocks // CHUNK,)),
        ],
        name="row_pass_first",
        compiler_params=pltpu.CompilerParams(vmem_limit_bytes=VMEM_LIMIT),
    )(*in_hbm)


def row_pass(cols, counts, x, y, f_pot, g_pot, g_first, log_b, mass, slots):
    return pl.pallas_call(
        functools.partial(row_pass_kernel, None, slots),
        out_shape=jax.ShapeDtypeStruct((f_pot.shape[0] + 16, TILE), jnp.float32),
        in_specs=[SMEM(), SMEM()] + [VMEM()] * 7,
        out_specs=VMEM(),
        scratch_shapes=[pltpu.VMEM((TILE, f_pot.shape[0]), jnp.float32)],
        name="row_pass",
        compiler_params=pltpu.CompilerParams(vmem_limit_bytes=VMEM_LIMIT),
    )(cols, counts, x, y, f_pot, g_pot, g_first, log_b, mass)


def col_pass(cols, counts, x, y, f_pot, g_pot, slots, devices, last=None):
    target_blocks = g_pot.shape[0]
    out = jax.ShapeDtypeStruct((devices, target_blocks // devices, TILE), jnp.float32)
    scratch = [pltpu.VMEM((target_blocks, TILE), jnp.float32)]
    more, scales, out_specs = (), None, VMEM()
    if last is not None:
        more, scales = last[:2], last[2:]
        out, out_specs = (out, pltpu.HBM(f_pot.shape, jnp.float32)), (VMEM(), ANY())
        scratch += [pltpu.VMEM(f_pot.shape, jnp.float32), pltpu.SemaphoreType.DMA]
    return pl.pallas_call(
        functools.partial(col_pass_kernel, slots, scales),
        out_shape=out,
        in_specs=[SMEM(), SMEM()] + [VMEM()] * (4 + len(more)),
        out_specs=out_specs,
        scratch_shapes=scratch,
        name="col_pass",
        compiler_params=pltpu.CompilerParams(vmem_limit_bytes=VMEM_LIMIT),
    )(cols, counts, x, y, f_pot, g_pot, *more)


def combine_kernel(epsilon, both_eps, *refs):
    if both_eps is None:
        first_own, stack_ref, b_ref, g_ref, send_ref, new_ref = refs
    else:
        first_own, stack_ref, b_ref, g_ref, first_ref, totals_ref, send_ref = refs
    devices, own, _ = stack_ref.shape
    here = pl.ds(pl.multiple_of(first_own[0], own), own)
    top = stack_ref[0]
    for d in range(1, devices):
        top = jnp.maximum(top, stack_ref[d])
    summed = jnp.exp2(stack_ref[0] - top)
    for d in range(1, devices):
        summed += jnp.exp2(stack_ref[d] - top)
    gain = b_ref[here, :] - (top + jnp.log2(summed))
    if both_eps is None:
        new = 2.0 * (g_ref[here, :] + gain)
        new_ref[...] = new
    else:
        difference = totals_ref[8:9, :] - totals_ref[:1, :]
        half = first_ref[here, :] * first_epsilon
        new = LN2 * (epsilon * (g_ref[...] + gain) + both_eps * difference - half)
    for d in range(devices):
        send_ref[d] = new


def combine(first_own, stack, log_b, g_pot, last):
    shape = jax.ShapeDtypeStruct
    send = shape(stack.shape, jnp.float32)
    if last is None:
        more, scales = (), (None, None)
        out = (send, shape(stack.shape[1:], jnp.float32))
    else:
        more, scales = last[:2], last[2:]
        out = send
    return pl.pallas_call(
        functools.partial(combine_kernel, *scales),
        out_shape=out,
        in_specs=[SMEM()] + [VMEM()] * (3 + len(more)),
        out_specs=jax.tree.map(lambda _: VMEM(), out),
        name="combine",
        compiler_params=pltpu.CompilerParams(vmem_limit_bytes=VMEM_LIMIT // 2),
    )(first_own, stack, log_b, g_pot, *more)


def lse_of(parts):
    top = functools.reduce(jnp.maximum, parts)
    return top + jnp.log2(sum(jnp.exp2(part - top) for part in parts))


def over_cols(part, cols):
    def moved(value, pairs):
        return lax.ppermute(value, "col", pairs)

    part = lse_of([part, moved(part, [(i, i ^ 1) for i in range(cols)])])
    masks = range(2, cols, 2)
    return lse_of([part] + [moved(part, [(i, i ^ mask) for i in range(cols)]) for mask in masks])


def exchange(blocks, rest):
    blocks, rest = lax.optimization_barrier((blocks, rest))
    return lax.optimization_barrier((lax.all_to_all(blocks, "row", 0, 0), rest))


def body(source_points, target_points, source_mass, target_mass, tile_cols, tile_counts):
    width, rows = source_points.shape
    row_blocks = rows // TILE
    target_cells = target_points.shape[1]
    target_blocks = target_cells // TILE
    slots = tile_cols.shape[2]
    row_devices = lax.axis_size("row")
    col_devices = lax.axis_size("col")
    own_blocks = target_blocks // row_devices

    cols = tile_cols.transpose(1, 2, 0).reshape(slots, row_blocks)
    counts = tile_counts.reshape(row_blocks)
    mass_a = source_mass.reshape(row_blocks, TILE)
    first_own = (lax.axis_index("row") * own_blocks).reshape(1)
    counts, first_own = lax.optimization_barrier((counts, first_own))

    part, x1, x2, y, g_first, half_x, log_a, log_b, mass = first_row_pass(
        cols,
        counts,
        mass_a,
        target_mass.reshape(target_blocks, TILE),
        source_points,
        target_points,
        slots,
    )
    x1, x2, y = (pltpu.with_memory_space_constraint(v, pltpu.VMEM) for v in (x1, x2, y))

    f_pot = log_a - over_cols(part, col_devices)
    part = col_pass(cols, counts, x1, y, f_pot, g_first, slots, row_devices)
    stack, (f_pot, first_own) = exchange(part, (2.0 * f_pot, first_own))
    send, g_own = combine(first_own, stack, log_b, g_first, None)
    g_pot, (f_pot, first_own) = exchange(send, (f_pot, first_own))
    g_pot = g_pot.reshape(target_blocks, TILE)

    first, second = first_epsilon, 0.5 * first_epsilon
    part = row_pass(cols, counts, x2, y, f_pot, g_pot, g_first, log_b, mass, slots)
    both = over_cols(part, col_devices)
    part, totals = both[:row_blocks], both[row_blocks:]
    f_pot = f_pot + (log_a - part)
    part, source = col_pass(
        cols, counts, x2, y, f_pot, g_pot, slots, row_devices, (half_x, totals, second, first)
    )
    stack, (totals, first_own) = exchange(part, (totals, first_own))
    send = combine(first_own, stack, log_b, g_own, (g_first, totals, second, first + second))
    target = lax.all_to_all(send, "row", 0, 0)
    return (source.reshape(rows), target.reshape(target_cells))


def solution(mesh):
    return jax.shard_map(
        body,
        mesh=mesh,
        in_specs=(
            P(None, "row"),
            P(None, "col"),
            P("row"),
            P("col"),
            P("row", "col", None),
            P("row", "col"),
        ),
        out_specs=(P("row"), P("col")),
        check_vma=False,
    )
```

```python
import functools

import jax
import jax.numpy as jnp
from jax import lax
from jax.experimental import pallas as pl
from jax.experimental.pallas import tpu as pltpu
from jax.sharding import PartitionSpec as P

TILE = 128
very_negative = -1e30
first_epsilon = 0.5
LOG2E = 1.4426950408889634
LN2 = 0.6931471805599453
SMALLEST = 2.0**-100
LARGEST = 2.0**120
VMEM_LIMIT = 16 * 1024 * 1024
TAIL = 32
ROW_UNROLL = 96
COL_UNROLL = 48
CHUNK = 64
ROW_OFFSET = 64.0
COL_OFFSET = 80.0


def split3(row):
    hi = row.astype(jnp.bfloat16).astype(jnp.float32)
    rest = row - hi
    mid = rest.astype(jnp.bfloat16).astype(jnp.float32)
    lo = (rest - mid).astype(jnp.bfloat16).astype(jnp.float32)
    return hi, mid, lo


def products(x_ref, y_ref, f_ref, cols, slots, r, offset):
    lhs = x_ref[r]
    picked = [
        y_ref[:, pl.ds(pl.multiple_of(cols[k, r] * TILE, TILE), TILE)]
        for k in range(slots)
    ]
    yb = jnp.concatenate(picked, axis=1)
    rhs = [yb, yb]
    if f_ref is not None:
        hi, mid, lo = split3(f_ref[pl.ds(r, 1), :] + offset)
        place = lax.broadcasted_iota(jnp.int32, (16, TILE), 0)
        extra = jnp.where(
            place == 0, hi, jnp.where(place == 1, mid, jnp.where(place == 2, lo, 0.0))
        )
        lhs = jnp.concatenate([lhs, extra.astype(jnp.bfloat16).T], axis=1)
        rhs.append(jnp.ones((16, yb.shape[1]), jnp.bfloat16))
    return jnp.dot(lhs, jnp.concatenate(rhs, axis=0), preferred_element_type=jnp.float32)


def shifts(cols, counts, g_ref, slots, r):
    live = counts[r]
    return [
        jnp.where(k < live, g_ref[pl.ds(cols[k, r], 1), :], very_negative)
        for k in range(slots)
    ]


def make_order(order, counts, blocks, slots):
    def place(r, found):
        full, half = found
        is_full = counts[r] > slots // 2
        order[jnp.where(is_full, full, blocks - 1 - half)] = r
        return jnp.where(is_full, full + 1, full), jnp.where(is_full, half, half + 1)

    order[blocks] = lax.fori_loop(0, blocks, place, (0, 0), unroll=4)[1]


def over_rows(order, blocks, slots, unroll, visit):
    short = order[blocks] >= TAIL

    def run(first, last, width, unroll):
        visit(first, last, unroll, lambda at: (order[at], width))

    run(0, blocks - TAIL, slots, unroll)

    @pl.when(short)
    def _():
        run(blocks - TAIL, blocks, slots // 2, TAIL)

    @pl.when(jnp.logical_not(short))
    def _():
        run(blocks - TAIL, blocks, slots, 8)


def log2_sum(values):
    summed = jnp.sum(jnp.sum(values, axis=0, keepdims=True), axis=1, keepdims=True)
    return jnp.broadcast_to(jnp.log2(summed), (8, TILE))


def prepare(kappa, x_hbm, y_hbm, x_ref, x2_ref, y_ref, g_ref, hx_ref, x_in, x_sem, y_sem, others, then):
    width = y_ref.shape[0]
    blocks = hx_ref.shape[0]
    target_blocks = g_ref.shape[0]
    chunks = target_blocks // CHUNK
    x_copy = pltpu.make_async_copy(x_hbm, x_in, x_sem)
    beside = blocks * 8 // target_blocks

    def y_copy(c):
        at = pl.ds(pl.multiple_of(c * (CHUNK * TILE), CHUNK * TILE), CHUNK * TILE)
        return pltpu.make_async_copy(y_hbm.at[:, at], y_ref.at[:, at], y_sem.at[c])

    def source_block(r):
        xf = x_in[:, pl.ds(pl.multiple_of(r * TILE, TILE), TILE)].astype(jnp.float32)
        hx_ref[pl.ds(r, 1), :] = 0.5 * jnp.sum(xf * xf, axis=0, keepdims=True)
        scaled = xf * kappa
        hi = scaled.astype(jnp.bfloat16)
        lo = (scaled - hi.astype(jnp.float32)).astype(jnp.bfloat16)
        turned = jnp.concatenate([hi, lo], axis=0).T
        x_ref[r] = turned
        x2_ref[r] = turned + turned

    for other in others:
        other.start()
    x_copy.start()

    @pl.loop(0, chunks)
    def _(c):
        y_copy(c).start()

    for other in others:
        other.wait()
    then()
    x_copy.wait()

    @pl.loop(0, chunks)
    def _(c):
        y_copy(c).wait()

        @pl.loop(0, CHUNK // 8, unroll=4)
        def _(q):
            group = c * (CHUNK // 8) + q
            at = pl.ds(pl.multiple_of(group * (8 * TILE), 8 * TILE), 8 * TILE)
            yf = y_ref[:, at].astype(jnp.float32)
            half = (-0.5 * kappa) * jnp.sum(yf * yf, axis=0, keepdims=True)
            for k in range(8):
                g_ref[pl.ds(group * 8 + k, 1), :] = half[:, k * TILE : (k + 1) * TILE]
            for k in range(beside):
                source_block(group * beside + k)


def row_pass_kernel(kappa, slots, *refs):
    if kappa is not None:
        (cols_hbm, counts_hbm, a_hbm, b_hbm, x_hbm, y_hbm, out_ref, x_ref, x2_ref,
         y_ref, g_ref, hx_ref, a_ref, b_ref, mass_ref, order, total, x_in, cols, counts, sems,
         y_sem) = refs
        f_ref = None
        small = ((a_hbm, a_ref), (b_hbm, b_ref), (cols_hbm, cols), (counts_hbm, counts))
        others = [
            pltpu.make_async_copy(source, target, sems.at[1 + i])
            for i, (source, target) in enumerate(small)
        ]
        prepare(kappa, x_hbm, y_hbm, x_ref, x2_ref, y_ref, g_ref, hx_ref, x_in, sems.at[0],
                y_sem, others, lambda: make_order(order, counts, total.shape[1], slots))
        offset = 0.0
    else:
        (cols, counts, order, x_ref, y_ref, f_ref, g_ref, g_first_ref, b_ref, mass_ref, out_ref,
         total) = refs
        offset = ROW_OFFSET
    blocks = total.shape[1]
    lane = lax.broadcasted_iota(jnp.int32, (TILE, TILE), 1)

    def visit(first, last, unroll, place):
        @pl.loop(first, last, unroll=unroll)
        def _(at):
            r, width = place(at)
            scores = products(x_ref, y_ref, f_ref, cols, width, r, offset)
            terms = None
            for k, row in enumerate(shifts(cols, counts, g_ref, width, r)):
                term = jnp.exp2(scores[:, k * TILE : (k + 1) * TILE] + row)
                terms = term if terms is None else terms + term
            summed = jnp.sum(terms, axis=1, keepdims=True)
            total[...] = jnp.where(lane == r, summed, total[...])

    over_rows(order, blocks, slots, ROW_UNROLL, visit)

    sums = total[...]
    out_ref[:blocks, :] = (jnp.log2(sums) - offset).T
    if kappa is not None:
        mass_ref[...] = log2_sum(b_ref[...])
        a_ref[...] = jnp.log2(a_ref[...])
        b_ref[...] = jnp.log2(b_ref[...])
    else:
        out_ref[blocks : blocks + 8, :] = mass_ref[...]
        last = g_first_ref[...] + b_ref[...] - 0.5 * g_ref[...]
        out_ref[blocks + 8 :, :] = log2_sum(jnp.exp2(last))
    fine = jnp.logical_and(jnp.min(sums) >= SMALLEST, jnp.max(sums) <= LARGEST)

    @pl.when(jnp.logical_not(fine))
    def _():
        @pl.loop(0, blocks)
        def _(r):
            scores = products(x_ref, y_ref, f_ref, cols, slots, r, offset)
            rows = shifts(cols, counts, g_ref, slots, r)
            parts = [scores[:, k * TILE : (k + 1) * TILE] + row for k, row in enumerate(rows)]
            top = functools.reduce(jnp.maximum, parts)
            top = jnp.max(top, axis=1, keepdims=True)
            terms = sum(jnp.exp2(part - top) for part in parts)
            summed = jnp.sum(terms, axis=1, keepdims=True)
            total[...] = jnp.where(lane == r, top + jnp.log2(summed), total[...])

        out_ref[:blocks, :] = (total[...] - offset).T


def col_pass_kernel(slots, last, *refs):
    if last is None:
        cols, counts, order, x_ref, y_ref, f_ref, g_ref, out_ref, total, bounds = refs
    else:
        (cols, counts, order, x_ref, y_ref, f_ref, g_ref, hx_ref, totals_ref, out_ref, source_hbm,
         total, bounds, source, sem) = refs
        second, first = last
        total_b, total_a = totals_ref[:1, :], totals_ref[8:9, :]
        shift = first * total_b - (second + first) * total_a
        source[...] = hx_ref[...] + LN2 * (second * f_ref[...] + shift)
        source_copy = pltpu.make_async_copy(source, source_hbm, sem)
        source_copy.start()
    blocks = f_ref.shape[0]
    total[...] = jnp.zeros_like(total)

    bounds[...] = jnp.ones_like(bounds)

    def visit(first, last, unroll, place):
        def one(at, carry):
            least, most = carry
            r, width = place(at)
            scores = products(x_ref, y_ref, f_ref, cols, width, r, COL_OFFSET)
            live = counts[r]
            for k, row in enumerate(shifts(cols, counts, g_ref, width, r)):
                terms = jnp.exp2(scores[:, k * TILE : (k + 1) * TILE] + row)
                summed = jnp.sum(terms, axis=0, keepdims=True)
                total[pl.ds(cols[k, r], 1), :] += summed
                least = jnp.minimum(least, jnp.where(k < live, summed, 1.0))
                most = jnp.maximum(most, summed)
            return least, most

        carry = (bounds[:1, :], bounds[1:2, :])
        least, most = lax.fori_loop(first, last, one, carry, unroll=unroll)
        bounds[:1, :] = least
        bounds[1:2, :] = most

    over_rows(order, blocks, slots, COL_UNROLL, visit)
    least, most = bounds[:1, :], bounds[1:2, :]
    sums = total[...]
    result = jnp.where(sums > 0.0, jnp.log2(sums) - COL_OFFSET, very_negative)
    out_ref[...] = result.reshape(out_ref.shape)
    fine = jnp.logical_and(jnp.min(least) >= SMALLEST, jnp.max(most) <= LARGEST / blocks)

    @pl.when(jnp.logical_not(fine))
    def _():
        total[...] = jnp.full_like(total, very_negative)

        @pl.loop(0, blocks)
        def _(r):
            scores = products(x_ref, y_ref, f_ref, cols, slots, r, COL_OFFSET)
            live = counts[r]
            for k, row in enumerate(shifts(cols, counts, g_ref, slots, r)):

                @pl.when(k < live)
                def _():
                    part = scores[:, k * TILE : (k + 1) * TILE] + row
                    top = jnp.max(part, axis=0, keepdims=True)
                    summed = jnp.sum(jnp.exp2(part - top), axis=0, keepdims=True)
                    mine = top - COL_OFFSET + jnp.log2(summed)
                    at = pl.ds(cols[k, r], 1)
                    old = total[at, :]
                    peak = jnp.maximum(old, mine)
                    total[at, :] = peak + jnp.log2(jnp.exp2(old - peak) + jnp.exp2(mine - peak))

        out_ref[...] = total[...].reshape(out_ref.shape)

    if last is not None:
        source_copy.wait()


SMEM = functools.partial(pl.BlockSpec, memory_space=pltpu.SMEM)
VMEM = functools.partial(pl.BlockSpec, memory_space=pltpu.VMEM)
ANY = functools.partial(pl.BlockSpec, memory_space=pl.ANY)


def first_row_pass(cols, counts, source_mass, target_mass, source_points, target_points, slots):
    width, rows = source_points.shape
    blocks = rows // TILE
    target_blocks = target_points.shape[1] // TILE
    shape = jax.ShapeDtypeStruct
    bf16, f32 = jnp.bfloat16, jnp.float32
    in_hbm = [
        pltpu.with_memory_space_constraint(v, pltpu.HBM)
        for v in (cols, counts, source_mass, target_mass, source_points, target_points)
    ]
    return pl.pallas_call(
        functools.partial(row_pass_kernel, LOG2E / first_epsilon, slots),
        out_shape=(
            shape((blocks, TILE), f32),
            pltpu.VMEM((blocks, TILE, 2 * width), bf16),
            pltpu.VMEM((blocks, TILE, 2 * width), bf16),
            pltpu.VMEM(target_points.shape, bf16),
            shape((target_blocks, TILE), f32),
            shape((blocks, TILE), f32),
            shape((blocks, TILE), f32),
            shape((target_blocks, TILE), f32),
            shape((8, TILE), f32),
            shape((blocks + 1,), jnp.int32),
        ),
        in_specs=[ANY()] * 6,
        out_specs=(VMEM(),) * 9 + (SMEM(),),
        scratch_shapes=[
            pltpu.VMEM((TILE, blocks), f32),
            pltpu.VMEM(source_points.shape, bf16),
            pltpu.SMEM(cols.shape, jnp.int32),
            pltpu.SMEM(counts.shape, jnp.int32),
            pltpu.SemaphoreType.DMA((5,)),
            pltpu.SemaphoreType.DMA((target_blocks // CHUNK,)),
        ],
        name="row_pass_first",
        compiler_params=pltpu.CompilerParams(vmem_limit_bytes=VMEM_LIMIT),
    )(*in_hbm)


def row_pass(lists, x, y, f_pot, g_pot, g_first, log_b, mass, slots):
    return pl.pallas_call(
        functools.partial(row_pass_kernel, None, slots),
        out_shape=jax.ShapeDtypeStruct((f_pot.shape[0] + 16, TILE), jnp.float32),
        in_specs=[SMEM()] * 3 + [VMEM()] * 7,
        out_specs=VMEM(),
        scratch_shapes=[pltpu.VMEM((TILE, f_pot.shape[0]), jnp.float32)],
        name="row_pass",
        compiler_params=pltpu.CompilerParams(vmem_limit_bytes=VMEM_LIMIT),
    )(*lists, x, y, f_pot, g_pot, g_first, log_b, mass)


def col_pass(lists, x, y, f_pot, g_pot, slots, devices, last=None):
    target_blocks = g_pot.shape[0]
    out = jax.ShapeDtypeStruct((devices, target_blocks // devices, TILE), jnp.float32)
    scratch = [pltpu.VMEM((target_blocks, TILE), jnp.float32), pltpu.VMEM((8, TILE), jnp.float32)]
    more, scales, out_specs = (), None, VMEM()
    if last is not None:
        more, scales = last[:2], last[2:]
        out, out_specs = (out, pltpu.HBM(f_pot.shape, jnp.float32)), (VMEM(), ANY())
        scratch += [pltpu.VMEM(f_pot.shape, jnp.float32), pltpu.SemaphoreType.DMA]
    return pl.pallas_call(
        functools.partial(col_pass_kernel, slots, scales),
        out_shape=out,
        in_specs=[SMEM()] * 3 + [VMEM()] * (4 + len(more)),
        out_specs=out_specs,
        scratch_shapes=scratch,
        name="col_pass",
        compiler_params=pltpu.CompilerParams(vmem_limit_bytes=VMEM_LIMIT),
    )(*lists, x, y, f_pot, g_pot, *more)


def combine_kernel(epsilon, both_eps, *refs):
    if both_eps is None:
        first_own, stack_ref, b_ref, g_ref, send_ref, new_ref = refs
    else:
        first_own, stack_ref, b_ref, g_ref, first_ref, totals_ref, send_ref = refs
    devices, own, _ = stack_ref.shape
    here = pl.ds(pl.multiple_of(first_own[0], own), own)
    top = stack_ref[0]
    for d in range(1, devices):
        top = jnp.maximum(top, stack_ref[d])
    summed = jnp.exp2(stack_ref[0] - top)
    for d in range(1, devices):
        summed += jnp.exp2(stack_ref[d] - top)
    gain = b_ref[here, :] - (top + jnp.log2(summed))
    if both_eps is None:
        new = 2.0 * (g_ref[here, :] + gain)
        new_ref[...] = new
    else:
        difference = totals_ref[8:9, :] - totals_ref[:1, :]
        half = first_ref[here, :] * first_epsilon
        new = LN2 * (epsilon * (g_ref[...] + gain) + both_eps * difference - half)
    for d in range(devices):
        send_ref[d] = new


def combine(first_own, stack, log_b, g_pot, last):
    shape = jax.ShapeDtypeStruct
    send = shape(stack.shape, jnp.float32)
    if last is None:
        more, scales = (), (None, None)
        out = (send, shape(stack.shape[1:], jnp.float32))
    else:
        more, scales = last[:2], last[2:]
        out = send
    return pl.pallas_call(
        functools.partial(combine_kernel, *scales),
        out_shape=out,
        in_specs=[SMEM()] + [VMEM()] * (3 + len(more)),
        out_specs=jax.tree.map(lambda _: VMEM(), out),
        name="combine",
        compiler_params=pltpu.CompilerParams(vmem_limit_bytes=VMEM_LIMIT // 2),
    )(first_own, stack, log_b, g_pot, *more)


def lse_of(parts):
    top = functools.reduce(jnp.maximum, parts)
    return top + jnp.log2(sum(jnp.exp2(part - top) for part in parts))


def over_cols(part, cols):
    def moved(value, pairs):
        return lax.ppermute(value, "col", pairs)

    part = lse_of([part, moved(part, [(i, i ^ 1) for i in range(cols)])])
    masks = range(2, cols, 2)
    return lse_of([part] + [moved(part, [(i, i ^ mask) for i in range(cols)]) for mask in masks])


def exchange(blocks, rest):
    blocks, rest = lax.optimization_barrier((blocks, rest))
    return lax.optimization_barrier((lax.all_to_all(blocks, "row", 0, 0), rest))


def body(source_points, target_points, source_mass, target_mass, tile_cols, tile_counts):
    width, rows = source_points.shape
    row_blocks = rows // TILE
    target_cells = target_points.shape[1]
    target_blocks = target_cells // TILE
    slots = tile_cols.shape[2]
    row_devices = lax.axis_size("row")
    col_devices = lax.axis_size("col")
    own_blocks = target_blocks // row_devices

    cols = tile_cols.transpose(1, 2, 0).reshape(slots, row_blocks)
    counts = tile_counts.reshape(row_blocks)
    mass_a = source_mass.reshape(row_blocks, TILE)
    first_own = (lax.axis_index("row") * own_blocks).reshape(1)
    counts, first_own = lax.optimization_barrier((counts, first_own))

    part, x1, x2, y, g_first, half_x, log_a, log_b, mass, order = first_row_pass(
        cols,
        counts,
        mass_a,
        target_mass.reshape(target_blocks, TILE),
        source_points,
        target_points,
        slots,
    )
    lists = (cols, counts, order)
    x1, x2, y = (pltpu.with_memory_space_constraint(v, pltpu.VMEM) for v in (x1, x2, y))

    f_pot = log_a - over_cols(part, col_devices)
    part = col_pass(lists, x1, y, f_pot, g_first, slots, row_devices)
    stack, (f_pot, first_own) = exchange(part, (2.0 * f_pot, first_own))
    send, g_own = combine(first_own, stack, log_b, g_first, None)
    g_pot, (f_pot, first_own) = exchange(send, (f_pot, first_own))
    g_pot = g_pot.reshape(target_blocks, TILE)

    first, second = first_epsilon, 0.5 * first_epsilon
    part = row_pass(lists, x2, y, f_pot, g_pot, g_first, log_b, mass, slots)
    both = over_cols(part, col_devices)
    part, totals = both[:row_blocks], both[row_blocks:]
    f_pot = f_pot + (log_a - part)
    part, source = col_pass(
        lists, x2, y, f_pot, g_pot, slots, row_devices, (half_x, totals, second, first)
    )
    stack, (totals, first_own) = exchange(part, (totals, first_own))
    send = combine(first_own, stack, log_b, g_own, (g_first, totals, second, first + second))
    target = lax.all_to_all(send, "row", 0, 0)
    return (source.reshape(rows), target.reshape(target_cells))


def solution(mesh):
    return jax.shard_map(
        body,
        mesh=mesh,
        in_specs=(
            P(None, "row"),
            P(None, "col"),
            P("row"),
            P("col"),
            P("row", "col", None),
            P("row", "col"),
        ),
        out_specs=(P("row"), P("col")),
        check_vma=False,
    )
```

```python
import functools

import jax
import jax.numpy as jnp
from jax import lax
from jax.experimental import pallas as pl
from jax.experimental.pallas import tpu as pltpu
from jax.sharding import PartitionSpec as P

TILE = 128
very_negative = -1e30
first_epsilon = 0.5
LOG2E = 1.4426950408889634
LN2 = 0.6931471805599453
SMALLEST = 2.0**-100
LARGEST = 2.0**120
VMEM_LIMIT = 16 * 1024 * 1024
LESS = 56
HALF = 32
UNROLL = 8
CHUNK = 64
ROW_OFFSET = 64.0
COL_OFFSET = 80.0


def split3(row):
    hi = row.astype(jnp.bfloat16).astype(jnp.float32)
    rest = row - hi
    mid = rest.astype(jnp.bfloat16).astype(jnp.float32)
    lo = (rest - mid).astype(jnp.bfloat16).astype(jnp.float32)
    return hi, mid, lo


def products(x_ref, y_ref, f_ref, cols, slots, r, offset):
    lhs = x_ref[r]
    picked = [
        y_ref[:, pl.ds(pl.multiple_of(cols[k, r] * TILE, TILE), TILE)]
        for k in range(slots)
    ]
    yb = jnp.concatenate(picked, axis=1)
    rhs = [yb, yb]
    if f_ref is not None:
        hi, mid, lo = split3(f_ref[pl.ds(r, 1), :] + offset)
        place = lax.broadcasted_iota(jnp.int32, (16, TILE), 0)
        extra = jnp.where(
            place == 0, hi, jnp.where(place == 1, mid, jnp.where(place == 2, lo, 0.0))
        )
        lhs = jnp.concatenate([lhs, extra.astype(jnp.bfloat16).T], axis=1)
        rhs.append(jnp.ones((16, yb.shape[1]), jnp.bfloat16))
    return jnp.dot(lhs, jnp.concatenate(rhs, axis=0), preferred_element_type=jnp.float32)


def shifts(cols, counts, g_ref, slots, r):
    live = counts[r]
    return [
        jnp.where(k < live, g_ref[pl.ds(cols[k, r], 1), :], very_negative)
        for k in range(slots)
    ]


def make_order(order, counts, blocks, slots):
    def count(r, found):
        return found + jnp.where(counts[r] == slots, 1, 0)

    whole = lax.fori_loop(0, blocks, count, 0, unroll=8)

    def place(r, found):
        full, less, half = found
        is_full, is_half = counts[r] == slots, counts[r] <= slots // 2
        at = jnp.where(is_full, full, jnp.where(is_half, blocks - 1 - half, less))
        order[at] = r
        one = jnp.where(is_half, 0, 1)
        return (
            full + jnp.where(is_full, 1, 0),
            less + jnp.where(is_full, 0, one),
            half + 1 - one,
        )

    half = lax.fori_loop(0, blocks, place, (0, whole, 0), unroll=4)[2]
    short = jnp.logical_and(blocks - whole >= LESS, half >= HALF)
    order[blocks] = jnp.where(short, 1, 0)


def over_rows(order, blocks, slots, visit, load, store):
    short = order[blocks] == 1

    @pl.when(short)
    def _():
        carry = load()
        for at in range(blocks):
            width = slots if at < blocks - LESS else slots - 1
            width = width if at < blocks - HALF else slots // 2
            carry = visit(order[at], width, carry)
        store(carry)

    @pl.when(jnp.logical_not(short))
    def _():
        def one(at, carry):
            return visit(order[at], slots, carry)

        store(lax.fori_loop(0, blocks, one, load(), unroll=UNROLL))


def log2_sum(values):
    summed = jnp.sum(jnp.sum(values, axis=0, keepdims=True), axis=1, keepdims=True)
    return jnp.broadcast_to(jnp.log2(summed), (8, TILE))


def prepare(kappa, x_hbm, y_hbm, x_ref, x2_ref, y_ref, g_ref, hx_ref, x_in, x_sem, y_sem, others, masses, then):
    width = y_ref.shape[0]
    blocks = hx_ref.shape[0]
    target_blocks = g_ref.shape[0]
    chunks = target_blocks // CHUNK
    x_copy = pltpu.make_async_copy(x_hbm, x_in, x_sem)
    beside = blocks * 8 // target_blocks

    def y_copy(c):
        at = pl.ds(pl.multiple_of(c * (CHUNK * TILE), CHUNK * TILE), CHUNK * TILE)
        return pltpu.make_async_copy(y_hbm.at[:, at], y_ref.at[:, at], y_sem.at[c])

    def source_block(r):
        xf = x_in[:, pl.ds(pl.multiple_of(r * TILE, TILE), TILE)].astype(jnp.float32)
        hx_ref[pl.ds(r, 1), :] = 0.5 * jnp.sum(xf * xf, axis=0, keepdims=True)
        scaled = xf * kappa
        hi = scaled.astype(jnp.bfloat16)
        lo = (scaled - hi.astype(jnp.float32)).astype(jnp.bfloat16)
        turned = jnp.concatenate([hi, lo], axis=0).T
        x_ref[r] = turned
        x2_ref[r] = turned + turned

    for other in others:
        other.start()
    x_copy.start()

    @pl.loop(0, chunks)
    def _(c):
        y_copy(c).start()

    for other in masses:
        other.start()
    for other in others:
        other.wait()
    then()
    x_copy.wait()

    @pl.loop(0, chunks)
    def _(c):
        y_copy(c).wait()

        @pl.loop(0, CHUNK // 8, unroll=4)
        def _(q):
            group = c * (CHUNK // 8) + q
            at = pl.ds(pl.multiple_of(group * (8 * TILE), 8 * TILE), 8 * TILE)
            yf = y_ref[:, at].astype(jnp.float32)
            half = (-0.5 * kappa) * jnp.sum(yf * yf, axis=0, keepdims=True)
            for k in range(8):
                g_ref[pl.ds(group * 8 + k, 1), :] = half[:, k * TILE : (k + 1) * TILE]
            for k in range(beside):
                source_block(group * beside + k)


def row_pass_kernel(kappa, slots, *refs):
    if kappa is not None:
        (cols_hbm, counts_hbm, a_hbm, b_hbm, x_hbm, y_hbm, out_ref, x_ref, x2_ref,
         y_ref, g_ref, hx_ref, a_ref, b_ref, mass_ref, order, total, x_in, cols, counts, sems,
         y_sem) = refs
        f_ref = None
        small = ((cols_hbm, cols), (counts_hbm, counts), (a_hbm, a_ref), (b_hbm, b_ref))
        copies = [
            pltpu.make_async_copy(source, target, sems.at[1 + i])
            for i, (source, target) in enumerate(small)
        ]
        others, masses = copies[:2], copies[2:]
        prepare(kappa, x_hbm, y_hbm, x_ref, x2_ref, y_ref, g_ref, hx_ref, x_in, sems.at[0],
                y_sem, others, masses, lambda: make_order(order, counts, total.shape[1], slots))
        offset = 0.0
    else:
        (cols, counts, order, x_ref, y_ref, f_ref, g_ref, g_first_ref, b_ref, mass_ref, out_ref,
         total) = refs
        offset = ROW_OFFSET
    blocks = total.shape[1]
    lane = lax.broadcasted_iota(jnp.int32, (TILE, TILE), 1)

    def visit(r, width, carry):
        scores = products(x_ref, y_ref, f_ref, cols, width, r, offset)
        terms = None
        for k, row in enumerate(shifts(cols, counts, g_ref, width, r)):
            term = jnp.exp2(scores[:, k * TILE : (k + 1) * TILE] + row)
            terms = term if terms is None else terms + term
        summed = jnp.sum(terms, axis=1, keepdims=True)
        total[...] = jnp.where(lane == r, summed, total[...])
        return carry

    over_rows(order, blocks, slots, visit, lambda: 0, lambda carry: None)

    sums = total[...]
    out_ref[:blocks, :] = (jnp.log2(sums) - offset).T
    if kappa is not None:
        for other in masses:
            other.wait()
        mass_ref[...] = log2_sum(b_ref[...])
        a_ref[...] = jnp.log2(a_ref[...])
        b_ref[...] = jnp.log2(b_ref[...])
    else:
        out_ref[blocks : blocks + 8, :] = mass_ref[...]
        last = g_first_ref[...] + b_ref[...] - 0.5 * g_ref[...]
        out_ref[blocks + 8 :, :] = log2_sum(jnp.exp2(last))
    fine = jnp.logical_and(jnp.min(sums) >= SMALLEST, jnp.max(sums) <= LARGEST)

    @pl.when(jnp.logical_not(fine))
    def _():
        @pl.loop(0, blocks)
        def _(r):
            scores = products(x_ref, y_ref, f_ref, cols, slots, r, offset)
            rows = shifts(cols, counts, g_ref, slots, r)
            parts = [scores[:, k * TILE : (k + 1) * TILE] + row for k, row in enumerate(rows)]
            top = functools.reduce(jnp.maximum, parts)
            top = jnp.max(top, axis=1, keepdims=True)
            terms = sum(jnp.exp2(part - top) for part in parts)
            summed = jnp.sum(terms, axis=1, keepdims=True)
            total[...] = jnp.where(lane == r, top + jnp.log2(summed), total[...])

        out_ref[:blocks, :] = (total[...] - offset).T


def col_pass_kernel(slots, last, *refs):
    if last is None:
        cols, counts, order, x_ref, y_ref, f_ref, g_ref, out_ref, total, bounds = refs
    else:
        (cols, counts, order, x_ref, y_ref, f_ref, g_ref, hx_ref, totals_ref, out_ref, source_hbm,
         total, bounds, source, sem) = refs
        second, first = last
        total_b, total_a = totals_ref[:1, :], totals_ref[8:9, :]
        shift = first * total_b - (second + first) * total_a
        source[...] = hx_ref[...] + LN2 * (second * f_ref[...] + shift)
        source_copy = pltpu.make_async_copy(source, source_hbm, sem)
        source_copy.start()
    blocks = f_ref.shape[0]
    total[...] = jnp.zeros_like(total)

    bounds[...] = jnp.ones_like(bounds)

    def visit(r, width, carry):
        least, most = carry
        scores = products(x_ref, y_ref, f_ref, cols, width, r, COL_OFFSET)
        live = counts[r]
        for k, row in enumerate(shifts(cols, counts, g_ref, width, r)):
            terms = jnp.exp2(scores[:, k * TILE : (k + 1) * TILE] + row)
            summed = jnp.sum(terms, axis=0, keepdims=True)
            total[pl.ds(cols[k, r], 1), :] += summed
            least = jnp.minimum(least, jnp.where(k < live, summed, 1.0))
            most = jnp.maximum(most, summed)
        return least, most

    def load():
        return bounds[:1, :], bounds[1:2, :]

    def store(carry):
        bounds[:1, :], bounds[1:2, :] = carry

    over_rows(order, blocks, slots, visit, load, store)
    least, most = bounds[:1, :], bounds[1:2, :]
    sums = total[...]
    result = jnp.where(sums > 0.0, jnp.log2(sums) - COL_OFFSET, very_negative)
    out_ref[...] = result.reshape(out_ref.shape)
    fine = jnp.logical_and(jnp.min(least) >= SMALLEST, jnp.max(most) <= LARGEST / blocks)

    @pl.when(jnp.logical_not(fine))
    def _():
        total[...] = jnp.full_like(total, very_negative)

        @pl.loop(0, blocks)
        def _(r):
            scores = products(x_ref, y_ref, f_ref, cols, slots, r, COL_OFFSET)
            live = counts[r]
            for k, row in enumerate(shifts(cols, counts, g_ref, slots, r)):

                @pl.when(k < live)
                def _():
                    part = scores[:, k * TILE : (k + 1) * TILE] + row
                    top = jnp.max(part, axis=0, keepdims=True)
                    summed = jnp.sum(jnp.exp2(part - top), axis=0, keepdims=True)
                    mine = top - COL_OFFSET + jnp.log2(summed)
                    at = pl.ds(cols[k, r], 1)
                    old = total[at, :]
                    peak = jnp.maximum(old, mine)
                    total[at, :] = peak + jnp.log2(jnp.exp2(old - peak) + jnp.exp2(mine - peak))

        out_ref[...] = total[...].reshape(out_ref.shape)

    if last is not None:
        source_copy.wait()


SMEM = functools.partial(pl.BlockSpec, memory_space=pltpu.SMEM)
VMEM = functools.partial(pl.BlockSpec, memory_space=pltpu.VMEM)
ANY = functools.partial(pl.BlockSpec, memory_space=pl.ANY)


def first_row_pass(cols, counts, source_mass, target_mass, source_points, target_points, slots):
    width, rows = source_points.shape
    blocks = rows // TILE
    target_blocks = target_points.shape[1] // TILE
    shape = jax.ShapeDtypeStruct
    bf16, f32 = jnp.bfloat16, jnp.float32
    in_hbm = [
        pltpu.with_memory_space_constraint(v, pltpu.HBM)
        for v in (cols, counts, source_mass, target_mass, source_points, target_points)
    ]
    return pl.pallas_call(
        functools.partial(row_pass_kernel, LOG2E / first_epsilon, slots),
        out_shape=(
            shape((blocks, TILE), f32),
            pltpu.VMEM((blocks, TILE, 2 * width), bf16),
            pltpu.VMEM((blocks, TILE, 2 * width), bf16),
            pltpu.VMEM(target_points.shape, bf16),
            shape((target_blocks, TILE), f32),
            shape((blocks, TILE), f32),
            shape((blocks, TILE), f32),
            shape((target_blocks, TILE), f32),
            shape((8, TILE), f32),
            shape((blocks + 1,), jnp.int32),
        ),
        in_specs=[ANY()] * 6,
        out_specs=(VMEM(),) * 9 + (SMEM(),),
        scratch_shapes=[
            pltpu.VMEM((TILE, blocks), f32),
            pltpu.VMEM(source_points.shape, bf16),
            pltpu.SMEM(cols.shape, jnp.int32),
            pltpu.SMEM(counts.shape, jnp.int32),
            pltpu.SemaphoreType.DMA((5,)),
            pltpu.SemaphoreType.DMA((target_blocks // CHUNK,)),
        ],
        name="row_pass_first",
        compiler_params=pltpu.CompilerParams(vmem_limit_bytes=VMEM_LIMIT),
    )(*in_hbm)


def row_pass(lists, x, y, f_pot, g_pot, g_first, log_b, mass, slots):
    return pl.pallas_call(
        functools.partial(row_pass_kernel, None, slots),
        out_shape=jax.ShapeDtypeStruct((f_pot.shape[0] + 16, TILE), jnp.float32),
        in_specs=[SMEM()] * 3 + [VMEM()] * 7,
        out_specs=VMEM(),
        scratch_shapes=[pltpu.VMEM((TILE, f_pot.shape[0]), jnp.float32)],
        name="row_pass",
        compiler_params=pltpu.CompilerParams(vmem_limit_bytes=VMEM_LIMIT),
    )(*lists, x, y, f_pot, g_pot, g_first, log_b, mass)


def col_pass(lists, x, y, f_pot, g_pot, slots, devices, last=None):
    target_blocks = g_pot.shape[0]
    out = jax.ShapeDtypeStruct((devices, target_blocks // devices, TILE), jnp.float32)
    scratch = [pltpu.VMEM((target_blocks, TILE), jnp.float32), pltpu.VMEM((8, TILE), jnp.float32)]
    more, scales, out_specs = (), None, VMEM()
    if last is not None:
        more, scales = last[:2], last[2:]
        out, out_specs = (out, pltpu.HBM(f_pot.shape, jnp.float32)), (VMEM(), ANY())
        scratch += [pltpu.VMEM(f_pot.shape, jnp.float32), pltpu.SemaphoreType.DMA]
    return pl.pallas_call(
        functools.partial(col_pass_kernel, slots, scales),
        out_shape=out,
        in_specs=[SMEM()] * 3 + [VMEM()] * (4 + len(more)),
        out_specs=out_specs,
        scratch_shapes=scratch,
        name="col_pass",
        compiler_params=pltpu.CompilerParams(vmem_limit_bytes=VMEM_LIMIT),
    )(*lists, x, y, f_pot, g_pot, *more)


def combine_kernel(epsilon, both_eps, *refs):
    if both_eps is None:
        first_own, stack_ref, b_ref, g_ref, send_ref, new_ref = refs
    else:
        first_own, stack_ref, b_ref, g_ref, first_ref, totals_ref, send_ref = refs
    devices, own, _ = stack_ref.shape
    here = pl.ds(pl.multiple_of(first_own[0], own), own)
    top = stack_ref[0]
    for d in range(1, devices):
        top = jnp.maximum(top, stack_ref[d])
    summed = jnp.exp2(stack_ref[0] - top)
    for d in range(1, devices):
        summed += jnp.exp2(stack_ref[d] - top)
    gain = b_ref[here, :] - (top + jnp.log2(summed))
    if both_eps is None:
        new = 2.0 * (g_ref[here, :] + gain)
        new_ref[...] = new
    else:
        difference = totals_ref[8:9, :] - totals_ref[:1, :]
        half = first_ref[here, :] * first_epsilon
        new = LN2 * (epsilon * (g_ref[...] + gain) + both_eps * difference - half)
    for d in range(devices):
        send_ref[d] = new


def combine(first_own, stack, log_b, g_pot, last):
    shape = jax.ShapeDtypeStruct
    send = shape(stack.shape, jnp.float32)
    if last is None:
        more, scales = (), (None, None)
        out = (send, shape(stack.shape[1:], jnp.float32))
    else:
        more, scales = last[:2], last[2:]
        out = send
    return pl.pallas_call(
        functools.partial(combine_kernel, *scales),
        out_shape=out,
        in_specs=[SMEM()] + [VMEM()] * (3 + len(more)),
        out_specs=jax.tree.map(lambda _: VMEM(), out),
        name="combine",
        compiler_params=pltpu.CompilerParams(vmem_limit_bytes=VMEM_LIMIT // 2),
    )(first_own, stack, log_b, g_pot, *more)


def lse_of(parts):
    top = functools.reduce(jnp.maximum, parts)
    return top + jnp.log2(sum(jnp.exp2(part - top) for part in parts))


def over_cols(part, cols):
    def moved(value, pairs):
        return lax.ppermute(value, "col", pairs)

    part = lse_of([part, moved(part, [(i, i ^ 1) for i in range(cols)])])
    masks = range(2, cols, 2)
    return lse_of([part] + [moved(part, [(i, i ^ mask) for i in range(cols)]) for mask in masks])


def exchange(blocks, rest):
    blocks, rest = lax.optimization_barrier((blocks, rest))
    return lax.optimization_barrier((lax.all_to_all(blocks, "row", 0, 0), rest))


def body(source_points, target_points, source_mass, target_mass, tile_cols, tile_counts):
    width, rows = source_points.shape
    row_blocks = rows // TILE
    target_cells = target_points.shape[1]
    target_blocks = target_cells // TILE
    slots = tile_cols.shape[2]
    row_devices = lax.axis_size("row")
    col_devices = lax.axis_size("col")
    own_blocks = target_blocks // row_devices

    cols = tile_cols.transpose(1, 2, 0).reshape(slots, row_blocks)
    counts = tile_counts.reshape(row_blocks)
    mass_a = source_mass.reshape(row_blocks, TILE)
    first_own = (lax.axis_index("row") * own_blocks).reshape(1)
    counts, first_own = lax.optimization_barrier((counts, first_own))

    part, x1, x2, y, g_first, half_x, log_a, log_b, mass, order = first_row_pass(
        cols,
        counts,
        mass_a,
        target_mass.reshape(target_blocks, TILE),
        source_points,
        target_points,
        slots,
    )
    lists = (cols, counts, order)
    x1, x2, y = (pltpu.with_memory_space_constraint(v, pltpu.VMEM) for v in (x1, x2, y))

    f_pot = log_a - over_cols(part, col_devices)
    part = col_pass(lists, x1, y, f_pot, g_first, slots, row_devices)
    stack, (f_pot, first_own) = exchange(part, (2.0 * f_pot, first_own))
    send, g_own = combine(first_own, stack, log_b, g_first, None)
    g_pot, (f_pot, first_own) = exchange(send, (f_pot, first_own))
    g_pot = g_pot.reshape(target_blocks, TILE)

    first, second = first_epsilon, 0.5 * first_epsilon
    part = row_pass(lists, x2, y, f_pot, g_pot, g_first, log_b, mass, slots)
    both = over_cols(part, col_devices)
    part, totals = both[:row_blocks], both[row_blocks:]
    f_pot = f_pot + (log_a - part)
    part, source = col_pass(
        lists, x2, y, f_pot, g_pot, slots, row_devices, (half_x, totals, second, first)
    )
    stack, (totals, first_own) = exchange(part, (totals, first_own))
    send = combine(first_own, stack, log_b, g_own, (g_first, totals, second, first + second))
    target = lax.all_to_all(send, "row", 0, 0)
    return (source.reshape(rows), target.reshape(target_cells))


def solution(mesh):
    return jax.shard_map(
        body,
        mesh=mesh,
        in_specs=(
            P(None, "row"),
            P(None, "col"),
            P("row"),
            P("col"),
            P("row", "col", None),
            P("row", "col"),
        ),
        out_specs=(P("row"), P("col")),
        check_vma=False,
    )
```

```python
import functools

import jax
import jax.numpy as jnp
from jax import lax
from jax.experimental import pallas as pl
from jax.experimental.pallas import tpu as pltpu
from jax.sharding import PartitionSpec as P

TILE = 128
very_negative = -1e30
first_epsilon = 0.5
LOG2E = 1.4426950408889634
LN2 = 0.6931471805599453
SMALLEST = 2.0**-100
LARGEST = 2.0**120
VMEM_LIMIT = 16 * 1024 * 1024
LESS = 56
HALF = 32
UNROLL = 8
CHUNK = 64
ROW_OFFSET = 64.0
COL_OFFSET = 80.0


def split3(row):
    hi = row.astype(jnp.bfloat16).astype(jnp.float32)
    rest = row - hi
    mid = rest.astype(jnp.bfloat16).astype(jnp.float32)
    lo = (rest - mid).astype(jnp.bfloat16).astype(jnp.float32)
    return hi, mid, lo


def products(x_ref, y_ref, f_ref, cols, slots, r, offset):
    lhs = x_ref[r]
    picked = [
        y_ref[:, pl.ds(pl.multiple_of(cols[k, r] * TILE, TILE), TILE)]
        for k in range(slots)
    ]
    yb = jnp.concatenate(picked, axis=1)
    rhs = [yb, yb]
    if f_ref is not None:
        hi, mid, lo = split3(f_ref[pl.ds(r, 1), :] + offset)
        place = lax.broadcasted_iota(jnp.int32, (16, TILE), 0)
        extra = jnp.where(
            place == 0, hi, jnp.where(place == 1, mid, jnp.where(place == 2, lo, 0.0))
        )
        lhs = jnp.concatenate([lhs, extra.astype(jnp.bfloat16).T], axis=1)
        rhs.append(jnp.ones((16, yb.shape[1]), jnp.bfloat16))
    return jnp.dot(lhs, jnp.concatenate(rhs, axis=0), preferred_element_type=jnp.float32)


def shifts(cols, counts, g_ref, slots, r):
    live = counts[r]
    return [
        jnp.where(k < live, g_ref[pl.ds(cols[k, r], 1), :], very_negative)
        for k in range(slots)
    ]


def make_order(order, counts, blocks, slots):
    def count(r, found):
        return found + jnp.where(counts[r] == slots, 1, 0)

    whole = lax.fori_loop(0, blocks, count, 0, unroll=8)

    def place(r, found):
        full, less, half = found
        is_full, is_half = counts[r] == slots, counts[r] <= slots // 2
        at = jnp.where(is_full, full, jnp.where(is_half, blocks - 1 - half, less))
        order[at] = r
        one = jnp.where(is_half, 0, 1)
        return (
            full + jnp.where(is_full, 1, 0),
            less + jnp.where(is_full, 0, one),
            half + 1 - one,
        )

    half = lax.fori_loop(0, blocks, place, (0, whole, 0), unroll=4)[2]
    short = jnp.logical_and(blocks - whole >= LESS, half >= HALF)
    order[blocks] = jnp.where(short, 1, 0)


def over_rows(order, blocks, slots, visit, load, store):
    short = order[blocks] == 1

    @pl.when(short)
    def _():
        carry = load()
        for at in range(blocks):
            width = slots if at < blocks - LESS else slots - 1
            width = width if at < blocks - HALF else slots // 2
            carry = visit(order[at], width, carry)
        store(carry)

    @pl.when(jnp.logical_not(short))
    def _():
        def one(at, carry):
            return visit(order[at], slots, carry)

        store(lax.fori_loop(0, blocks, one, load(), unroll=UNROLL))


def log2_sum(values):
    summed = jnp.sum(jnp.sum(values, axis=0, keepdims=True), axis=1, keepdims=True)
    return jnp.broadcast_to(jnp.log2(summed), (8, TILE))


def prepare(kappa, x_hbm, y_hbm, x_ref, x2_ref, y_ref, g_ref, hx_ref, x_in, x_sem, y_sem, others, masses, then):
    width = y_ref.shape[0]
    blocks = hx_ref.shape[0]
    target_blocks = g_ref.shape[0]
    chunks = target_blocks // CHUNK
    x_copy = pltpu.make_async_copy(x_hbm, x_in, x_sem)
    beside = blocks * 8 // target_blocks

    def y_copy(c):
        at = pl.ds(pl.multiple_of(c * (CHUNK * TILE), CHUNK * TILE), CHUNK * TILE)
        return pltpu.make_async_copy(y_hbm.at[:, at], y_ref.at[:, at], y_sem.at[c])

    def source_block(r):
        xf = x_in[:, pl.ds(pl.multiple_of(r * TILE, TILE), TILE)].astype(jnp.float32)
        hx_ref[pl.ds(r, 1), :] = 0.5 * jnp.sum(xf * xf, axis=0, keepdims=True)
        scaled = xf * kappa
        hi = scaled.astype(jnp.bfloat16)
        lo = (scaled - hi.astype(jnp.float32)).astype(jnp.bfloat16)
        turned = jnp.concatenate([hi, lo], axis=0).T
        x_ref[r] = turned
        x2_ref[r] = turned + turned

    for other in others:
        other.start()
    x_copy.start()

    @pl.loop(0, chunks)
    def _(c):
        y_copy(c).start()

    for other in masses:
        other.start()
    for other in others:
        other.wait()
    then()
    x_copy.wait()

    @pl.loop(0, chunks)
    def _(c):
        y_copy(c).wait()

        @pl.loop(0, CHUNK // 8, unroll=4)
        def _(q):
            group = c * (CHUNK // 8) + q
            at = pl.ds(pl.multiple_of(group * (8 * TILE), 8 * TILE), 8 * TILE)
            yf = y_ref[:, at].astype(jnp.float32)
            half = (-0.5 * kappa) * jnp.sum(yf * yf, axis=0, keepdims=True)
            for k in range(8):
                g_ref[pl.ds(group * 8 + k, 1), :] = half[:, k * TILE : (k + 1) * TILE]
            for k in range(beside):
                source_block(group * beside + k)


def start_lists(sources, targets, sems):
    copies = [
        pltpu.make_async_copy(source, target, sems.at[i])
        for i, (source, target) in enumerate(zip(sources, targets))
    ]
    for copy in copies:
        copy.start()
    return copies


def list_scratch(lists):
    return [pltpu.SMEM(v.shape, v.dtype) for v in lists] + [
        pltpu.SemaphoreType.DMA((len(lists),))
    ]


def row_pass_kernel(kappa, slots, *refs):
    if kappa is not None:
        (cols_hbm, counts_hbm, a_hbm, b_hbm, x_hbm, y_hbm, out_ref, x_ref, x2_ref,
         y_ref, g_ref, hx_ref, a_ref, b_ref, mass_ref, order, total, x_in, cols, counts, sems,
         y_sem) = refs
        f_ref = None
        small = ((cols_hbm, cols), (counts_hbm, counts), (a_hbm, a_ref), (b_hbm, b_ref))
        copies = [
            pltpu.make_async_copy(source, target, sems.at[1 + i])
            for i, (source, target) in enumerate(small)
        ]
        others, masses = copies[:2], copies[2:]
        prepare(kappa, x_hbm, y_hbm, x_ref, x2_ref, y_ref, g_ref, hx_ref, x_in, sems.at[0],
                y_sem, others, masses, lambda: make_order(order, counts, total.shape[1], slots))
        offset = 0.0
    else:
        (*lists, x_ref, y_ref, f_ref, g_ref, g_first_ref, b_ref, mass_ref, out_ref, total, cols,
         counts, order, list_sems) = refs
        lists = start_lists(lists, (cols, counts, order), list_sems)
        blocks = total.shape[1]
        out_ref[blocks : blocks + 8, :] = mass_ref[...]
        last = g_first_ref[...] + b_ref[...] - 0.5 * g_ref[...]
        out_ref[blocks + 8 :, :] = log2_sum(jnp.exp2(last))
        for copy in lists:
            copy.wait()
        offset = ROW_OFFSET
    blocks = total.shape[1]
    lane = lax.broadcasted_iota(jnp.int32, (TILE, TILE), 1)

    def visit(r, width, carry):
        scores = products(x_ref, y_ref, f_ref, cols, width, r, offset)
        terms = None
        for k, row in enumerate(shifts(cols, counts, g_ref, width, r)):
            term = jnp.exp2(scores[:, k * TILE : (k + 1) * TILE] + row)
            terms = term if terms is None else terms + term
        summed = jnp.sum(terms, axis=1, keepdims=True)
        total[...] = jnp.where(lane == r, summed, total[...])
        return carry

    over_rows(order, blocks, slots, visit, lambda: 0, lambda carry: None)

    sums = total[...]
    out_ref[:blocks, :] = (jnp.log2(sums) - offset).T
    if kappa is not None:
        for other in masses:
            other.wait()
        mass_ref[...] = log2_sum(b_ref[...])
        a_ref[...] = jnp.log2(a_ref[...])
        b_ref[...] = jnp.log2(b_ref[...])
    fine = jnp.logical_and(jnp.min(sums) >= SMALLEST, jnp.max(sums) <= LARGEST)

    @pl.when(jnp.logical_not(fine))
    def _():
        @pl.loop(0, blocks)
        def _(r):
            scores = products(x_ref, y_ref, f_ref, cols, slots, r, offset)
            rows = shifts(cols, counts, g_ref, slots, r)
            parts = [scores[:, k * TILE : (k + 1) * TILE] + row for k, row in enumerate(rows)]
            top = functools.reduce(jnp.maximum, parts)
            top = jnp.max(top, axis=1, keepdims=True)
            terms = sum(jnp.exp2(part - top) for part in parts)
            summed = jnp.sum(terms, axis=1, keepdims=True)
            total[...] = jnp.where(lane == r, top + jnp.log2(summed), total[...])

        out_ref[:blocks, :] = (total[...] - offset).T


def col_pass_kernel(slots, last, *refs):
    if last is None:
        cols, counts, order, x_ref, y_ref, f_ref, g_ref, out_ref, total, bounds = refs
    else:
        (cols, counts, order, x_ref, y_ref, f_ref, g_ref, hx_ref, totals_ref, out_ref, source_hbm,
         total, bounds, source, sem) = refs
        second, first = last
        total_b, total_a = totals_ref[:1, :], totals_ref[8:9, :]
        shift = first * total_b - (second + first) * total_a
        source[...] = hx_ref[...] + LN2 * (second * f_ref[...] + shift)
        source_copy = pltpu.make_async_copy(source, source_hbm, sem)
        source_copy.start()
    blocks = f_ref.shape[0]
    total[...] = jnp.zeros_like(total)

    bounds[...] = jnp.ones_like(bounds)

    def visit(r, width, carry):
        least, most = carry
        scores = products(x_ref, y_ref, f_ref, cols, width, r, COL_OFFSET)
        live = counts[r]
        for k, row in enumerate(shifts(cols, counts, g_ref, width, r)):
            terms = jnp.exp2(scores[:, k * TILE : (k + 1) * TILE] + row)
            summed = jnp.sum(terms, axis=0, keepdims=True)
            total[pl.ds(cols[k, r], 1), :] += summed
            least = jnp.minimum(least, jnp.where(k < live, summed, 1.0))
            most = jnp.maximum(most, summed)
        return least, most

    def load():
        return bounds[:1, :], bounds[1:2, :]

    def store(carry):
        bounds[:1, :], bounds[1:2, :] = carry

    over_rows(order, blocks, slots, visit, load, store)
    least, most = bounds[:1, :], bounds[1:2, :]
    sums = total[...]
    result = jnp.where(sums > 0.0, jnp.log2(sums) - COL_OFFSET, very_negative)
    out_ref[...] = result.reshape(out_ref.shape)
    fine = jnp.logical_and(jnp.min(least) >= SMALLEST, jnp.max(most) <= LARGEST / blocks)

    @pl.when(jnp.logical_not(fine))
    def _():
        total[...] = jnp.full_like(total, very_negative)

        @pl.loop(0, blocks)
        def _(r):
            scores = products(x_ref, y_ref, f_ref, cols, slots, r, COL_OFFSET)
            live = counts[r]
            for k, row in enumerate(shifts(cols, counts, g_ref, slots, r)):

                @pl.when(k < live)
                def _():
                    part = scores[:, k * TILE : (k + 1) * TILE] + row
                    top = jnp.max(part, axis=0, keepdims=True)
                    summed = jnp.sum(jnp.exp2(part - top), axis=0, keepdims=True)
                    mine = top - COL_OFFSET + jnp.log2(summed)
                    at = pl.ds(cols[k, r], 1)
                    old = total[at, :]
                    peak = jnp.maximum(old, mine)
                    total[at, :] = peak + jnp.log2(jnp.exp2(old - peak) + jnp.exp2(mine - peak))

        out_ref[...] = total[...].reshape(out_ref.shape)

    if last is not None:
        source_copy.wait()


SMEM = functools.partial(pl.BlockSpec, memory_space=pltpu.SMEM)
VMEM = functools.partial(pl.BlockSpec, memory_space=pltpu.VMEM)
ANY = functools.partial(pl.BlockSpec, memory_space=pl.ANY)


def first_row_pass(cols, counts, source_mass, target_mass, source_points, target_points, slots):
    width, rows = source_points.shape
    blocks = rows // TILE
    target_blocks = target_points.shape[1] // TILE
    shape = jax.ShapeDtypeStruct
    bf16, f32 = jnp.bfloat16, jnp.float32
    in_hbm = [
        pltpu.with_memory_space_constraint(v, pltpu.HBM)
        for v in (cols, counts, source_mass, target_mass, source_points, target_points)
    ]
    return pl.pallas_call(
        functools.partial(row_pass_kernel, LOG2E / first_epsilon, slots),
        out_shape=(
            shape((blocks, TILE), f32),
            pltpu.VMEM((blocks, TILE, 2 * width), bf16),
            pltpu.VMEM((blocks, TILE, 2 * width), bf16),
            pltpu.VMEM(target_points.shape, bf16),
            shape((target_blocks, TILE), f32),
            shape((blocks, TILE), f32),
            shape((blocks, TILE), f32),
            shape((target_blocks, TILE), f32),
            shape((8, TILE), f32),
            shape((2 * blocks,), jnp.int32),
        ),
        in_specs=[ANY()] * 6,
        out_specs=(VMEM(),) * 9 + (SMEM(),),
        scratch_shapes=[
            pltpu.VMEM((TILE, blocks), f32),
            pltpu.VMEM(source_points.shape, bf16),
            pltpu.SMEM(cols.shape, jnp.int32),
            pltpu.SMEM(counts.shape, jnp.int32),
            pltpu.SemaphoreType.DMA((5,)),
            pltpu.SemaphoreType.DMA((target_blocks // CHUNK,)),
        ],
        name="row_pass_first",
        compiler_params=pltpu.CompilerParams(vmem_limit_bytes=VMEM_LIMIT),
    )(*in_hbm)


def row_pass(lists, x, y, f_pot, g_pot, g_first, log_b, mass, slots):
    return pl.pallas_call(
        functools.partial(row_pass_kernel, None, slots),
        out_shape=jax.ShapeDtypeStruct((f_pot.shape[0] + 16, TILE), jnp.float32),
        in_specs=[ANY()] * 3 + [VMEM()] * 7,
        out_specs=VMEM(),
        scratch_shapes=[pltpu.VMEM((TILE, f_pot.shape[0]), jnp.float32), *list_scratch(lists)],
        name="row_pass",
        compiler_params=pltpu.CompilerParams(vmem_limit_bytes=VMEM_LIMIT),
    )(*lists, x, y, f_pot, g_pot, g_first, log_b, mass)


def col_pass(lists, x, y, f_pot, g_pot, slots, devices, last=None):
    target_blocks = g_pot.shape[0]
    out = jax.ShapeDtypeStruct((devices, target_blocks // devices, TILE), jnp.float32)
    scratch = [pltpu.VMEM((target_blocks, TILE), jnp.float32), pltpu.VMEM((8, TILE), jnp.float32)]
    more, scales, out_specs = (), None, VMEM()
    if last is not None:
        more, scales = last[:2], last[2:]
        out, out_specs = (out, pltpu.HBM(f_pot.shape, jnp.float32)), (VMEM(), ANY())
        scratch += [pltpu.VMEM(f_pot.shape, jnp.float32), pltpu.SemaphoreType.DMA]
    return pl.pallas_call(
        functools.partial(col_pass_kernel, slots, scales),
        out_shape=out,
        in_specs=[SMEM()] * 3 + [VMEM()] * (4 + len(more)),
        out_specs=out_specs,
        scratch_shapes=scratch,
        name="col_pass",
        compiler_params=pltpu.CompilerParams(vmem_limit_bytes=VMEM_LIMIT),
    )(*lists, x, y, f_pot, g_pot, *more)


def combine_kernel(epsilon, both_eps, *refs):
    if both_eps is None:
        first_own, stack_ref, b_ref, g_ref, send_ref, new_ref = refs
    else:
        first_own, stack_ref, b_ref, g_ref, first_ref, totals_ref, send_ref = refs
    devices, own, _ = stack_ref.shape
    here = pl.ds(pl.multiple_of(first_own[0], own), own)
    top = stack_ref[0]
    for d in range(1, devices):
        top = jnp.maximum(top, stack_ref[d])
    summed = jnp.exp2(stack_ref[0] - top)
    for d in range(1, devices):
        summed += jnp.exp2(stack_ref[d] - top)
    gain = b_ref[here, :] - (top + jnp.log2(summed))
    if both_eps is None:
        new = 2.0 * (g_ref[here, :] + gain)
        new_ref[...] = new
    else:
        difference = totals_ref[8:9, :] - totals_ref[:1, :]
        half = first_ref[here, :] * first_epsilon
        new = LN2 * (epsilon * (g_ref[...] + gain) + both_eps * difference - half)
    for d in range(devices):
        send_ref[d] = new


def combine(first_own, stack, log_b, g_pot, last):
    shape = jax.ShapeDtypeStruct
    send = shape(stack.shape, jnp.float32)
    if last is None:
        more, scales = (), (None, None)
        out = (send, shape(stack.shape[1:], jnp.float32))
    else:
        more, scales = last[:2], last[2:]
        out = send
    return pl.pallas_call(
        functools.partial(combine_kernel, *scales),
        out_shape=out,
        in_specs=[SMEM()] + [VMEM()] * (3 + len(more)),
        out_specs=jax.tree.map(lambda _: VMEM(), out),
        name="combine",
        compiler_params=pltpu.CompilerParams(vmem_limit_bytes=VMEM_LIMIT // 2),
    )(first_own, stack, log_b, g_pot, *more)


def lse_of(parts):
    top = functools.reduce(jnp.maximum, parts)
    return top + jnp.log2(sum(jnp.exp2(part - top) for part in parts))


def over_cols(part, cols):
    def moved(value, pairs):
        return lax.ppermute(value, "col", pairs)

    part = lse_of([part, moved(part, [(i, i ^ 1) for i in range(cols)])])
    masks = range(2, cols, 2)
    return lse_of([part] + [moved(part, [(i, i ^ mask) for i in range(cols)]) for mask in masks])


def exchange(blocks, rest):
    blocks, rest = lax.optimization_barrier((blocks, rest))
    return lax.optimization_barrier((lax.all_to_all(blocks, "row", 0, 0), rest))


def body(source_points, target_points, source_mass, target_mass, tile_cols, tile_counts):
    width, rows = source_points.shape
    row_blocks = rows // TILE
    target_cells = target_points.shape[1]
    target_blocks = target_cells // TILE
    slots = tile_cols.shape[2]
    row_devices = lax.axis_size("row")
    col_devices = lax.axis_size("col")
    own_blocks = target_blocks // row_devices

    cols = tile_cols.transpose(1, 2, 0).reshape(slots, row_blocks)
    counts = tile_counts.reshape(row_blocks)
    mass_a = source_mass.reshape(row_blocks, TILE)
    first_own = (lax.axis_index("row") * own_blocks).reshape(1)
    counts, first_own = lax.optimization_barrier((counts, first_own))

    part, x1, x2, y, g_first, half_x, log_a, log_b, mass, order = first_row_pass(
        cols,
        counts,
        mass_a,
        target_mass.reshape(target_blocks, TILE),
        source_points,
        target_points,
        slots,
    )
    lists = (cols, counts, order)
    x1, x2, y = (pltpu.with_memory_space_constraint(v, pltpu.VMEM) for v in (x1, x2, y))

    f_pot = log_a - over_cols(part, col_devices)
    part = col_pass(lists, x1, y, f_pot, g_first, slots, row_devices)
    stack, (f_pot, first_own) = exchange(part, (2.0 * f_pot, first_own))
    send, g_own = combine(first_own, stack, log_b, g_first, None)
    g_pot, (f_pot, first_own) = exchange(send, (f_pot, first_own))
    g_pot = g_pot.reshape(target_blocks, TILE)

    first, second = first_epsilon, 0.5 * first_epsilon
    part = row_pass(lists, x2, y, f_pot, g_pot, g_first, log_b, mass, slots)
    both = over_cols(part, col_devices)
    part, totals = both[:row_blocks], both[row_blocks:]
    f_pot = f_pot + (log_a - part)
    part, source = col_pass(
        lists, x2, y, f_pot, g_pot, slots, row_devices, (half_x, totals, second, first)
    )
    stack, (totals, first_own) = exchange(part, (totals, first_own))
    send = combine(first_own, stack, log_b, g_own, (g_first, totals, second, first + second))
    target = lax.all_to_all(send, "row", 0, 0)
    return (source.reshape(rows), target.reshape(target_cells))


def solution(mesh):
    return jax.shard_map(
        body,
        mesh=mesh,
        in_specs=(
            P(None, "row"),
            P(None, "col"),
            P("row"),
            P("col"),
            P("row", "col", None),
            P("row", "col"),
        ),
        out_specs=(P("row"), P("col")),
        check_vma=False,
    )
```
